32 devices in a mesh: fsdp: 8 (over z, y), dp: 4 (over x, core).
Axes of the slice: x: 2, y: 2, z: 4, core: 2. Of those that a mesh axis runs over, the one named last changes fastest.
Arguments:
- inputs: bfloat16 [16384, 640], P(('fsdp', 'dp')), may hold values from -6 to 6
- targets: int32 [16384], P(('fsdp', 'dp')), may hold values from 0 to 24
- masked: int32 [16384], P(('fsdp', 'dp')), may hold values from 0 to 1, as said below
- lengths: int32 [128], P(('fsdp', 'dp')), may hold values from 64 to 128, as said below
- attn_weight: bfloat16 [2, 12800, 128], P(None, 'fsdp'), may hold values from -2 to 2
- up_weight: bfloat16 [2, 25600, 128], P(None, 'fsdp'), may hold values from -0.25 to 0.25
- down_weight: bfloat16 [2, 25600, 128], P(None, 'fsdp'), may hold values from -0.078125 to 0.078125
- norm_gains: float32 [2, 2, 640], replicated, may hold values from 0.5 to 1.5
- layer_biases: float32 [2, 6, 640], replicated, may hold values from -1.75 to 1.75
- up_bias: float32 [2, 5120], replicated, may hold values from -1.75 to 1.75
- head_weight: bfloat16 [640, 25], replicated, may hold values from -0.5 to 0.5
- final_gain: float32 [640], replicated, may hold values from 0.5 to 1.5
- final_shift: float32 [640], replicated, may hold values from -1.75 to 1.75
- head_bias: float32 [25], replicated, may hold values from -3 to 3
Outputs:
- activations: bfloat16 [16384, 640], P(('fsdp', 'dp'))
- input_grad: float32 [16384, 640], P(('fsdp', 'dp'))
- attn_grad: float32 [2, 12800, 128], P(None, 'fsdp')
- up_grad: float32 [2, 25600, 128], P(None, 'fsdp')
- down_grad: float32 [2, 25600, 128], P(None, 'fsdp')
- gains_grad: float32 [2, 2, 640], replicated
- biases_grad: float32 [2, 6, 640], replicated
- up_bias_grad: float32 [2, 5120], replicated
- head_weight_grad: float32 [640, 25], replicated
- final_gain_grad: float32 [640], replicated
- final_shift_grad: float32 [640], replicated
- head_bias_grad: float32 [25], replicated
- loss: float32 [], replicated
- accuracy: float32 [], replicated
- counts: int32 [], replicated
The draws below stay inside these ranges and needn't reach their ends.
Inputs may be any that keep to these rules, and one draw needn't show every extreme that they name: `lengths`: number of valid rows of each sequence; some sequence has all 128 rows. `masked`: 1 only at rows below the sequence's length; every sequence has at least one 1.
All inputs are finite; a program needn't handle non-finite values.
Results may differ from the reference program's by a relative error of at most 0.013.
Values may be sent and summed in bfloat16 or wider, within the bound.
No kernel may reach another device: no remote copies, remote signals or barrier semaphores. Data moves between devices by JAX's collectives and lax.ppermute only.
A program may use at most 320 MiB of HBM per device.

```python
import math
import jax
import jax.numpy as jnp
from jax import lax

D = 640
HEADS = 20
HEAD_DIM = 32
FF = 5120
VOCAB = 25
LAYERS = 2
LEN = 128
SEQS = 128
TOKENS = 16384


def sequence_lengths(key):
    key = jax.random.fold_in(key, 11)
    drawn = jax.random.randint(key, (SEQS,), LEN // 2, LEN + 1)
    chosen = jax.random.randint(jax.random.fold_in(key, 1), (), 0, SEQS)
    places = jnp.arange(SEQS)
    drawn = jnp.where(places == chosen, LEN, drawn)
    drawn = jnp.where(places == (chosen + 1) % SEQS, LEN // 2, drawn)
    return drawn.astype(jnp.int32)


def draw_lengths(key, part):
    return sequence_lengths(key)


def draw_masked(key, part):
    seq_lengths = sequence_lengths(key)
    key = jax.random.fold_in(key, 5)
    rate_key, bit_key, pick_key = jax.random.split(key, 3)
    places = jnp.arange(SEQS)
    base_rate = 50 + 150 * places // max(SEQS - 1, 1)
    seq_rates = base_rate * jax.random.randint(rate_key, (SEQS,), 50, 151) // 100
    coin_draws = jax.random.randint(bit_key, (SEQS, LEN), 0, 1000)
    positions = jnp.arange(LEN)[None, :]
    inside = positions < seq_lengths[:, None]
    forced = positions == jax.random.randint(pick_key, (SEQS, 1), 0, seq_lengths[:, None])
    chosen = (coin_draws < seq_rates[:, None]) & inside | forced
    return chosen.astype(jnp.int32).reshape(SEQS * LEN)


def draw_attn_weight(key, part):
    key = jax.random.fold_in(key, 7)
    samples = jnp.clip(jax.random.normal(key, (LAYERS, D, 4, D), jnp.float32), -5.0, 5.0)
    factors = jnp.array([1.0, 1.0, 1.0, 4.0], jnp.float32) / math.sqrt(D)
    return (samples * factors[None, None, :, None]).reshape(LAYERS, 4 * D * D // 128, 128).astype(jnp.bfloat16)


def place_ends(values, key, least, largest):
    index_at = [jax.random.randint(jax.random.fold_in(key, axis), (), 0, length) for axis, length in enumerate(values.shape)]
    widest = values.shape.index(max(values.shape))
    beside = index_at[:widest] + [(index_at[widest] + 1) % values.shape[widest]] + index_at[widest + 1:]
    return values.at[tuple(index_at)].set(least).at[tuple(beside)].set(largest)


def shard_levels(rng, dims, pieces, low, top_value):
    loudness = 1.0
    for axis_at, blocks in pieces:
        draws = jax.random.uniform(jax.random.fold_in(jax.random.fold_in(rng, 6), axis_at), (blocks,), jnp.float32, low / len(pieces), top_value / len(pieces))
        loudness = loudness * jnp.repeat(jnp.exp(draws), dims[axis_at] // blocks).reshape((-1,) + (1,) * (len(dims) - 1 - axis_at))
    return loudness


def scatter_about(rng, dims, spread, limit, cuts=(), held_as=jnp.bfloat16):
    values = jax.random.normal(rng, dims, jnp.float32) * spread
    if len(cuts) > 0:
        values = shard_levels(rng, dims, cuts, -0.22, 0.18) * values
    return jnp.clip(values, min=-limit, max=limit).astype(held_as)


def setup_inputs(seed: int = 0) -> dict:
    splits = jax.random.split(jax.random.key(seed), 15)
    return {
        "inputs": scatter_about(splits[0], (TOKENS, D), 1.0, 6.0, ((0, 32),)),
        "targets": place_ends(jax.random.randint(splits[1], (TOKENS,), 0, VOCAB), jax.random.fold_in(splits[1], 1), 0, VOCAB - 1).astype(jnp.int32),
        "masked": draw_masked(jax.random.fold_in(splits[14], 71), 0),
        "lengths": draw_lengths(jax.random.fold_in(splits[14], 71), 0),
        "attn_weight": draw_attn_weight(jax.random.fold_in(splits[14], 71), 0),
        "up_weight": scatter_about(splits[5], (LAYERS, D * FF // 128, 128), D ** -0.5, 0.25, ((1, 8),)),
        "down_weight": scatter_about(splits[6], (LAYERS, FF * D // 128, 128), FF ** -0.5, 0.078125, ((1, 8),)),
        "norm_gains": jnp.clip(1.0 + 0.1 * jax.random.normal(splits[7], (LAYERS, 2, D), jnp.float32), 0.5, 1.5),
        "layer_biases": scatter_about(splits[8], (LAYERS, 6, D), 0.3, 1.75, (), jnp.float32),
        "up_bias": scatter_about(splits[9], (LAYERS, FF), 0.3, 1.75, (), jnp.float32),
        "head_weight": scatter_about(splits[10], (D, VOCAB), (D // 4) ** -0.5, 0.5),
        "final_gain": jnp.clip(1.0 + 0.1 * jax.random.normal(splits[11], (D,), jnp.float32), 0.5, 1.5),
        "final_shift": scatter_about(splits[12], (D,), 0.3, 1.75, (), jnp.float32),
        "head_bias": scatter_about(splits[13], (VOCAB,), 0.5, 3.0, (), jnp.float32),
    }


@jax.custom_vjp
def low(v):
    return lax.optimization_barrier(v.astype(jnp.bfloat16)).astype(jnp.float32)

@jax.custom_vjp
def low_back(v):
    return v

def low_keep(v):
    return (low(v), None)

def low_pass(kept, grad):
    return (grad,)

def back_keep(v):
    return (v, None)

def back_low(kept, grad):
    return (low(grad),)
low.defvjp(low_keep, low_pass)
low_back.defvjp(back_keep, back_low)

def product(left, right):
    return jnp.dot(left, right, precision=lax.Precision.HIGHEST, preferred_element_type=jnp.float32)

def normalize(values):
    centered = values - lax.optimization_barrier(jnp.mean(values, -1, keepdims=True))
    return centered * lax.rsqrt(lax.optimization_barrier(jnp.mean(centered * centered, -1, keepdims=True)) + 1e-05)

def layer_apply(residual, attn_flat, up_flat, down_flat, gain_rows, bias_rows, up_shift, key_valid):
    seq_count = key_valid.shape[0]
    head_shape = (seq_count, LEN, HEADS, HEAD_DIM)
    attn_matrix = attn_flat.reshape(D, 4 * D)
    normed_in = low(normalize(residual) * gain_rows[0] + bias_rows[0])
    packed = product(normed_in, attn_matrix[:, :3 * D])
    queries = low(low_back(packed[:, :D] + bias_rows[2])).reshape(head_shape)
    key_rows = low(low_back(packed[:, D:2 * D])).reshape(head_shape)
    value_rows = low(low_back(packed[:, 2 * D:] + bias_rows[3])).reshape(head_shape)
    scores = jnp.einsum('sqhd,skhd->shqk', queries, key_rows, precision=lax.Precision.HIGHEST) * (1.0 / math.sqrt(HEAD_DIM))
    scores = jnp.where(key_valid[:, None, None, :], low_back(scores), -1e+30)
    attention = low(jax.nn.softmax(scores, axis=-1))
    mixed_rows = jnp.einsum('shqk,skhd->sqhd', attention, value_rows, precision=lax.Precision.HIGHEST)
    mixed_rows = low(low_back(mixed_rows.reshape(seq_count * LEN, D)))
    middle = residual + low_back(product(mixed_rows, attn_matrix[:, 3 * D:]) + bias_rows[4])
    second = low(normalize(middle) * gain_rows[1] + bias_rows[1])
    hidden = low_back(product(second, up_flat.reshape(D, FF)) + up_shift)
    active = low(jax.nn.gelu(hidden, approximate=False))
    return middle + low_back(product(active, down_flat.reshape(FF, D)) + bias_rows[5])

def group_objective(params, residual, target_rows, mask_rows, length_rows):
    attn_all, up_all, down_all, gains_all, biases_all, upshift_all, head_matrix, fin_gain, fin_shift, head_shift = params
    key_valid = jnp.arange(LEN)[None, :] < length_rows[:, None]
    for layer_index in range(LAYERS):
        residual = layer_apply(residual, attn_all[layer_index], up_all[layer_index], down_all[layer_index], gains_all[layer_index], biases_all[layer_index], upshift_all[layer_index], key_valid)
    final_rows = low(normalize(residual) * fin_gain + fin_shift)
    logits = low_back(product(final_rows, head_matrix) + head_shift)
    log_total = jax.nn.logsumexp(logits, axis=-1)
    onehot = (target_rows[:, None] == jnp.arange(VOCAB)[None, :]).astype(jnp.float32)
    picked = lax.optimization_barrier(jnp.sum(logits * onehot, -1))
    weights_mask = mask_rows.astype(jnp.float32)
    objective_value = jnp.sum(weights_mask * (log_total - picked))
    prob_total = jnp.sum(weights_mask * jnp.exp(picked - log_total))
    return (objective_value, (residual, prob_total, jnp.sum(mask_rows)))

def reference(inputs, targets, masked, lengths, attn_weight, up_weight, down_weight, norm_gains, layer_biases, up_bias, head_weight, final_gain, final_shift, head_bias):
    params = (attn_weight.astype(jnp.float32), up_weight.astype(jnp.float32), down_weight.astype(jnp.float32), norm_gains, layer_biases, up_bias, head_weight.astype(jnp.float32), final_gain, final_shift, head_bias)
    group_size = math.gcd(SEQS, max(1, 4096 // LEN))
    group_count = SEQS // group_size
    row_count = group_size * LEN
    blocks = (inputs.astype(jnp.float32).reshape(group_count, row_count, D), targets.reshape(group_count, row_count), masked.reshape(group_count, row_count), lengths.reshape(group_count, group_size))

    def advance(carried, block_data):
        gradients, totals = carried
        residual, target_rows, mask_rows, length_rows = block_data

        def objective(weights, start):
            return group_objective(weights, start, target_rows, mask_rows, length_rows)
        objective_value, backward, extras = jax.vjp(objective, params, residual, has_aux=True)
        last_residual, prob_total, mask_count = extras
        weight_grads, residual_grad = backward(jnp.ones_like(objective_value))
        gradients = jax.tree.map(jnp.add, gradients, weight_grads)
        totals = (totals[0] + objective_value, totals[1] + prob_total, totals[2] + mask_count.astype(jnp.int32))
        return ((gradients, totals), (last_residual.astype(jnp.bfloat16), residual_grad))
    initial = (jax.tree.map(jnp.zeros_like, params), (jnp.zeros((), jnp.float32), jnp.zeros((), jnp.float32), jnp.zeros((), jnp.int32)))
    (gradients, totals), (outputs, input_grads) = lax.scan(advance, initial, blocks)
    count_float = totals[2].astype(jnp.float32)
    return (outputs.reshape(TOKENS, D), input_grads.reshape(TOKENS, D), gradients[0], gradients[1], gradients[2], gradients[3], gradients[4], gradients[5], gradients[6], gradients[7], gradients[8], gradients[9], totals[0] / count_float, totals[1] / count_float, totals[2])
```

```python
import math

import jax
import jax.numpy as jnp
from jax import lax
from jax.experimental import pallas as pl
from jax.experimental.pallas import tpu as pltpu
from jax.sharding import Mesh
from jax.sharding import PartitionSpec as P

D = 640
HEADS = 20
HEAD_DIM = 32
FF = 5120
VOCAB = 25
LAYERS = 2
LEN = 128
SEQ_DEV = 4
ROWS = SEQ_DEV * LEN
TILE = 640
TILES = FF // TILE
GROUPS = HEADS * HEAD_DIM // 128
PER_GROUP = 128 // HEAD_DIM
CHUNK = 128
BF = jnp.bfloat16
F32 = jnp.float32
MIB = 2**20

VMEM_SPEC = pl.BlockSpec(memory_space=pltpu.VMEM)
SMEM_SPEC = pl.BlockSpec(memory_space=pltpu.SMEM)
ANY_SPEC = pl.BlockSpec(memory_space=pl.ANY)


def dot(left, right, dims):
    return lax.dot_general(left, right, (dims, ((), ())), preferred_element_type=F32)


def mul_nn(left, right):
    return dot(left, right, ((1,), (0,)))


def mul_nt(left, right):
    return dot(left, right, ((1,), (1,)))


def mul_tn(left, right):
    return dot(left, right, ((0,), (0,)))


def normalize(values):
    centered = values - jnp.mean(values, -1, keepdims=True)
    inverse = lax.rsqrt(jnp.mean(centered * centered, -1, keepdims=True) + 1e-05)
    return (centered * inverse, inverse)


def norm_back(grad_normed, normed, inverse):
    return inverse * (
        grad_normed
        - jnp.mean(grad_normed, -1, keepdims=True)
        - normed * jnp.mean(grad_normed * normed, -1, keepdims=True)
    )


def col_sum(values):
    return jnp.sum(values, 0, keepdims=True)


def sds(shape, dtype):
    return jax.ShapeDtypeStruct(shape, dtype)


def over_chunks(body, start):
    def step(index, carry):
        return body(pl.ds(pl.multiple_of(index * CHUNK, CHUNK), CHUNK), carry)

    return lax.fori_loop(0, ROWS // CHUNK, step, start)


def quarter_copies(place_ref, buffers, held, sems):
    x_at, y_at, c_at = place_ref[0], place_ref[1], place_ref[2]
    copies = []
    for number, buffer in enumerate(buffers):
        quarter = (x_at ^ (number >> 1)) * 2 + (c_at ^ (number & 1))
        for dy in range(2):
            copies.append(
                pltpu.make_async_copy(
                    buffer.at[dy], held.at[quarter, :, y_at ^ dy], sems.at[2 * number + dy]
                )
            )
    return copies


def tile_copies(place_ref, buffers, held, sems):
    x_at, y_at, c_at = place_ref[0], place_ref[1], place_ref[2]
    copies = []
    for number, buffer in enumerate(buffers):
        quarter = (x_at ^ (number >> 1)) * 2 + (c_at ^ (number & 1))
        for dy in range(2):
            for half in range(2):
                copies.append(
                    pltpu.make_async_copy(
                        buffer.at[dy, :, :, pl.ds(half * TILE, TILE)],
                        held.at[quarter * 2 + half, :, y_at ^ dy],
                        sems.at[4 * number + 2 * dy + half],
                    )
                )
    return copies


def half_copies(place_ref, buffers, held, sems):
    y_at, c_at = place_ref[1], place_ref[2]
    copies = []
    for number, buffer in enumerate(buffers):
        for dy in range(2):
            copies.append(
                pltpu.make_async_copy(
                    buffer.at[dy], held.at[:, y_at ^ dy, c_at ^ number], sems.at[2 * number + dy]
                )
            )
    return copies


def square(values):
    return values.reshape(D, values.shape[-1])


def head_masks():
    lanes = lax.broadcasted_iota(jnp.int32, (LEN, 128), 1) // HEAD_DIM
    return [(lanes == member) for member in range(PER_GROUP)]


def stack_heads(values, masks):
    zero = jnp.zeros_like(values)
    return jnp.concatenate([jnp.where(mask, values, zero) for mask in masks], 0)


def unstack_heads(values):
    parts = [
        values[HEAD_DIM * member : HEAD_DIM * (member + 1), LEN * member : LEN * (member + 1)]
        for member in range(PER_GROUP)
    ]
    return jnp.concatenate(parts, 0).T


def scores_of(keys, queries, valid):
    scores = mul_nt(keys, queries) * (1.0 / math.sqrt(HEAD_DIM))
    return jnp.where(valid, scores, -1e30)


def mix_kernel(
    place_ref,
    lengths_ref,
    residual_ref,
    w0_ref,
    w1_ref,
    w2_ref,
    w3_ref,
    gains_ref,
    biases_ref,
    packed_ref,
    log_ref,
    mixed_ref,
    middle_ref,
    second_ref,
    held,
    pre_ref,
    sems,
):
    copies = quarter_copies(place_ref, (w0_ref, w1_ref, w2_ref, w3_ref), held, sems)
    for copy in copies:
        copy.start()

    def first(rows, carry):
        normed, inverse = normalize(residual_ref[rows, :].astype(F32))
        pre_ref[rows, :] = (normed * gains_ref[0:1, :] + biases_ref[0:1, :]).astype(BF)
        return carry

    over_chunks(first, 0)
    for copy in copies:
        copy.wait()
    shifts = (biases_ref[2:3, :], None, biases_ref[3:4, :])
    for part in range(3):
        result = mul_nn(pre_ref[...], square(held[part]))
        if shifts[part] is not None:
            result = result + shifts[part]
        packed_ref[:, part * D : (part + 1) * D] = result.astype(BF)
    masks = head_masks()
    row_ids = lax.broadcasted_iota(jnp.int32, (LEN, 1), 0)

    def one_sequence(seq, carry):
        rows = pl.ds(pl.multiple_of(seq * LEN, LEN), LEN)
        valid = row_ids < lengths_ref[seq]
        for group in range(GROUPS):
            lanes = slice(group * 128, (group + 1) * 128)
            queries = stack_heads(packed_ref[rows, lanes], masks)
            key_rows = packed_ref[rows, D + group * 128 : D + (group + 1) * 128]
            value_rows = packed_ref[rows, 2 * D + group * 128 : 2 * D + (group + 1) * 128]
            scores = scores_of(key_rows, queries, valid)
            top = jnp.max(scores, 0, keepdims=True)
            expos = jnp.exp(scores - top)
            total = jnp.sum(expos, 0, keepdims=True)
            probs = (expos * (1.0 / total)).astype(BF)
            log_ref[seq * GROUPS + group] = top + jnp.log(total)
            mixed_ref[rows, lanes] = unstack_heads(mul_tn(value_rows, probs)).astype(BF)
        return carry

    lax.fori_loop(0, SEQ_DEV, one_sequence, 0)
    middle_ref[...] = mul_nn(mixed_ref[...], square(held[3])) + biases_ref[4:5, :]

    def last(rows, carry):
        middle = middle_ref[rows, :] + residual_ref[rows, :].astype(F32)
        middle_ref[rows, :] = middle
        normed, inverse = normalize(middle)
        second_ref[rows, :] = (normed * gains_ref[1:2, :] + biases_ref[1:2, :]).astype(BF)
        return carry

    over_chunks(last, 0)


def mix(place, lengths, residual, quarters, gains, biases):
    return pl.pallas_call(
        mix_kernel,
        out_shape=(
            sds((ROWS, 3 * D), BF),
            sds((SEQ_DEV * GROUPS, 1, PER_GROUP * LEN), F32),
            sds((ROWS, D), BF),
            sds((ROWS, D), F32),
            sds((ROWS, D), BF),
        ),
        in_specs=[SMEM_SPEC, SMEM_SPEC, VMEM_SPEC] + [ANY_SPEC] * 4 + [VMEM_SPEC] * 2,
        out_specs=(VMEM_SPEC,) * 5,
        scratch_shapes=[
            pltpu.VMEM((4, 4, 2, D // 8, D), BF),
            pltpu.VMEM((ROWS, D), BF),
            pltpu.SemaphoreType.DMA((8,)),
        ],
        compiler_params=pltpu.CompilerParams(vmem_limit_bytes=40 * MIB),
        cost_estimate=pl.CostEstimate(
            flops=2 * ROWS * D * 4 * D * 4, bytes_accessed=10 * MIB, transcendentals=0
        ),
    )(place, lengths, residual, *quarters, gains, biases)


def wide_kernel(
    place_ref,
    second_ref,
    middle_ref,
    u0_ref,
    u1_ref,
    u2_ref,
    u3_ref,
    d0_ref,
    d1_ref,
    shift_ref,
    biases_ref,
    active_ref,
    slope_ref,
    out_ref,
    held_up,
    held_down,
    up_sems,
    down_sems,
):
    tile = pl.program_id(0)
    up_copies = tile_copies(place_ref, (u0_ref, u1_ref, u2_ref, u3_ref), held_up, up_sems)
    down_copies = half_copies(place_ref, (d0_ref, d1_ref), held_down, down_sems)

    @pl.when(tile == 0)
    def _():
        for copy in up_copies + down_copies:
            copy.start()
        out_ref[...] = middle_ref[...] + biases_ref[5:6, :]
        for copy in up_copies + down_copies:
            copy.wait()

    up_tile = square(held_up[tile])
    down_tile = square(held_down[tile // 2, tile % 2])
    shift = shift_ref[pl.ds(tile, 1), :]
    for chunk in range(ROWS // CHUNK):
        rows = slice(chunk * CHUNK, (chunk + 1) * CHUNK)
        hidden = mul_nn(second_ref[rows, :], up_tile) + shift
        phi = 0.5 + 0.5 * lax.erf(hidden * math.sqrt(0.5))
        density = jnp.exp(hidden * hidden * -0.5) * (1.0 / math.sqrt(2.0 * math.pi))
        active = (hidden * phi).astype(BF)
        active_ref[0, rows, :] = active
        slope_ref[0, rows, :] = (phi + hidden * density).astype(BF)
        out_ref[rows, :] += mul_nn(active, down_tile)


def whole_block(shape):
    zeros = (0,) * len(shape)
    return pl.BlockSpec(shape, lambda *_: zeros)


def wide(place, second, middle, up_parts, down_parts, shift, biases):
    tile_block = pl.BlockSpec((1, ROWS, TILE), lambda tile: (tile, 0, 0))
    return pl.pallas_call(
        wide_kernel,
        grid=(TILES,),
        out_shape=(
            sds((TILES, ROWS, TILE), BF),
            sds((TILES, ROWS, TILE), BF),
            sds((ROWS, D), F32),
        ),
        in_specs=[SMEM_SPEC, whole_block((ROWS, D)), whole_block((ROWS, D))]
        + [ANY_SPEC] * 6
        + [whole_block((TILES, TILE)), whole_block((6, D))],
        out_specs=(tile_block, tile_block, whole_block((ROWS, D))),
        scratch_shapes=[
            pltpu.VMEM((TILES, 4, 2, D // 8, TILE), BF),
            pltpu.VMEM((4, 2, 2, TILE // 2, D), BF),
            pltpu.SemaphoreType.DMA((16,)),
            pltpu.SemaphoreType.DMA((4,)),
        ],
        compiler_params=pltpu.CompilerParams(vmem_limit_bytes=52 * MIB),
        cost_estimate=pl.CostEstimate(
            flops=2 * ROWS * D * FF * 6, bytes_accessed=30 * MIB, transcendentals=0
        ),
    )(place, second, middle, *up_parts, *down_parts, shift, biases)


def head_kernel(
    residual_ref,
    targets_ref,
    masked_ref,
    weight_ref,
    shift_ref,
    gain_ref,
    move_ref,
    activations_ref,
    grad_ref,
    rounded_ref,
    small_ref,
):
    small_ref[...] = jnp.zeros_like(small_ref)
    lanes = lax.broadcasted_iota(jnp.int32, (1, 128), 1)

    def body(rows, carry):
        weight_grad, gain_grad, move_grad, shift_grad, stats = carry
        residual = residual_ref[rows, :]
        activations_ref[rows, :] = residual.astype(BF)
        normed, inverse = normalize(residual)
        final = (normed * gain_ref[...] + move_ref[...]).astype(BF)
        logits = mul_nn(final, weight_ref[...]) + shift_ref[...]
        top = jnp.max(logits, -1, keepdims=True)
        log_total = top + jnp.log(jnp.sum(jnp.exp(logits - top), -1, keepdims=True))
        onehot = (targets_ref[rows, :] == lanes).astype(F32)
        picked = jnp.sum(logits * onehot, -1, keepdims=True)
        mask = masked_ref[rows, :].astype(F32)
        loss = col_sum(mask * (log_total - picked))
        hits = col_sum(mask * jnp.exp(picked - log_total))
        count = col_sum(mask)
        stats = stats + (
            jnp.where(lanes == 0, loss, 0.0)
            + jnp.where(lanes == 1, hits, 0.0)
            + jnp.where(lanes == 2, count, 0.0)
        )
        grad_logits = (mask * (jnp.exp(logits - log_total) - onehot)).astype(BF)
        weight_grad = weight_grad + mul_tn(grad_logits, final)
        shift_grad = shift_grad + col_sum(grad_logits.astype(F32))
        grad_final = mul_nt(grad_logits, weight_ref[...])
        gain_grad = gain_grad + col_sum(grad_final * normed)
        move_grad = move_grad + col_sum(grad_final)
        grad = norm_back(grad_final * gain_ref[...], normed, inverse)
        grad_ref[rows, :] = grad
        rounded_ref[rows, :] = grad.astype(BF)
        return weight_grad, gain_grad, move_grad, shift_grad, stats

    row = jnp.zeros((1, D), F32)
    narrow = jnp.zeros((1, 128), F32)
    weight_grad, gain_grad, move_grad, shift_grad, stats = over_chunks(
        body, (jnp.zeros((128, D), F32), row, row, narrow, narrow)
    )
    small_ref[0:32, :] = weight_grad[0:32, :]
    small_ref[32:33, :] = gain_grad
    small_ref[33:34, :] = move_grad
    small_ref[34:35, 0:128] = shift_grad
    small_ref[35:36, 0:128] = stats


def head(residual, targets, masked, weight, shift, gain, move):
    return pl.pallas_call(
        head_kernel,
        out_shape=(
            sds((ROWS, D), BF),
            sds((ROWS, D), F32),
            sds((ROWS, D), BF),
            sds((40, D), F32),
        ),
        in_specs=[VMEM_SPEC] * 7,
        out_specs=(VMEM_SPEC,) * 4,
        compiler_params=pltpu.CompilerParams(vmem_limit_bytes=32 * MIB),
        cost_estimate=pl.CostEstimate(
            flops=2 * ROWS * D * 128 * 8, bytes_accessed=5 * MIB, transcendentals=0
        ),
    )(residual, targets, masked, weight, shift, gain, move)


def down_back_kernel(place_ref, grad_ref, active_ref, send_ref, keep_ref, turned):
    @pl.when(pl.program_id(0) == 0)
    def _():
        for half in range(2):
            turned[half] = grad_ref[:, half * (D // 2) : (half + 1) * (D // 2)].T

    c_at = place_ref[2]
    active = active_ref[0]
    send_ref[0, 0] = mul_nn(turned[1 - c_at], active).astype(BF)
    keep_ref[0, 0] = mul_nn(turned[c_at], active).astype(BF)


def down_back(place, grad, active):
    def block_at(step, place_ref):
        return ((step % 4) * 2 + (place_ref[1] ^ (1 - step // 4)), 0, 0)

    out_block = pl.BlockSpec(
        (1, 1, D // 2, TILE), lambda step, place_ref: (1 - step // 4, step % 4, 0, 0)
    )
    out = sds((2, 4, D // 2, TILE), BF)
    return pl.pallas_call(
        down_back_kernel,
        grid_spec=pltpu.PrefetchScalarGridSpec(
            num_scalar_prefetch=1,
            grid=(TILES,),
            in_specs=[whole_block((ROWS, D)), pl.BlockSpec((1, ROWS, TILE), block_at)],
            out_specs=(out_block, out_block),
            scratch_shapes=[pltpu.VMEM((2, D // 2, ROWS), BF)],
        ),
        out_shape=(out, out),
        compiler_params=pltpu.CompilerParams(vmem_limit_bytes=32 * MIB),
        cost_estimate=pl.CostEstimate(
            flops=2 * ROWS * D * FF, bytes_accessed=13 * MIB, transcendentals=0
        ),
    )(place, grad, active)


def wide_back_kernel(
    place_ref,
    rounded_ref,
    grad_ref,
    second_ref,
    middle_ref,
    slope_ref,
    u0_ref,
    u1_ref,
    u2_ref,
    u3_ref,
    d0_ref,
    d1_ref,
    gains_ref,
    send_ref,
    keep_ref,
    shift_ref,
    middle_grad_ref,
    middle_rounded_ref,
    small_ref,
    held_up,
    held_down,
    turned,
    total,
    up_sems,
    down_sems,
):
    step = pl.program_id(0)
    up_copies = tile_copies(place_ref, (u0_ref, u1_ref, u2_ref, u3_ref), held_up, up_sems)
    down_copies = half_copies(place_ref, (d0_ref, d1_ref), held_down, down_sems)

    @pl.when(step == 0)
    def _():
        for copy in down_copies + up_copies:
            copy.start()
        turned[...] = second_ref[...].T
        total[...] = jnp.zeros_like(total)
        for copy in down_copies + up_copies:
            copy.wait()

    tile = wide_back_tile(step, place_ref)
    y_at = place_ref[1]
    grad_active = mul_nt(rounded_ref[...], square(held_down[tile // 2, tile % 2]))
    grad_hidden = (grad_active * slope_ref[0].astype(F32)).astype(BF)
    shift_ref[pl.ds(tile, 1), :] = col_sum(grad_hidden.astype(F32))
    total[...] += mul_nt(grad_hidden, square(held_up[tile]))
    up_grad = mul_nn(turned[...], grad_hidden).astype(BF).reshape(4, 2, D // 8, TILE)

    def store(out_ref):
        for side in range(2):
            out_ref[0, side ^ y_at] = up_grad[:, side]

    @pl.when(step < 4)
    def _():
        store(send_ref)

    @pl.when(step >= 4)
    def _():
        store(keep_ref)

    @pl.when(step == TILES - 1)
    def _():
        def body(rows, carry):
            gain_sum, move_sum, out_sum, down_sum = carry
            normed, inverse = normalize(middle_ref[rows, :])
            grad_second = total[rows, :]
            grad = grad_ref[rows, :] + norm_back(grad_second * gains_ref[1:2, :], normed, inverse)
            rounded = grad.astype(BF)
            middle_grad_ref[rows, :] = grad
            middle_rounded_ref[rows, :] = rounded
            return (
                gain_sum + col_sum(grad_second * normed),
                move_sum + col_sum(grad_second),
                out_sum + col_sum(rounded.astype(F32)),
                down_sum + col_sum(rounded_ref[rows, :].astype(F32)),
            )

        row = jnp.zeros((1, D), F32)
        sums = over_chunks(body, (row, row, row, row))
        small_ref[...] = jnp.zeros_like(small_ref)
        for number in range(4):
            small_ref[number : number + 1, :] = sums[number]


def wide_back_tile(step, place_ref):
    inner = step % 4
    quarter = (place_ref[0] ^ (1 - inner // 2)) * 2 + (place_ref[2] ^ (1 - step // 4))
    return quarter * 2 + inner % 2


def wide_back(place, rounded, grad, second, middle, slope, up_parts, down_parts, gains):
    def send_at(step, place_ref):
        inner = jnp.minimum(step, 3)
        return (1 - inner // 2, 0, 0, 0, inner % 2)

    def keep_at(step, place_ref):
        inner = jnp.maximum(step - 4, 0)
        return (1 - inner // 2, 0, 0, 0, inner % 2)

    out = sds((2, 2, 4, D // 8, 2 * TILE), BF)
    out_shape = (1, 2, 4, D // 8, TILE)
    full = whole_block((ROWS, D))
    return pl.pallas_call(
        wide_back_kernel,
        grid_spec=pltpu.PrefetchScalarGridSpec(
            num_scalar_prefetch=1,
            grid=(TILES,),
            in_specs=[full] * 4
            + [
                pl.BlockSpec(
                    (1, ROWS, TILE),
                    lambda step, place_ref: (wide_back_tile(step, place_ref), 0, 0),
                )
            ]
            + [ANY_SPEC] * 6
            + [whole_block((2, D))],
            out_specs=(
                pl.BlockSpec(out_shape, send_at),
                pl.BlockSpec(out_shape, keep_at),
                whole_block((TILES, TILE)),
                full,
                full,
                whole_block((8, D)),
            ),
            scratch_shapes=[
                pltpu.VMEM((TILES, 4, 2, D // 8, TILE), BF),
                pltpu.VMEM((4, 2, 2, TILE // 2, D), BF),
                pltpu.VMEM((D, ROWS), BF),
                pltpu.VMEM((ROWS, D), F32),
                pltpu.SemaphoreType.DMA((16,)),
                pltpu.SemaphoreType.DMA((4,)),
            ],
        ),
        out_shape=(
            out,
            out,
            sds((TILES, TILE), F32),
            sds((ROWS, D), F32),
            sds((ROWS, D), BF),
            sds((8, D), F32),
        ),
        compiler_params=pltpu.CompilerParams(vmem_limit_bytes=56 * MIB),
        cost_estimate=pl.CostEstimate(
            flops=2 * ROWS * D * FF * 4, bytes_accessed=30 * MIB, transcendentals=0
        ),
    )(place, rounded, grad, second, middle, slope, *up_parts, *down_parts, gains)


def mix_back_kernel(
    place_ref,
    lengths_ref,
    rounded_ref,
    middle_grad_ref,
    residual_ref,
    w0_ref,
    w1_ref,
    w2_ref,
    w3_ref,
    packed_ref,
    log_ref,
    mixed_ref,
    gains_ref,
    biases_ref,
    send_ref,
    keep_ref,
    grad_ref,
    grad_rounded_ref,
    small_ref,
    held,
    turned,
    grad_mixed,
    grad_packed,
    total,
    sems,
):
    x_at, y_at, c_at = place_ref[0], place_ref[1], place_ref[2]
    copies = quarter_copies(place_ref, (w0_ref, w1_ref, w2_ref, w3_ref), held, sems)
    for copy in copies:
        copy.start()

    def store_grad(part, value):
        value = value.astype(BF).reshape(4, 2, D // 8, D)
        dx, dc = x_at ^ (part >> 1), c_at ^ (part & 1)

        @pl.when(dc == 1)
        def _():
            for side in range(2):
                send_ref[dx, side ^ y_at] = value[:, side]

        @pl.when(dc == 0)
        def _():
            for side in range(2):
                keep_ref[dx, side ^ y_at] = value[:, side]

    turned[...] = mixed_ref[...].T
    store_grad(3, mul_nn(turned[...], rounded_ref[...]))

    def first(rows, carry):
        normed, inverse = normalize(residual_ref[rows, :].astype(F32))
        total[rows, :] = normed * gains_ref[0:1, :] + biases_ref[0:1, :]
        return carry

    over_chunks(first, 0)
    turned[...] = total[...].astype(BF).T
    for copy in copies:
        copy.wait()
    grad_mixed[...] = mul_nt(rounded_ref[...], square(held[3])).astype(BF)
    masks = head_masks()
    row_ids = lax.broadcasted_iota(jnp.int32, (LEN, 1), 0)
    scale = 1.0 / math.sqrt(HEAD_DIM)

    def one_sequence(seq, carry):
        rows = pl.ds(pl.multiple_of(seq * LEN, LEN), LEN)
        valid = row_ids < lengths_ref[seq]
        for group in range(GROUPS):
            at_query = slice(group * 128, (group + 1) * 128)
            at_key = slice(D + group * 128, D + (group + 1) * 128)
            at_value = slice(2 * D + group * 128, 2 * D + (group + 1) * 128)
            queries = stack_heads(packed_ref[rows, at_query], masks)
            key_rows = packed_ref[rows, at_key]
            value_rows = packed_ref[rows, at_value]
            grads = stack_heads(grad_mixed[rows, at_query], masks)
            scores = scores_of(key_rows, queries, valid)
            probs = jnp.exp(scores - log_ref[seq * GROUPS + group])
            grad_probs = mul_nt(value_rows, grads)
            inner = jnp.sum(grad_probs * probs, 0, keepdims=True)
            grad_scores = (probs * (grad_probs - inner)).astype(BF)
            grad_packed[rows, at_value] = mul_nn(probs.astype(BF), grads).astype(BF)
            grad_packed[rows, at_key] = (mul_nn(grad_scores, queries) * scale).astype(BF)
            grad_queries = unstack_heads(mul_tn(key_rows, grad_scores))
            grad_packed[rows, at_query] = (grad_queries * scale).astype(BF)
        return carry

    lax.fori_loop(0, SEQ_DEV, one_sequence, 0)
    for part in range(3):
        grads = grad_packed[:, part * D : (part + 1) * D]
        store_grad(part, mul_nn(turned[...], grads))
        result = mul_nt(grads, square(held[part]))
        if part == 0:
            total[...] = result
        else:
            total[...] += result

    def body(rows, carry):
        gain_sum, move_sum, query_sum, value_sum = carry
        normed, inverse = normalize(residual_ref[rows, :].astype(F32))
        grad_pre = total[rows, :]
        grad = middle_grad_ref[rows, :] + norm_back(grad_pre * gains_ref[0:1, :], normed, inverse)
        grad_ref[rows, :] = grad
        grad_rounded_ref[rows, :] = grad.astype(BF)
        return (
            gain_sum + col_sum(grad_pre * normed),
            move_sum + col_sum(grad_pre),
            query_sum + col_sum(grad_packed[rows, 0:D].astype(F32)),
            value_sum + col_sum(grad_packed[rows, 2 * D : 3 * D].astype(F32)),
        )

    row = jnp.zeros((1, D), F32)
    sums = over_chunks(body, (row, row, row, row))
    small_ref[...] = jnp.zeros_like(small_ref)
    for number in range(4):
        small_ref[number : number + 1, :] = sums[number]


def mix_back(
    place, lengths, rounded, middle_grad, residual, quarters, packed, logs, mixed, gains, biases
):
    out = sds((2, 2, 4, D // 8, D), BF)
    return pl.pallas_call(
        mix_back_kernel,
        out_shape=(out, out, sds((ROWS, D), F32), sds((ROWS, D), BF), sds((8, D), F32)),
        in_specs=[SMEM_SPEC, SMEM_SPEC] + [VMEM_SPEC] * 3 + [ANY_SPEC] * 4 + [VMEM_SPEC] * 5,
        out_specs=(VMEM_SPEC,) * 5,
        scratch_shapes=[
            pltpu.VMEM((4, 4, 2, D // 8, D), BF),
            pltpu.VMEM((D, ROWS), BF),
            pltpu.VMEM((ROWS, D), BF),
            pltpu.VMEM((ROWS, 3 * D), BF),
            pltpu.VMEM((ROWS, D), F32),
            pltpu.SemaphoreType.DMA((8,)),
        ],
        compiler_params=pltpu.CompilerParams(vmem_limit_bytes=48 * MIB),
        cost_estimate=pl.CostEstimate(
            flops=2 * ROWS * D * 4 * D * 8, bytes_accessed=18 * MIB, transcendentals=0
        ),
    )(
        place, lengths, rounded, middle_grad, residual, *quarters, packed, logs, mixed, gains, biases
    )


def swap(value, axis):
    return lax.ppermute(value, axis, [(0, 1), (1, 0)])


def as_rows(flat, width):
    return flat.reshape(-1, width // 128, 128)


class Moves:
    def __init__(self, fsdp):
        self.z_size = fsdp // 2
        self.staged = fsdp == 8
        self.x_at = lax.axis_index("x")
        self.y_at = lax.axis_index("y")
        self.c_at = lax.axis_index("c")
        self.place = jnp.stack([self.x_at, self.y_at, self.c_at]).astype(jnp.int32)

    def relative(self, value):
        value = value.swapaxes(0, 1)
        return jnp.where(self.y_at == 0, value, value[::-1])

    def natural(self, value):
        value = jnp.where(self.y_at == 0, value, value[::-1]).swapaxes(0, 1)
        return value.reshape(-1, value.shape[-1])

    def gather_quarters(self, flat, width):
        shard = as_rows(flat, width)
        rows, blocks, _ = shard.shape
        step = blocks // 4
        if not self.staged:
            whole = lax.all_gather(flat, ("z", "y"), axis=0, tiled=True).reshape(4, 2, D // 8, width)
            parts = []
            for number in range(4):
                quarter = (self.x_at ^ (number >> 1)) * 2 + (self.c_at ^ (number & 1))
                part = lax.dynamic_slice_in_dim(whole, quarter * (width // 4), width // 4, 3)
                parts.append(self.relative(part))
            return tuple(parts)
        own = lax.dynamic_slice_in_dim(shard, (self.x_at * 2 + self.c_at) * step, step, 1)
        own = own.reshape(rows, step * 128)
        line = lax.all_gather(own, "z", axis=0, tiled=False)
        plane = jnp.stack([line, swap(line, "y")])
        beside = swap(plane, "x")
        return (plane, swap(plane, "c"), beside, swap(beside, "c"))

    def gather_halves(self, flat):
        if not self.staged:
            whole = lax.all_gather(flat, ("z", "y"), axis=0, tiled=True)
            whole = whole.reshape(4, 2, 2, TILE // 2, D)
            return tuple(
                self.relative(lax.dynamic_index_in_dim(whole, self.c_at ^ number, 2, False))
                for number in range(2)
            )
        shard = as_rows(flat, D)
        half = shard.shape[0] // 2
        own = lax.dynamic_slice_in_dim(shard, self.c_at * half, half, 0).reshape(half, D)
        line = lax.all_gather(own, "z", axis=0, tiled=False)
        plane = jnp.stack([line, swap(line, "y")])
        return (plane, swap(plane, "c"))

    def reduce_quarters(self, send, keep):
        width = 4 * send.shape[-1]
        got_c = swap(send, "c").astype(F32)
        keep = keep.astype(F32)
        got_x = swap((keep[1] + got_c[1]).astype(BF), "x").astype(F32)
        if not self.staged:
            part = self.natural(keep[0] + got_c[0] + got_x).astype(BF)
            part = lax.psum_scatter(part, ("z", "y"), scatter_dimension=0, tiled=True)
        else:
            got_y = swap((keep[0, 1] + got_c[0, 1] + got_x[1]).astype(BF), "y").astype(F32)
            part = (keep[0, 0] + got_c[0, 0] + got_x[0] + got_y).astype(BF)
            part = lax.psum_scatter(part, "z", scatter_dimension=0, tiled=False)
        parts = lax.all_gather(part, ("x", "c"), axis=0, tiled=False)
        return parts.swapaxes(0, 1).reshape(-1, width).astype(F32).reshape(-1, 128)

    def reduce_halves(self, send, keep):
        got_c = swap(send, "c").astype(F32)
        keep = keep.astype(F32)
        if not self.staged:
            part = keep + got_c
            part = jnp.where(self.y_at == 0, part, part[::-1]).transpose(1, 0, 3, 2)
            part = part.reshape(FF, D // 2).astype(BF)
            part = lax.psum_scatter(part, ("z", "y"), scatter_dimension=0, tiled=True).T
        else:
            got_y = swap((keep[1] + got_c[1]).astype(BF), "y").astype(F32)
            part = (keep[0] + got_c[0] + got_y).astype(BF)
            part = lax.psum_scatter(part, "z", scatter_dimension=0, tiled=False)
        part = (part.astype(F32) + swap(part, "x").astype(F32)).astype(BF)
        parts = lax.all_gather(part, "c", axis=0, tiled=True)
        return parts.T.astype(F32).reshape(-1, 128)

    def sum_all(self, value):
        value = value + swap(value, "c")
        value = value + swap(value, "x")
        value = value + swap(value, "y")
        reach = 1
        while reach < self.z_size:
            pairs = [(at, at ^ reach) for at in range(self.z_size)]
            value = value + lax.ppermute(value, "z", pairs)
            reach *= 2
        return value


def local(
    fsdp,
    inputs,
    targets,
    masked,
    lengths,
    attn_weight,
    up_weight,
    down_weight,
    norm_gains,
    layer_biases,
    up_bias,
    head_weight,
    final_gain,
    final_shift,
    head_bias,
):
    moves = Moves(fsdp)
    place = moves.place
    targets = targets.reshape(ROWS, 1)
    masked = masked.reshape(ROWS, 1)
    head_padded = jnp.pad(head_weight, ((0, 0), (0, 128 - VOCAB)))
    bias_padded = jnp.pad(head_bias.reshape(1, VOCAB), ((0, 0), (0, 128 - VOCAB)), constant_values=-1e30)
    shifts = up_bias.reshape(LAYERS, TILES, TILE)
    residual = inputs
    saved = []
    for layer in range(LAYERS):
        quarters = moves.gather_quarters(attn_weight[layer], 4 * D)
        up_parts = moves.gather_quarters(up_weight[layer], FF)
        down_parts = moves.gather_halves(down_weight[layer])
        packed, logs, mixed, middle, second = mix(
            place, lengths, residual, quarters, norm_gains[layer], layer_biases[layer]
        )
        active, slope, output = wide(
            place, second, middle, up_parts, down_parts, shifts[layer], layer_biases[layer]
        )
        saved.append(
            (quarters, up_parts, down_parts, residual, packed, logs, mixed, middle, second, active, slope)
        )
        residual = output
    activations, grad, rounded, head_small = head(
        residual,
        targets,
        masked,
        head_padded,
        bias_padded,
        final_gain.reshape(1, D),
        final_shift.reshape(1, D),
    )
    small = [head_small]
    attn_grads = [None] * LAYERS
    up_grads = [None] * LAYERS
    down_grads = [None] * LAYERS
    for layer in reversed(range(LAYERS)):
        (quarters, up_parts, down_parts, residual, packed, logs, mixed, middle, second, active, slope) = (
            saved[layer]
        )
        send, keep = down_back(place, rounded, active)
        down_grads[layer] = moves.reduce_halves(send, keep)
        send, keep, shift_grad, middle_grad, middle_rounded, wide_small = wide_back(
            place, rounded, grad, second, middle, slope, up_parts, down_parts, norm_gains[layer]
        )
        up_grads[layer] = moves.reduce_quarters(send, keep)
        send, keep, grad, rounded, mix_small = mix_back(
            place,
            lengths,
            middle_rounded,
            middle_grad,
            residual,
            quarters,
            packed,
            logs,
            mixed,
            norm_gains[layer],
            layer_biases[layer],
        )
        attn_grads[layer] = moves.reduce_quarters(send, keep)
        small += [shift_grad, wide_small, mix_small]
    summed = moves.sum_all(jnp.concatenate(small, 0))
    gains_grad, biases_grad, shifts_grad = [], [], []
    for layer in range(LAYERS):
        base = 40 + 24 * (LAYERS - 1 - layer)
        shifts_grad.append(summed[base : base + 8].reshape(FF))
        wide_sums = summed[base + 8 : base + 16]
        mix_sums = summed[base + 16 : base + 24]
        gains_grad.append(jnp.stack([mix_sums[0], wide_sums[0]]))
        biases_grad.append(
            jnp.stack([mix_sums[1], wide_sums[1], mix_sums[2], mix_sums[3], wide_sums[2], wide_sums[3]])
        )
    totals = summed[35]
    return (
        activations,
        grad,
        jnp.stack(attn_grads),
        jnp.stack(up_grads),
        jnp.stack(down_grads),
        jnp.stack(gains_grad),
        jnp.stack(biases_grad),
        jnp.stack(shifts_grad),
        summed[:VOCAB].T,
        summed[32],
        summed[33],
        summed[34, :VOCAB],
        totals[0] / totals[2],
        totals[1] / totals[2],
        totals[2].astype(jnp.int32),
    )


def solution(mesh):
    fsdp, dp = mesh.shape["fsdp"], mesh.shape["dp"]
    fine = Mesh(mesh.devices.reshape(fsdp // 2, 2, dp // 2, 2), ("z", "y", "x", "c"))
    tokens = ("z", "y", "x", "c")
    flat = P(None, ("z", "y"), None)
    placed = (P(tokens, None), P(tokens), P(tokens), P(tokens), flat, flat, flat) + (P(),) * 7

    def run(*arrays):
        return local(fsdp, *arrays)

    return jax.shard_map(
        run,
        mesh=fine,
        in_specs=placed,
        out_specs=(P(tokens, None), P(tokens, None), flat, flat, flat) + (P(),) * 10,
        check_vma=False,
    )
```

```python
import math

import jax
import jax.numpy as jnp
from jax import lax
from jax.experimental import pallas as pl
from jax.experimental.pallas import tpu as pltpu
from jax.sharding import Mesh
from jax.sharding import PartitionSpec as P

D = 640
HEADS = 20
HEAD_DIM = 32
FF = 5120
VOCAB = 25
LAYERS = 2
LEN = 128
SEQ_DEV = 4
ROWS = SEQ_DEV * LEN
TILE = 640
TILES = FF // TILE
GROUPS = HEADS * HEAD_DIM // 128
PER_GROUP = 128 // HEAD_DIM
CHUNK = 128
BF = jnp.bfloat16
F32 = jnp.float32
MIB = 2**20

SMEM_SPEC = pl.BlockSpec(memory_space=pltpu.SMEM)
ANY_SPEC = pl.BlockSpec(memory_space=pl.ANY)


def dot(left, right, dims):
    return lax.dot_general(left, right, (dims, ((), ())), preferred_element_type=F32)


def mul_nn(left, right):
    return dot(left, right, ((1,), (0,)))


def mul_nt(left, right):
    return dot(left, right, ((1,), (1,)))


def mul_tn(left, right):
    return dot(left, right, ((0,), (0,)))


def normalize(values):
    centered = values - jnp.mean(values, -1, keepdims=True)
    inverse = lax.rsqrt(jnp.mean(centered * centered, -1, keepdims=True) + 1e-05)
    return (centered * inverse, inverse)


def norm_back(grad_normed, normed, inverse):
    return inverse * (
        grad_normed
        - jnp.mean(grad_normed, -1, keepdims=True)
        - normed * jnp.mean(grad_normed * normed, -1, keepdims=True)
    )


def col_sum(values):
    return jnp.sum(values, 0, keepdims=True)


def sds(shape, dtype):
    return jax.ShapeDtypeStruct(shape, dtype)


def whole_block(shape):
    zeros = (0,) * len(shape)
    return pl.BlockSpec(shape, lambda *_: zeros)


def over_chunks(body, start):
    def step(index, carry):
        return body(pl.ds(pl.multiple_of(index * CHUNK, CHUNK), CHUNK), carry)

    return lax.fori_loop(0, ROWS // CHUNK, step, start)


def quarter_copies(place_ref, buffers, held, sems):
    x_at, y_at, c_at = place_ref[0], place_ref[1], place_ref[2]
    copies = []
    for number, buffer in enumerate(buffers):
        quarter = (x_at ^ (number >> 1)) * 2 + (c_at ^ (number & 1))
        for dy in range(2):
            copies.append(
                pltpu.make_async_copy(
                    buffer.at[dy], held.at[quarter, :, y_at ^ dy], sems.at[2 * number + dy]
                )
            )
    return copies


def square(values):
    return values.reshape(D, values.shape[-1])


def head_masks():
    lanes = lax.broadcasted_iota(jnp.int32, (LEN, 128), 1) // HEAD_DIM
    return [(lanes == member) for member in range(PER_GROUP)]


def stack_heads(values, masks):
    zero = jnp.zeros_like(values)
    return jnp.concatenate([jnp.where(mask, values, zero) for mask in masks], 0)


def unstack_heads(values):
    parts = [
        values[HEAD_DIM * member : HEAD_DIM * (member + 1), LEN * member : LEN * (member + 1)]
        for member in range(PER_GROUP)
    ]
    return jnp.concatenate(parts, 0).T


def scores_of(keys, queries, valid):
    scores = mul_nt(keys, queries) * (1.0 / math.sqrt(HEAD_DIM))
    return jnp.where(valid, scores, -1e30)


def mix_kernel(
    place_ref,
    lengths_ref,
    residual_ref,
    w0_ref,
    w1_ref,
    w2_ref,
    w3_ref,
    gains_ref,
    biases_ref,
    packed_ref,
    log_ref,
    mixed_ref,
    middle_ref,
    second_ref,
    held,
    pre_ref,
    sems,
):
    copies = quarter_copies(place_ref, (w0_ref, w1_ref, w2_ref, w3_ref), held, sems)
    for copy in copies:
        copy.start()

    def first(rows, carry):
        normed, inverse = normalize(residual_ref[rows, :].astype(F32))
        pre_ref[rows, :] = (normed * gains_ref[0:1, :] + biases_ref[0:1, :]).astype(BF)
        return carry

    over_chunks(first, 0)
    for copy in copies:
        copy.wait()
    shifts = (biases_ref[2:3, :], None, biases_ref[3:4, :])
    for part in range(3):
        result = mul_nn(pre_ref[...], square(held[part]))
        if shifts[part] is not None:
            result = result + shifts[part]
        packed_ref[:, part * D : (part + 1) * D] = result.astype(BF)
    masks = head_masks()
    row_ids = lax.broadcasted_iota(jnp.int32, (LEN, 1), 0)

    def one_sequence(seq, carry):
        rows = pl.ds(pl.multiple_of(seq * LEN, LEN), LEN)
        valid = row_ids < lengths_ref[seq]
        for group in range(GROUPS):
            lanes = slice(group * 128, (group + 1) * 128)
            queries = stack_heads(packed_ref[rows, lanes], masks)
            key_rows = packed_ref[rows, D + group * 128 : D + (group + 1) * 128]
            value_rows = packed_ref[rows, 2 * D + group * 128 : 2 * D + (group + 1) * 128]
            scores = scores_of(key_rows, queries, valid)
            top = jnp.max(scores, 0, keepdims=True)
            expos = jnp.exp(scores - top)
            total = jnp.sum(expos, 0, keepdims=True)
            probs = (expos * (1.0 / total)).astype(BF)
            log_ref[seq * GROUPS + group] = top + jnp.log(total)
            mixed_ref[rows, lanes] = unstack_heads(mul_tn(value_rows, probs)).astype(BF)
        return carry

    lax.fori_loop(0, SEQ_DEV, one_sequence, 0)
    middle_ref[...] = mul_nn(mixed_ref[...], square(held[3])) + biases_ref[4:5, :]

    def last(rows, carry):
        middle = middle_ref[rows, :] + residual_ref[rows, :].astype(F32)
        middle_ref[rows, :] = middle
        normed, inverse = normalize(middle)
        second_ref[rows, :] = (normed * gains_ref[1:2, :] + biases_ref[1:2, :]).astype(BF)
        return carry

    over_chunks(last, 0)


def mix(place, lengths, residual, quarters, gains, biases):
    return pl.pallas_call(
        mix_kernel,
        out_shape=(
            sds((ROWS, 3 * D), BF),
            sds((SEQ_DEV * GROUPS, 1, PER_GROUP * LEN), F32),
            sds((ROWS, D), BF),
            sds((ROWS, D), F32),
            sds((ROWS, D), BF),
        ),
        grid=(1,),
        in_specs=[SMEM_SPEC, SMEM_SPEC, whole_block((ROWS, D))]
        + [ANY_SPEC] * 4
        + [whole_block((2, D)), whole_block((6, D))],
        out_specs=(
            whole_block((ROWS, 3 * D)),
            whole_block((SEQ_DEV * GROUPS, 1, PER_GROUP * LEN)),
            whole_block((ROWS, D)),
            whole_block((ROWS, D)),
            whole_block((ROWS, D)),
        ),
        scratch_shapes=[
            pltpu.VMEM((4, 4, 2, D // 8, D), BF),
            pltpu.VMEM((ROWS, D), BF),
            pltpu.SemaphoreType.DMA((8,)),
        ],
        compiler_params=pltpu.CompilerParams(vmem_limit_bytes=26 * MIB),
        cost_estimate=pl.CostEstimate(
            flops=2 * ROWS * D * 4 * D * 4, bytes_accessed=10 * MIB, transcendentals=0
        ),
    )(place, lengths, residual, *quarters, gains, biases)


def up_kernel(place_ref, second_ref, *refs):
    buffers, (shift_ref, active_ref, slope_ref, held, sems) = refs[:8], refs[8:]
    tile = pl.program_id(0)

    @pl.when(tile == 0)
    def _():
        for number, buffer in enumerate(buffers):
            dx, dc, half = number // 4, number // 2 % 2, number % 2
            at = ((place_ref[0] ^ dx) * 2 + (place_ref[2] ^ dc)) * 2 + half
            for dy in range(2):
                pltpu.make_async_copy(
                    buffer.at[dy], held.at[at, :, place_ref[1] ^ dy], sems.at[at, dy]
                ).start()

    for dy in range(2):
        pltpu.make_async_copy(buffers[0].at[dy], held.at[tile, :, dy], sems.at[tile, dy]).wait()
    up_tile = square(held[tile])
    shift = shift_ref[pl.ds(tile, 1), :]
    for chunk in range(ROWS // CHUNK):
        rows = slice(chunk * CHUNK, (chunk + 1) * CHUNK)
        hidden = mul_nn(second_ref[rows, :], up_tile) + shift
        phi = 0.5 + 0.5 * lax.erf(hidden * math.sqrt(0.5))
        density = jnp.exp(hidden * hidden * -0.5) * (1.0 / math.sqrt(2.0 * math.pi))
        active_ref[0, rows, :] = (hidden * phi).astype(BF)
        slope_ref[0, rows, :] = (phi + hidden * density).astype(BF)


def up(place, second, parts, shift):
    tile_block = pl.BlockSpec((1, ROWS, TILE), lambda tile: (tile, 0, 0))
    return pl.pallas_call(
        up_kernel,
        grid=(TILES,),
        out_shape=(sds((TILES, ROWS, TILE), BF), sds((TILES, ROWS, TILE), BF)),
        in_specs=[SMEM_SPEC, whole_block((ROWS, D))]
        + [ANY_SPEC] * 8
        + [whole_block((TILES, TILE))],
        out_specs=(tile_block, tile_block),
        scratch_shapes=[
            pltpu.VMEM((TILES, 4, 2, D // 8, TILE), BF),
            pltpu.SemaphoreType.DMA((TILES, 2)),
        ],
        compiler_params=pltpu.CompilerParams(vmem_limit_bytes=26 * MIB),
        cost_estimate=pl.CostEstimate(
            flops=2 * ROWS * D * FF * 4, bytes_accessed=20 * MIB, transcendentals=0
        ),
    )(place, second, *parts, shift)


def down_kernel(
    place_ref, middle_ref, active_ref, d0_ref, d1_ref, biases_ref, out_ref, held, rows, sems, row_sems
):
    tile = pl.program_id(0)

    @pl.when(tile == 0)
    def _():
        for at in range(TILES):
            for number, buffer in enumerate((d0_ref, d1_ref)):
                pltpu.make_async_copy(
                    buffer.at[at], held.at[at, place_ref[2] ^ number], sems.at[at, number]
                ).start()
            pltpu.make_async_copy(active_ref.at[at], rows.at[at], row_sems.at[at]).start()
        out_ref[...] = middle_ref[...] + biases_ref[5:6, :]

    for number in range(2):
        pltpu.make_async_copy(d0_ref.at[tile], held.at[tile, number], sems.at[tile, number]).wait()
    pltpu.make_async_copy(active_ref.at[0], rows.at[tile], row_sems.at[tile]).wait()
    out_ref[...] += mul_nn(rows[tile], square(held[tile]))


def down(place, middle, active, parts, biases):
    return pl.pallas_call(
        down_kernel,
        grid=(TILES,),
        out_shape=sds((ROWS, D), F32),
        in_specs=[
            SMEM_SPEC,
            whole_block((ROWS, D)),
            ANY_SPEC,
            ANY_SPEC,
            ANY_SPEC,
            whole_block((6, D)),
        ],
        out_specs=whole_block((ROWS, D)),
        scratch_shapes=[
            pltpu.VMEM((TILES, 2, TILE // 2, D), BF),
            pltpu.VMEM((TILES, ROWS, TILE), BF),
            pltpu.SemaphoreType.DMA((TILES, 2)),
            pltpu.SemaphoreType.DMA((TILES,)),
        ],
        compiler_params=pltpu.CompilerParams(vmem_limit_bytes=24 * MIB),
        cost_estimate=pl.CostEstimate(
            flops=2 * ROWS * D * FF, bytes_accessed=14 * MIB, transcendentals=0
        ),
    )(place, middle, active, *parts, biases)


def head_kernel(
    residual_ref,
    targets_ref,
    masked_ref,
    weight_ref,
    shift_ref,
    gain_ref,
    move_ref,
    activations_ref,
    grad_ref,
    rounded_ref,
    small_ref,
):
    small_ref[...] = jnp.zeros_like(small_ref)
    lanes = lax.broadcasted_iota(jnp.int32, (1, 128), 1)

    def body(rows, carry):
        weight_grad, gain_grad, move_grad, shift_grad, stats = carry
        residual = residual_ref[rows, :]
        activations_ref[rows, :] = residual.astype(BF)
        normed, inverse = normalize(residual)
        final = (normed * gain_ref[...] + move_ref[...]).astype(BF)
        logits = mul_nn(final, weight_ref[...]) + shift_ref[...]
        top = jnp.max(logits, -1, keepdims=True)
        log_total = top + jnp.log(jnp.sum(jnp.exp(logits - top), -1, keepdims=True))
        onehot = (targets_ref[rows, :] == lanes).astype(F32)
        picked = jnp.sum(logits * onehot, -1, keepdims=True)
        mask = masked_ref[rows, :].astype(F32)
        loss = col_sum(mask * (log_total - picked))
        hits = col_sum(mask * jnp.exp(picked - log_total))
        count = col_sum(mask)
        stats = stats + (
            jnp.where(lanes == 0, loss, 0.0)
            + jnp.where(lanes == 1, hits, 0.0)
            + jnp.where(lanes == 2, count, 0.0)
        )
        grad_logits = (mask * (jnp.exp(logits - log_total) - onehot)).astype(BF)
        weight_grad = weight_grad + mul_tn(grad_logits, final)
        shift_grad = shift_grad + col_sum(grad_logits.astype(F32))
        grad_final = mul_nt(grad_logits, weight_ref[...])
        gain_grad = gain_grad + col_sum(grad_final * normed)
        move_grad = move_grad + col_sum(grad_final)
        grad = norm_back(grad_final * gain_ref[...], normed, inverse)
        grad_ref[rows, :] = grad
        rounded_ref[rows, :] = grad.astype(BF)
        return weight_grad, gain_grad, move_grad, shift_grad, stats

    row = jnp.zeros((1, D), F32)
    narrow = jnp.zeros((1, 128), F32)
    weight_grad, gain_grad, move_grad, shift_grad, stats = over_chunks(
        body, (jnp.zeros((128, D), F32), row, row, narrow, narrow)
    )
    small_ref[0:32, :] = weight_grad[0:32, :]
    small_ref[32:33, :] = gain_grad
    small_ref[33:34, :] = move_grad
    small_ref[34:35, 0:128] = shift_grad
    small_ref[35:36, 0:128] = stats


def head(residual, targets, masked, weight, shift, gain, move):
    return pl.pallas_call(
        head_kernel,
        out_shape=(
            sds((ROWS, D), BF),
            sds((ROWS, D), F32),
            sds((ROWS, D), BF),
            sds((40, D), F32),
        ),
        grid=(1,),
        in_specs=[
            whole_block((ROWS, D)),
            whole_block((ROWS, 1)),
            whole_block((ROWS, 1)),
            whole_block((D, 128)),
            whole_block((1, 128)),
            whole_block((1, D)),
            whole_block((1, D)),
        ],
        out_specs=(whole_block((ROWS, D)),) * 3 + (whole_block((40, D)),),
        compiler_params=pltpu.CompilerParams(vmem_limit_bytes=16 * MIB),
        cost_estimate=pl.CostEstimate(
            flops=2 * ROWS * D * 128 * 8, bytes_accessed=5 * MIB, transcendentals=0
        ),
    )(residual, targets, masked, weight, shift, gain, move)


def down_back_kernel(place_ref, grad_ref, active_ref, send_ref, keep_ref, turned, held, sems):
    step = pl.program_id(0)

    @pl.when(step == 0)
    def _():
        for at in range(TILES):
            tile = (at % 4) * 2 + (place_ref[1] ^ (1 - at // 4))
            pltpu.make_async_copy(active_ref.at[tile], held.at[at], sems.at[at]).start()
        for half in range(2):
            turned[half] = grad_ref[:, half * (D // 2) : (half + 1) * (D // 2)].T

    pltpu.make_async_copy(active_ref.at[0], held.at[step], sems.at[step]).wait()
    c_at = place_ref[2]
    active = held[step]
    send_ref[0, 0] = mul_nn(turned[1 - c_at], active).astype(BF)
    keep_ref[0, 0] = mul_nn(turned[c_at], active).astype(BF)


def down_back(place, grad, active):
    block = pl.BlockSpec((1, 1, D // 2, TILE), lambda step: (1 - step // 4, step % 4, 0, 0))
    out = sds((2, 4, D // 2, TILE), BF)
    return pl.pallas_call(
        down_back_kernel,
        grid=(TILES,),
        in_specs=[SMEM_SPEC, whole_block((ROWS, D)), ANY_SPEC],
        out_specs=(block, block),
        scratch_shapes=[
            pltpu.VMEM((2, D // 2, ROWS), BF),
            pltpu.VMEM((TILES, ROWS, TILE), BF),
            pltpu.SemaphoreType.DMA((TILES,)),
        ],
        out_shape=(out, out),
        compiler_params=pltpu.CompilerParams(vmem_limit_bytes=20 * MIB),
        cost_estimate=pl.CostEstimate(
            flops=2 * ROWS * D * FF, bytes_accessed=13 * MIB, transcendentals=0
        ),
    )(place, grad, active)


def wide_back_tile(phase, step, place_ref):
    quarter = (place_ref[0] ^ (1 - step // 2)) * 2 + (place_ref[2] ^ (1 - phase))
    return quarter * 2 + step % 2


def wide_back_step(
    phase, step, place_ref, rounded_ref, second_ref, slope_ref, ups, downs, held_up, held_down,
    up_sems, down_sems, turned, shift_ref, store, total_ref, slopes, slope_sems
):
    y_at, c_at = place_ref[1], place_ref[2]

    @pl.when(step == 0)
    def _():
        for at in range(4):
            tile = wide_back_tile(phase, at, place_ref)
            for number, buffer in enumerate(downs):
                pltpu.make_async_copy(
                    buffer.at[tile], held_down.at[at, c_at ^ number], down_sems.at[at, number]
                ).start()
            for dy in range(2):
                pltpu.make_async_copy(
                    ups[(1 - at // 2) * 2 + at % 2].at[dy],
                    held_up.at[at, :, y_at ^ dy],
                    up_sems.at[at, dy],
                ).start()
            pltpu.make_async_copy(slope_ref.at[tile], slopes.at[at], slope_sems.at[at]).start()
        turned[...] = second_ref[...].T

    for number in range(2):
        pltpu.make_async_copy(
            downs[0].at[0], held_down.at[step, number], down_sems.at[step, number]
        ).wait()
    for dy in range(2):
        pltpu.make_async_copy(
            ups[0].at[dy], held_up.at[step, :, dy], up_sems.at[step, dy]
        ).wait()
    grad_active = mul_nt(rounded_ref[...], square(held_down[step]))
    pltpu.make_async_copy(slope_ref.at[0], slopes.at[step], slope_sems.at[step]).wait()
    grad_hidden = (grad_active * slopes[step].astype(F32)).astype(BF)
    shift_ref[pl.ds(step, 1), :] = col_sum(grad_hidden.astype(F32))
    total_ref[...] += mul_nt(grad_hidden, square(held_up[step]))
    store(mul_nn(turned[...], grad_hidden).reshape(4, 2, D // 8, TILE))


def wide_back_first_kernel(
    place_ref,
    rounded_ref,
    second_ref,
    slope_ref,
    u0_ref,
    u1_ref,
    u2_ref,
    u3_ref,
    d0_ref,
    d1_ref,
    send_ref,
    shift_ref,
    total_ref,
    held_up,
    held_down,
    turned,
    up_sems,
    down_sems,
    slopes,
    slope_sems,
):
    step = pl.program_id(0)

    @pl.when(step == 0)
    def _():
        total_ref[...] = jnp.zeros_like(total_ref)

    def store(up_grad):
        for side in range(2):
            send_ref[0, side ^ place_ref[1], :, 0] = up_grad[:, side].astype(BF)

    wide_back_step(
        0, step, place_ref, rounded_ref, second_ref, slope_ref,
        (u0_ref, u1_ref, u2_ref, u3_ref), (d0_ref, d1_ref),
        held_up, held_down, up_sems, down_sems, turned, shift_ref, store, total_ref, slopes, slope_sems
    )


def wide_back_last_kernel(
    place_ref,
    rounded_ref,
    second_ref,
    slope_ref,
    u0_ref,
    u1_ref,
    u2_ref,
    u3_ref,
    d0_ref,
    d1_ref,
    before_ref,
    grad_ref,
    middle_ref,
    gains_ref,
    got_ref,
    pass_ref,
    keep_ref,
    shift_ref,
    middle_grad_ref,
    middle_rounded_ref,
    small_ref,
    held_up,
    held_down,
    turned,
    up_sems,
    down_sems,
    slopes,
    slope_sems,
    total,
):
    step = pl.program_id(0)

    @pl.when(step == 0)
    def _():
        total[...] = before_ref[...]

    def store(up_grad):
        def into(out_ref):
            for side in range(2):
                at = side ^ place_ref[1]
                out_ref[at, :, 0] = (up_grad[:, side] + got_ref[0, at, :, 0].astype(F32)).astype(BF)

        @pl.when(step < 2)
        def _():
            into(pass_ref)

        @pl.when(step >= 2)
        def _():
            into(keep_ref)

    wide_back_step(
        1, step, place_ref, rounded_ref, second_ref, slope_ref,
        (u0_ref, u1_ref, u2_ref, u3_ref), (d0_ref, d1_ref),
        held_up, held_down, up_sems, down_sems, turned, shift_ref, store, total, slopes, slope_sems
    )

    @pl.when(step == 3)
    def _():
        def body(rows, carry):
            gain_sum, move_sum, out_sum, down_sum = carry
            normed, inverse = normalize(middle_ref[rows, :])
            grad_second = total[rows, :]
            grad = grad_ref[rows, :] + norm_back(grad_second * gains_ref[1:2, :], normed, inverse)
            rounded = grad.astype(BF)
            middle_grad_ref[rows, :] = grad
            middle_rounded_ref[rows, :] = rounded
            return (
                gain_sum + col_sum(grad_second * normed),
                move_sum + col_sum(grad_second),
                out_sum + col_sum(rounded.astype(F32)),
                down_sum + col_sum(rounded_ref[rows, :].astype(F32)),
            )

        row = jnp.zeros((1, D), F32)
        sums = over_chunks(body, (row, row, row, row))
        small_ref[...] = jnp.zeros_like(small_ref)
        for number in range(4):
            small_ref[number : number + 1, :] = sums[number]


def wide_back_call(kernel, in_specs, out_specs, out_shape, scratch, arrays):
    full = whole_block((ROWS, D))
    return pl.pallas_call(
        kernel,
        grid_spec=pltpu.PrefetchScalarGridSpec(
            num_scalar_prefetch=1,
            grid=(4,),
            in_specs=[full] * 2 + [ANY_SPEC] * 7 + in_specs,
            out_specs=out_specs,
            scratch_shapes=[
                pltpu.VMEM((4, 4, 2, D // 8, TILE), BF),
                pltpu.VMEM((4, 2, TILE // 2, D), BF),
                pltpu.VMEM((D, ROWS), BF),
                pltpu.SemaphoreType.DMA((4, 2)),
                pltpu.SemaphoreType.DMA((4, 2)),
                pltpu.VMEM((4, ROWS, TILE), BF),
                pltpu.SemaphoreType.DMA((4,)),
            ]
            + scratch,
        ),
        out_shape=out_shape,
        compiler_params=pltpu.CompilerParams(vmem_limit_bytes=32 * MIB),
        cost_estimate=pl.CostEstimate(
            flops=2 * ROWS * D * FF * 2, bytes_accessed=18 * MIB, transcendentals=0
        ),
    )(*arrays)


def wide_back_block():
    return pl.BlockSpec(
        (1, 2, 4, 1, D // 8, TILE), lambda step, place_ref: (1 - step // 2, 0, 0, step % 2, 0, 0)
    )


def wide_back_first(place, rounded, second, slope, up_parts, down_parts):
    return wide_back_call(
        wide_back_first_kernel,
        [],
        (wide_back_block(), whole_block((4, TILE)), whole_block((ROWS, D))),
        (sds((2, 2, 4, 2, D // 8, TILE), BF), sds((4, TILE), F32), sds((ROWS, D), F32)),
        [],
        (place, rounded, second, slope, *up_parts[2:4], *up_parts[6:8], *down_parts),
    )


def wide_back_last(
    place, rounded, second, slope, up_parts, down_parts, before, grad, middle, gains, got
):
    full = whole_block((ROWS, D))
    out = sds((2, 4, 2, D // 8, TILE), BF)
    block = (2, 4, 1, D // 8, TILE)
    return wide_back_call(
        wide_back_last_kernel,
        [full] * 3 + [whole_block((2, D)), wide_back_block()],
        (
            pl.BlockSpec(block, lambda step, place_ref: (0, 0, jnp.minimum(step, 1), 0, 0)),
            pl.BlockSpec(block, lambda step, place_ref: (0, 0, jnp.maximum(step - 2, 0), 0, 0)),
            whole_block((4, TILE)),
            full,
            full,
            whole_block((8, D)),
        ),
        (out, out, sds((4, TILE), F32), sds((ROWS, D), F32), sds((ROWS, D), BF), sds((8, D), F32)),
        [pltpu.VMEM((ROWS, D), F32)],
        (
            place, rounded, second, slope, *up_parts[0:2], *up_parts[4:6], *down_parts,
            before, grad, middle, gains, got
        ),
    )


def mix_back_kernel(
    place_ref,
    lengths_ref,
    rounded_ref,
    middle_grad_ref,
    residual_ref,
    w0_ref,
    w1_ref,
    w2_ref,
    w3_ref,
    packed_ref,
    log_ref,
    mixed_ref,
    gains_ref,
    biases_ref,
    send_ref,
    lefts_ref,
    rights_ref,
    grad_ref,
    grad_rounded_ref,
    small_ref,
    held,
    grad_mixed,
    total,
    sems,
):
    x_at, y_at, c_at = place_ref[0], place_ref[1], place_ref[2]
    copies = quarter_copies(place_ref, (w0_ref, w1_ref, w2_ref, w3_ref), held, sems)
    for copy in copies:
        copy.start()

    def send_grad(part):
        @pl.when(c_at ^ (part & 1) == 1)
        def _():
            left = lefts_ref[1 if part == 3 else 0]
            value = mul_nn(left, rights_ref[part]).astype(BF).reshape(4, 2, D // 8, D)
            for side in range(2):
                send_ref[x_at ^ (part >> 1), side ^ y_at] = value[:, side]

    lefts_ref[1] = mixed_ref[...].T
    rights_ref[3] = rounded_ref[...]
    send_grad(3)

    def first(rows, carry):
        normed, inverse = normalize(residual_ref[rows, :].astype(F32))
        total[rows, :] = normed * gains_ref[0:1, :] + biases_ref[0:1, :]
        return carry

    over_chunks(first, 0)
    lefts_ref[0] = total[...].astype(BF).T
    for copy in copies:
        copy.wait()
    grad_mixed[...] = mul_nt(rounded_ref[...], square(held[3])).astype(BF)
    masks = head_masks()
    row_ids = lax.broadcasted_iota(jnp.int32, (LEN, 1), 0)
    scale = 1.0 / math.sqrt(HEAD_DIM)

    def one_sequence(seq, carry):
        rows = pl.ds(pl.multiple_of(seq * LEN, LEN), LEN)
        valid = row_ids < lengths_ref[seq]
        for group in range(GROUPS):
            at_query = slice(group * 128, (group + 1) * 128)
            at_key = slice(D + group * 128, D + (group + 1) * 128)
            at_value = slice(2 * D + group * 128, 2 * D + (group + 1) * 128)
            queries = stack_heads(packed_ref[rows, at_query], masks)
            key_rows = packed_ref[rows, at_key]
            value_rows = packed_ref[rows, at_value]
            grads = stack_heads(grad_mixed[rows, at_query], masks)
            scores = scores_of(key_rows, queries, valid)
            probs = jnp.exp(scores - log_ref[seq * GROUPS + group])
            grad_probs = mul_nt(value_rows, grads)
            inner = jnp.sum(grad_probs * probs, 0, keepdims=True)
            grad_scores = (probs * (grad_probs - inner)).astype(BF)
            rights_ref[2, rows, at_query] = mul_nn(probs.astype(BF), grads).astype(BF)
            rights_ref[1, rows, at_query] = (mul_nn(grad_scores, queries) * scale).astype(BF)
            grad_queries = unstack_heads(mul_tn(key_rows, grad_scores))
            rights_ref[0, rows, at_query] = (grad_queries * scale).astype(BF)
        return carry

    lax.fori_loop(0, SEQ_DEV, one_sequence, 0)
    for part in range(3):
        send_grad(part)
        result = mul_nt(rights_ref[part], square(held[part]))
        if part == 0:
            total[...] = result
        else:
            total[...] += result

    def body(rows, carry):
        gain_sum, move_sum, query_sum, value_sum = carry
        normed, inverse = normalize(residual_ref[rows, :].astype(F32))
        grad_pre = total[rows, :]
        grad = middle_grad_ref[rows, :] + norm_back(grad_pre * gains_ref[0:1, :], normed, inverse)
        grad_ref[rows, :] = grad
        grad_rounded_ref[rows, :] = grad.astype(BF)
        return (
            gain_sum + col_sum(grad_pre * normed),
            move_sum + col_sum(grad_pre),
            query_sum + col_sum(rights_ref[0, rows, :].astype(F32)),
            value_sum + col_sum(rights_ref[2, rows, :].astype(F32)),
        )

    row = jnp.zeros((1, D), F32)
    sums = over_chunks(body, (row, row, row, row))
    small_ref[...] = jnp.zeros_like(small_ref)
    for number in range(4):
        small_ref[number : number + 1, :] = sums[number]


def mix_back(
    place, lengths, rounded, middle_grad, residual, quarters, packed, logs, mixed, gains, biases
):
    out = sds((2, 2, 4, D // 8, D), BF)
    return pl.pallas_call(
        mix_back_kernel,
        out_shape=(
            out,
            sds((2, D, ROWS), BF),
            sds((4, ROWS, D), BF),
            sds((ROWS, D), F32),
            sds((ROWS, D), BF),
            sds((8, D), F32),
        ),
        grid=(1,),
        in_specs=[SMEM_SPEC, SMEM_SPEC]
        + [whole_block((ROWS, D))] * 3
        + [ANY_SPEC] * 4
        + [
            whole_block((ROWS, 3 * D)),
            whole_block((SEQ_DEV * GROUPS, 1, PER_GROUP * LEN)),
            whole_block((ROWS, D)),
            whole_block((2, D)),
            whole_block((6, D)),
        ],
        out_specs=(
            whole_block((2, 2, 4, D // 8, D)),
            whole_block((2, D, ROWS)),
            whole_block((4, ROWS, D)),
            whole_block((ROWS, D)),
            whole_block((ROWS, D)),
            whole_block((8, D)),
        ),
        scratch_shapes=[
            pltpu.VMEM((4, 4, 2, D // 8, D), BF),
            pltpu.VMEM((ROWS, D), BF),
            pltpu.VMEM((ROWS, D), F32),
            pltpu.SemaphoreType.DMA((8,)),
        ],
        compiler_params=pltpu.CompilerParams(vmem_limit_bytes=40 * MIB),
        cost_estimate=pl.CostEstimate(
            flops=2 * ROWS * D * 4 * D * 8, bytes_accessed=18 * MIB, transcendentals=0
        ),
    )(
        place, lengths, rounded, middle_grad, residual, *quarters, packed, logs, mixed, gains, biases
    )


def mix_back_last_kernel(place_ref, left_ref, right_ref, got_ref, pass_ref, keep_ref):
    step = pl.program_id(0)
    y_at = place_ref[1]
    value = mul_nn(left_ref[0], right_ref[0]).reshape(4, 2, D // 8, D)

    def into(out_ref):
        for side in range(2):
            at = side ^ y_at
            out_ref[at] = (value[:, side] + got_ref[0, at].astype(F32)).astype(BF)

    @pl.when(step == 0)
    def _():
        into(pass_ref)

    @pl.when(step == 1)
    def _():
        into(keep_ref)


def mix_back_last(place, lefts, rights, got):
    def part(step, place_ref):
        return (place_ref[0] ^ (1 - step)) * 2 + place_ref[2]

    out = sds((2, 4, D // 8, D), BF)
    return pl.pallas_call(
        mix_back_last_kernel,
        grid_spec=pltpu.PrefetchScalarGridSpec(
            num_scalar_prefetch=1,
            grid=(2,),
            in_specs=[
                pl.BlockSpec(
                    (1, D, ROWS), lambda step, place_ref: (part(step, place_ref) // 3, 0, 0)
                ),
                pl.BlockSpec((1, ROWS, D), lambda step, place_ref: (part(step, place_ref), 0, 0)),
                pl.BlockSpec(
                    (1, 2, 4, D // 8, D), lambda step, place_ref: (1 - step, 0, 0, 0, 0)
                ),
            ],
            out_specs=(whole_block((2, 4, D // 8, D)),) * 2,
        ),
        out_shape=(out, out),
        compiler_params=pltpu.CompilerParams(vmem_limit_bytes=16 * MIB),
        cost_estimate=pl.CostEstimate(
            flops=2 * ROWS * D * 2 * D, bytes_accessed=6 * MIB, transcendentals=0
        ),
    )(place, lefts, rights, got)


def swap(value, axis):
    return lax.ppermute(value, axis, [(0, 1), (1, 0)])


def after(value, *others):
    return lax.optimization_barrier((value, others))[0]


class Order:
    def __init__(self):
        self.last = None

    def hold(self, *arrays):
        if self.last is not None:
            arrays, self.last = lax.optimization_barrier((arrays, self.last))
        return arrays

    def __call__(self, function, *arrays):
        results = function(*self.hold(*arrays))
        self.last = jax.tree.leaves(results)[0]
        return results


def wide_sum(*values):
    total = values[0].astype(F32)
    for value in values[1:]:
        total = total + value.astype(F32)
    return total


def rounded_sum(*values):
    return wide_sum(*values).astype(BF)


class Moves:
    def __init__(self, fsdp):
        self.z_size = fsdp // 2
        self.staged = fsdp == 8
        self.x_at = lax.axis_index("x")
        self.y_at = lax.axis_index("y")
        self.z_at = lax.axis_index("z")
        self.c_at = lax.axis_index("c")
        self.place = jnp.stack([self.x_at, self.y_at, self.c_at]).astype(jnp.int32)

    def hop(self, value, reach):
        return lax.ppermute(value, "z", [(at, at ^ reach) for at in range(self.z_size)])

    def ordered(self, bit, own, other):
        return jnp.where(bit == 0, jnp.stack([own, other]), jnp.stack([other, own]))

    def by_side(self, value):
        value = value.reshape(4, 2, *value.shape[1:]).swapaxes(0, 1)
        return jnp.where(self.y_at == 0, value, value[::-1])

    def by_shard(self, value):
        value = jnp.where(self.y_at == 0, value, value[::-1]).swapaxes(0, 1)
        return value.reshape(8, *value.shape[2:])

    def own_quarter(self, flat):
        shard = flat.reshape(D // 8, -1, 128)
        step = shard.shape[1] // 4
        own = lax.dynamic_slice_in_dim(shard, (self.x_at * 2 + self.c_at) * step, step, 1)
        return own.reshape(D // 8, step // 5, 5, 128).swapaxes(0, 1).reshape(-1, D // 8, D)

    def gather_quarters(self, flat):
        whole = lax.all_gather(flat, ("z", "y"), axis=0, tiled=True)
        whole = whole.reshape(8, D // 8, 4, -1, D).transpose(2, 0, 3, 1, 4)
        parts = []
        for number in range(4):
            quarter = (self.x_at ^ (number >> 1)) * 2 + (self.c_at ^ (number & 1))
            parts.append(self.by_side(lax.dynamic_index_in_dim(whole, quarter, 0, False)))
        return tuple(parts)

    def low_bit(self, own, other):
        return self.ordered(self.z_at % 2, own, other)

    def high_bit(self, own, other):
        line = self.ordered(self.z_at // 2, own, other)
        line = line.reshape(4, *own.shape[1:])
        return tuple(line[:, tile] for tile in range(line.shape[1]))

    def part_far(self, *parts):
        total = wide_sum(*parts)
        total = total.reshape(2, 2, *total.shape[1:])
        far = self.z_at // 2
        return tuple(
            lax.dynamic_index_in_dim(total, at, 0, False).astype(BF) for at in (1 - far, far)
        )

    def part_near(self, *parts):
        total = wide_sum(*parts)
        near = self.z_at % 2
        return tuple(
            lax.dynamic_index_in_dim(total, at, 0, False).astype(BF) for at in (1 - near, near)
        )

    def gather_halves(self, flat):
        if not self.staged:
            whole = lax.all_gather(flat, ("z", "y"), axis=0, tiled=True).reshape(8, 2, TILE // 2, D)
            return tuple(
                lax.dynamic_index_in_dim(whole, self.c_at ^ number, 1, False) for number in range(2)
            )
        plane = lax.all_gather(self.own_half(flat), ("z", "y"), axis=0, tiled=False)
        return (plane, swap(plane, "c"))

    def own_half(self, flat):
        own = lax.dynamic_slice_in_dim(flat, self.c_at * (TILE // 2) * 5, (TILE // 2) * 5, 0)
        return own.reshape(TILE // 2, D)

    def sum_all(self, value):
        value = value + swap(value, "c")
        value = value + swap(value, "x")
        value = value + swap(value, "y")
        reach = 1
        while reach < self.z_size:
            value = value + self.hop(value, reach)
            reach *= 2
        return value

    def along_z(self, part):
        return lax.psum_scatter(part, "z", scatter_dimension=0, tiled=False)

    def quarters_flat(self, own, beside):
        four = jnp.concatenate([own, beside])
        four = jnp.where(self.c_at == 0, four, four[jnp.array([1, 0, 3, 2])])
        four = jnp.where(self.x_at == 0, four, four[jnp.array([2, 3, 0, 1])])
        return four.transpose(2, 0, 1, 3).astype(F32).reshape(-1, 128)

    def halves_flat(self, own, other):
        both = self.ordered(self.c_at, own, other)
        return both.reshape(D, TILE).T.astype(F32).reshape(-1, 128)

    def plain_quarters(self, passed, keep):
        part = self.by_shard(rounded_sum(keep, swap(passed, "x")))
        part = part.transpose(0, 2, 1, 3).reshape(D, -1)
        part = lax.psum_scatter(part, ("z", "y"), scatter_dimension=0, tiled=True)
        parts = lax.all_gather(part, ("x", "c"), axis=0, tiled=False)
        return parts.swapaxes(0, 1).astype(F32).reshape(-1, 128)

    def plain_halves(self, part):
        part = self.by_shard(part).transpose(0, 2, 1)
        part = part.reshape(FF, D // 2)
        part = lax.psum_scatter(part, ("z", "y"), scatter_dimension=0, tiled=True).T
        part = rounded_sum(part, swap(part, "x"))
        return lax.all_gather(part, "c", axis=0, tiled=True).T.astype(F32).reshape(-1, 128)


def local(
    fsdp,
    inputs,
    targets,
    masked,
    lengths,
    attn_weight,
    up_weight,
    down_weight,
    norm_gains,
    layer_biases,
    up_bias,
    head_weight,
    final_gain,
    final_shift,
    head_bias,
):
    moves = Moves(fsdp)
    place = moves.place
    shifts = up_bias.reshape(LAYERS, TILES, TILE)
    saved = []

    def mix_on(layer, residual, quarters):
        return mix(place, lengths, residual, quarters, norm_gains[layer], layer_biases[layer])

    def prepared(targets, masked, head_weight, head_bias):
        wide_bias = head_bias.reshape(1, VOCAB)
        return (
            targets.reshape(ROWS, 1),
            masked.reshape(ROWS, 1),
            jnp.pad(head_weight, ((0, 0), (0, 128 - VOCAB))),
            jnp.pad(wide_bias, ((0, 0), (0, 128 - VOCAB)), constant_values=-1e30),
        )

    def up_on(layer, second, parts):
        return up(place, second, parts, shifts[layer])

    def down_on(layer, middle, active, parts):
        return down(place, middle, active, parts, layer_biases[layer])

    def two(own, other):
        return jnp.stack([own, other])

    run = Order()
    if moves.staged:
        a0 = run(moves.own_quarter, attn_weight[0])
        a0_near = moves.hop(a0, 1)
        u0 = run(moves.own_quarter, up_weight[0])
        u0_near = moves.hop(u0, 1)
        a0 = run(moves.low_bit, a0, a0_near)
        a0_far = moves.hop(a0, 2)
        u0 = run(moves.low_bit, u0, u0_near)
        u0_far = moves.hop(u0, 2)
        (a0,) = run(moves.high_bit, a0, a0_far)
        a0_y = swap(a0, "y")
        d0 = run(moves.own_half, down_weight[0])
        d0 = lax.all_gather(d0, ("z", "y"), axis=0, tiled=False)
        a0 = run(two, a0, a0_y)
        a0_x = swap(a0, "x")
        a0_c = swap(a0, "c")
        u00, u01 = run(moves.high_bit, u0, u0_far)
        u00_y, u01_y = swap(u00, "y"), swap(u01, "y")
        a1 = run(moves.own_quarter, attn_weight[1])
        a1_near = moves.hop(a1, 1)
        u1 = run(moves.own_quarter, up_weight[1])
        u1_near = moves.hop(u1, 1)
        u00 = run(two, u00, u00_y)
        u00_x = swap(u00, "x")
        u00_c = swap(u00, "c")
        a1 = run(moves.low_bit, a1, a1_near)
        a1_far = moves.hop(a1, 2)
        (a0_x,) = run.hold(a0_x)
        a0_xc = swap(a0_x, "c")
        u01 = run(two, u01, u01_y)
        u01_x = swap(u01, "x")
        u01_c = swap(u01, "c")
        u1 = run(moves.low_bit, u1, u1_near)
        u1_far = moves.hop(u1, 2)
        ready = run(prepared, targets, masked, head_weight, head_bias)
        quarters0 = (a0, a0_c, a0_x, a0_xc)
        mixed0 = run(lambda r, *q: mix_on(0, r, q), inputs, *quarters0)
        (a1,) = run(moves.high_bit, a1, a1_far)
        a1_y = swap(a1, "y")
        u00_x, = run.hold(u00_x)
        u00_xc = swap(u00_x, "c")
        a1 = run(two, a1, a1_y)
        a1_x = swap(a1, "x")
        a1_c = swap(a1, "c")
        u10, u11 = run(moves.high_bit, u1, u1_far)
        u10_y, u11_y = swap(u10, "y"), swap(u11, "y")
        u01_x, = run.hold(u01_x)
        u01_xc = swap(u01_x, "c")
        ups0 = (u00, u01, u00_c, u01_c, u00_x, u01_x, u00_xc, u01_xc)
        wide0 = run(lambda m, *p: up_on(0, m, p), mixed0[4], *ups0)
        (d0,) = run.hold(d0)
        d0_c = swap(d0, "c")
        d1 = run(moves.own_half, down_weight[1])
        d1 = lax.all_gather(d1, ("z", "y"), axis=0, tiled=False)
        u10 = run(two, u10, u10_y)
        u10_x = swap(u10, "x")
        u10_c = swap(u10, "c")
        u11 = run(two, u11, u11_y)
        u11_x = swap(u11, "x")
        u11_c = swap(u11, "c")
        residual1 = run(lambda m, a, *p: down_on(0, m, a, p), mixed0[3], wide0[0], d0, d0_c)
        (a1_x,) = run.hold(a1_x)
        a1_xc = swap(a1_x, "c")
        quarters1 = (a1, a1_c, a1_x, a1_xc)
        mixed1 = run(lambda r, *q: mix_on(1, r, q), residual1, *quarters1)
        u10_x, u11_x = run.hold(u10_x, u11_x)
        u10_xc, u11_xc = swap(u10_x, "c"), swap(u11_x, "c")
        ups1 = (u10, u11, u10_c, u11_c, u10_x, u11_x, u10_xc, u11_xc)
        wide1 = run(lambda m, *p: up_on(1, m, p), mixed1[4], *ups1)
        (d1,) = run.hold(d1)
        d1_c = swap(d1, "c")
        residual = run(lambda m, a, *p: down_on(1, m, a, p), mixed1[3], wide1[0], d1, d1_c)
        weights = [(quarters0, ups0, (d0, d0_c)), (quarters1, ups1, (d1, d1_c))]
        saved = [(inputs, *mixed0, *wide0), (residual1, *mixed1, *wide1)]
    else:
        weights = []
        for layer in range(LAYERS):
            attn_parts = moves.gather_quarters(attn_weight[layer])
            up_parts = moves.gather_quarters(up_weight[layer])
            weights.append(
                (
                    [part[:, :, 0] for part in attn_parts],
                    [up_parts[number][:, :, tile] for number in range(4) for tile in range(2)],
                    moves.gather_halves(down_weight[layer]),
                )
            )
        residual = inputs
        for layer in range(LAYERS):
            quarters, up_parts, down_parts = weights[layer]
            mixed = mix_on(layer, residual, quarters)
            wide = up_on(layer, mixed[4], up_parts)
            saved.append((residual, *mixed, *wide))
            residual = down_on(layer, mixed[3], wide[0], down_parts)
        ready = prepared(targets, masked, head_weight, head_bias)
    activations, grad, rounded, head_small = run(
        head, residual, *ready, final_gain.reshape(1, D), final_shift.reshape(1, D)
    )

    def down_at(layer, rounded):
        return down_back(place, rounded, saved[layer][6])

    def wide_first(layer, rounded):
        _, up_parts, down_parts = weights[layer]
        return wide_back_first(
            place, rounded, saved[layer][5], saved[layer][7], up_parts, down_parts
        )

    def wide_last(layer, rounded, before, grad, got):
        _, up_parts, down_parts = weights[layer]
        _, _, _, _, middle, second, _, slope = saved[layer]
        return wide_back_last(
            place, rounded, second, slope, up_parts, down_parts, before, grad, middle, norm_gains[layer], got
        )

    def mix_first(layer, rounded, middle_grad):
        residual, packed, logs, mixed, _, _, _, _ = saved[layer]
        return mix_back(
            place,
            lengths,
            rounded,
            middle_grad,
            residual,
            weights[layer][0],
            packed,
            logs,
            mixed,
            norm_gains[layer],
            layer_biases[layer],
        )

    def mix_last(lefts, rights, got):
        return mix_back_last(place, lefts, rights, got)

    def shift_rows(shift_send, shift_keep):
        send, keep = (part.reshape(2, 2, TILE)[::-1] for part in (shift_send, shift_keep))
        parts = moves.ordered(moves.c_at, keep, send).swapaxes(0, 1)
        return jnp.where(moves.x_at == 0, parts, parts[::-1]).reshape(TILES, TILE)

    def packed_small(head_small, *rest):
        small = [head_small]
        for layer in range(LAYERS):
            shift_send, shift_keep, wide_small, mix_small = rest[4 * layer : 4 * layer + 4]
            small += [shift_rows(shift_send, shift_keep), wide_small, mix_small]
        return jnp.concatenate(small, 0)

    def plus(own, other):
        return own + other

    if moves.staged:
        d1_send, d1_keep = run(lambda g: down_at(1, g), rounded)
        d1_c = swap(d1_send, "c")
        u1_send, *tail1 = run(lambda g: wide_first(1, g), rounded)
        u1_c = swap(u1_send, "c")
        d1_y = swap(run(rounded_sum, d1_keep[1], d1_c[1]), "y")
        u1_pass, u1_keep, shift_keep1, middle_grad, middle_rounded, wide_small1 = run(
            lambda *a: wide_last(1, *a), rounded, tail1[1], grad, u1_c
        )
        u1_x = swap(u1_pass, "x")
        a1_send, lefts, rights, grad, rounded, mix_small1 = run(
            lambda *a: mix_first(1, *a), middle_rounded, middle_grad
        )
        a1_c = swap(a1_send, "c")
        d1 = moves.along_z(run(rounded_sum, d1_keep[0], d1_c[0], d1_y))
        a1_pass, a1_keep = run(mix_last, lefts, rights, a1_c)
        a1_x = swap(a1_pass, "x")
        d0_send, d0_keep = run(lambda g: down_at(0, g), rounded)
        d0_c = swap(d0_send, "c")
        u0_send, *tail0 = run(lambda g: wide_first(0, g), rounded)
        u0_c = swap(u0_send, "c")
        u1_y = swap(run(rounded_sum, u1_keep[1], u1_x[1]), "y")
        d0_y = swap(run(rounded_sum, d0_keep[1], d0_c[1]), "y")
        u0_pass, u0_keep, shift_keep0, middle_grad, middle_rounded, wide_small0 = run(
            lambda *a: wide_last(0, *a), rounded, tail0[1], grad, u0_c
        )
        u0_x = swap(u0_pass, "x")
        u1 = moves.along_z(run(rounded_sum, u1_keep[0], u1_x[0], u1_y))
        a1_y = swap(run(rounded_sum, a1_keep[1], a1_x[1]), "y")
        (d1,) = run.hold(d1)
        d1_x = swap(d1, "x")
        a0_send, lefts, rights, grad, rounded, mix_small0 = run(
            lambda *a: mix_first(0, *a), middle_rounded, middle_grad
        )
        a0_c = swap(a0_send, "c")
        small = run(
            packed_small,
            head_small,
            *(tail0[0], shift_keep0, wide_small0, mix_small0),
            *(tail1[0], shift_keep1, wide_small1, mix_small1),
        )
        small_next = moves.hop(small, 2)
        a0_pass, a0_keep = run(mix_last, lefts, rights, a0_c)
        a0_x = swap(a0_pass, "x")
        small = run(plus, small, small_next)
        small_next = moves.hop(small, 1)
        d1 = run(rounded_sum, d1, d1_x)
        d1_c = swap(d1, "c")
        d0 = moves.along_z(run(rounded_sum, d0_keep[0], d0_c[0], d0_y))
        u0_y = swap(run(rounded_sum, u0_keep[1], u0_x[1]), "y")
        small = run(plus, small, small_next)
        small_next = swap(small, "c")
        a1_send, a1_stay = run(moves.part_far, a1_keep[0], a1_x[0], a1_y)
        a1_far = moves.hop(a1_send, 2)
        small = run(plus, small, small_next)
        a0_y = swap(run(rounded_sum, a0_keep[1], a0_x[1]), "y")
        small_next = swap(small, "x")
        down_grad1 = run(moves.halves_flat, d1, d1_c)
        a1_send, a1_stay = run(moves.part_near, a1_stay, a1_far)
        a1_near = moves.hop(a1_send, 1)
        u0_send, u0_stay = run(moves.part_far, u0_keep[0], u0_x[0], u0_y)
        u0_far = moves.hop(u0_send, 2)
        small = run(plus, small, small_next)
        small_next = swap(small, "y")
        last1 = run(lambda u, *a: jnp.concatenate([u, rounded_sum(*a)[None]]), u1, a1_stay, a1_near)
        last1_c = swap(last1, "c")
        a0_send, a0_stay = run(moves.part_far, a0_keep[0], a0_x[0], a0_y)
        a0_far = moves.hop(a0_send, 2)
        last1 = run(two, last1, last1_c)
        last1_x = swap(last1, "x")
        u0_send, u0_stay = run(moves.part_near, u0_stay, u0_far)
        u0_near = moves.hop(u0_send, 1)
        (d0,) = run.hold(d0)
        d0_x = swap(d0, "x")
        summed = run(plus, small, small_next)
        a0_send, a0_stay = run(moves.part_near, a0_stay, a0_far)
        a0_near = moves.hop(a0_send, 1)
        up_grad1 = run(moves.quarters_flat, last1[:, :2], last1_x[:, :2])
        attn_grad1 = run(moves.quarters_flat, last1[:, 2:], last1_x[:, 2:])
        d0 = run(rounded_sum, d0, d0_x)
        d0_c = swap(d0, "c")
        last0 = run(
            lambda u0, u1, a0, a1: jnp.concatenate([rounded_sum(u0, u1), rounded_sum(a0, a1)[None]]),
            *(u0_stay, u0_near, a0_stay, a0_near),
        )
        last0_c = swap(last0, "c")
        down_grad0 = run(moves.halves_flat, d0, d0_c)
        last0 = run(two, last0, last0_c)
        last0_x = swap(last0, "x")
        up_grad0 = run(moves.quarters_flat, last0[:, :2], last0_x[:, :2])
        attn_grad0 = run(moves.quarters_flat, last0[:, 2:], last0_x[:, 2:])
        attn_grads = [attn_grad0, attn_grad1]
        up_grads = [up_grad0, up_grad1]
        down_grads = [down_grad0, down_grad1]
    else:
        attn_grads, up_grads, down_grads, smalls = ([None] * LAYERS for _ in range(4))
        for layer in reversed(range(LAYERS)):
            send, keep = down_at(layer, rounded)
            down_grads[layer] = moves.plain_halves(rounded_sum(keep, swap(send, "c")))
            send, shift_send, before = wide_first(layer, rounded)
            passed, keep, shift_keep, middle_grad, middle_rounded, wide_small = wide_last(
                layer, rounded, before, grad, swap(send, "c")
            )
            up_grads[layer] = moves.plain_quarters(passed, keep)
            send, lefts, rights, grad, rounded, mix_small = mix_first(
                layer, middle_rounded, middle_grad
            )
            passed, keep = mix_last(lefts, rights, swap(send, "c"))
            attn_grads[layer] = moves.plain_quarters(passed[:, :, None], keep[:, :, None])
            smalls[layer] = (shift_send, shift_keep, wide_small, mix_small)
        summed = moves.sum_all(packed_small(head_small, *smalls[0], *smalls[1]))

    gains_grad, biases_grad, shifts_grad = [], [], []
    for layer in range(LAYERS):
        base = 40 + 24 * layer
        shifts_grad.append(summed[base : base + 8].reshape(FF))
        wide_sums = summed[base + 8 : base + 16]
        mix_sums = summed[base + 16 : base + 24]
        gains_grad.append(jnp.stack([mix_sums[0], wide_sums[0]]))
        biases_grad.append(
            jnp.stack([mix_sums[1], wide_sums[1], mix_sums[2], mix_sums[3], wide_sums[2], wide_sums[3]])
        )
    totals = summed[35]
    return (
        activations,
        grad,
        jnp.stack(attn_grads),
        jnp.stack(up_grads),
        jnp.stack(down_grads),
        jnp.stack(gains_grad),
        jnp.stack(biases_grad),
        jnp.stack(shifts_grad),
        summed[:VOCAB].T,
        summed[32],
        summed[33],
        summed[34, :VOCAB],
        totals[0] / totals[2],
        totals[1] / totals[2],
        totals[2].astype(jnp.int32),
    )


def solution(mesh):
    fsdp, dp = mesh.shape["fsdp"], mesh.shape["dp"]
    fine = Mesh(mesh.devices.reshape(fsdp // 2, 2, dp // 2, 2), ("z", "y", "x", "c"))
    tokens = ("z", "y", "x", "c")
    flat = P(None, ("z", "y"), None)
    placed = (P(tokens, None), P(tokens), P(tokens), P(tokens), flat, flat, flat) + (P(),) * 7

    def run(*arrays):
        return local(fsdp, *arrays)

    return jax.shard_map(
        run,
        mesh=fine,
        in_specs=placed,
        out_specs=(P(tokens, None), P(tokens, None), flat, flat, flat) + (P(),) * 10,
        check_vma=False,
    )
```

```python
import math

import jax
import jax.numpy as jnp
from jax import lax
from jax.experimental import pallas as pl
from jax.experimental.pallas import tpu as pltpu
from jax.sharding import Mesh
from jax.sharding import PartitionSpec as P

D = 640
HEADS = 20
HEAD_DIM = 32
FF = 5120
VOCAB = 25
LAYERS = 2
LEN = 128
SEQ_DEV = 4
ROWS = SEQ_DEV * LEN
TILE = 640
TILES = FF // TILE
GROUPS = HEADS * HEAD_DIM // 128
PER_GROUP = 128 // HEAD_DIM
CHUNK = 128
BF = jnp.bfloat16
F32 = jnp.float32
MIB = 2**20

SMEM_SPEC = pl.BlockSpec(memory_space=pltpu.SMEM)
ANY_SPEC = pl.BlockSpec(memory_space=pl.ANY)


def dot(left, right, dims):
    return lax.dot_general(left, right, (dims, ((), ())), preferred_element_type=F32)


def mul_nn(left, right):
    return dot(left, right, ((1,), (0,)))


def mul_nt(left, right):
    return dot(left, right, ((1,), (1,)))


def mul_tn(left, right):
    return dot(left, right, ((0,), (0,)))


def normalize(values):
    centered = values - jnp.mean(values, -1, keepdims=True)
    inverse = lax.rsqrt(jnp.mean(centered * centered, -1, keepdims=True) + 1e-05)
    return (centered * inverse, inverse)


def norm_back(grad_normed, normed, inverse):
    return inverse * (
        grad_normed
        - jnp.mean(grad_normed, -1, keepdims=True)
        - normed * jnp.mean(grad_normed * normed, -1, keepdims=True)
    )


def col_sum(values):
    return jnp.sum(values, 0, keepdims=True)


def sds(shape, dtype):
    return jax.ShapeDtypeStruct(shape, dtype)


def whole_block(shape):
    zeros = (0,) * len(shape)
    return pl.BlockSpec(shape, lambda *_: zeros)


def over_chunks(body, start):
    def step(index, carry):
        return body(pl.ds(pl.multiple_of(index * CHUNK, CHUNK), CHUNK), carry)

    return lax.fori_loop(0, ROWS // CHUNK, step, start)


def quarter_copies(place_ref, buffers, held, sems):
    x_at, y_at, c_at = place_ref[0], place_ref[1], place_ref[2]
    copies = []
    for number, buffer in enumerate(buffers):
        quarter = (x_at ^ (number >> 1)) * 2 + (c_at ^ (number & 1))
        for dy in range(2):
            copies.append(
                pltpu.make_async_copy(
                    buffer.at[dy], held.at[quarter, :, y_at ^ dy], sems.at[2 * number + dy]
                )
            )
    return copies


def square(values):
    return values.reshape(D, values.shape[-1])


def head_masks():
    lanes = lax.broadcasted_iota(jnp.int32, (LEN, 128), 1) // HEAD_DIM
    return [(lanes == member) for member in range(PER_GROUP)]


def stack_heads(values, masks):
    zero = jnp.zeros_like(values)
    return jnp.concatenate([jnp.where(mask, values, zero) for mask in masks], 0)


def unstack_heads(values):
    parts = [
        values[HEAD_DIM * member : HEAD_DIM * (member + 1), LEN * member : LEN * (member + 1)]
        for member in range(PER_GROUP)
    ]
    return jnp.concatenate(parts, 0).T


def scores_of(keys, queries, valid):
    scores = mul_nt(keys, queries) * (1.0 / math.sqrt(HEAD_DIM))
    return jnp.where(valid, scores, -1e30)


def mix_kernel(
    place_ref,
    lengths_ref,
    residual_ref,
    w0_ref,
    w1_ref,
    w2_ref,
    w3_ref,
    gains_ref,
    biases_ref,
    packed_ref,
    log_ref,
    mixed_ref,
    middle_ref,
    second_ref,
    held,
    pre_ref,
    sems,
):
    copies = quarter_copies(place_ref, (w0_ref, w1_ref, w2_ref, w3_ref), held, sems)
    for copy in copies:
        copy.start()

    def first(rows, carry):
        normed, inverse = normalize(residual_ref[rows, :].astype(F32))
        pre_ref[rows, :] = (normed * gains_ref[0:1, :] + biases_ref[0:1, :]).astype(BF)
        return carry

    over_chunks(first, 0)
    for copy in copies:
        copy.wait()
    shifts = (biases_ref[2:3, :], None, biases_ref[3:4, :])
    for part in range(3):
        result = mul_nn(pre_ref[...], square(held[part]))
        if shifts[part] is not None:
            result = result + shifts[part]
        packed_ref[:, part * D : (part + 1) * D] = result.astype(BF)
    masks = head_masks()
    row_ids = lax.broadcasted_iota(jnp.int32, (LEN, 1), 0)

    def one_sequence(seq, carry):
        rows = pl.ds(pl.multiple_of(seq * LEN, LEN), LEN)
        valid = row_ids < lengths_ref[seq]
        for group in range(GROUPS):
            lanes = slice(group * 128, (group + 1) * 128)
            queries = stack_heads(packed_ref[rows, lanes], masks)
            key_rows = packed_ref[rows, D + group * 128 : D + (group + 1) * 128]
            value_rows = packed_ref[rows, 2 * D + group * 128 : 2 * D + (group + 1) * 128]
            scores = scores_of(key_rows, queries, valid)
            top = jnp.max(scores, 0, keepdims=True)
            expos = jnp.exp(scores - top)
            total = jnp.sum(expos, 0, keepdims=True)
            probs = (expos * (1.0 / total)).astype(BF)
            log_ref[seq * GROUPS + group] = top + jnp.log(total)
            mixed_ref[rows, lanes] = unstack_heads(mul_tn(value_rows, probs)).astype(BF)
        return carry

    lax.fori_loop(0, SEQ_DEV, one_sequence, 0)
    middle_ref[...] = mul_nn(mixed_ref[...], square(held[3])) + biases_ref[4:5, :]

    def last(rows, carry):
        middle = middle_ref[rows, :] + residual_ref[rows, :].astype(F32)
        middle_ref[rows, :] = middle
        normed, inverse = normalize(middle)
        second_ref[rows, :] = (normed * gains_ref[1:2, :] + biases_ref[1:2, :]).astype(BF)
        return carry

    over_chunks(last, 0)


def mix(place, lengths, residual, quarters, gains, biases):
    return pl.pallas_call(
        mix_kernel,
        out_shape=(
            sds((ROWS, 3 * D), BF),
            sds((SEQ_DEV * GROUPS, 1, PER_GROUP * LEN), F32),
            sds((ROWS, D), BF),
            sds((ROWS, D), F32),
            sds((ROWS, D), BF),
        ),
        grid=(1,),
        in_specs=[SMEM_SPEC, SMEM_SPEC, whole_block((ROWS, D))]
        + [ANY_SPEC] * 4
        + [whole_block((2, D)), whole_block((6, D))],
        out_specs=(
            whole_block((ROWS, 3 * D)),
            whole_block((SEQ_DEV * GROUPS, 1, PER_GROUP * LEN)),
            whole_block((ROWS, D)),
            whole_block((ROWS, D)),
            whole_block((ROWS, D)),
        ),
        scratch_shapes=[
            pltpu.VMEM((4, 4, 2, D // 8, D), BF),
            pltpu.VMEM((ROWS, D), BF),
            pltpu.SemaphoreType.DMA((8,)),
        ],
        compiler_params=pltpu.CompilerParams(vmem_limit_bytes=60 * MIB),
        cost_estimate=pl.CostEstimate(flops=int((2 * ROWS * D * 4 * D * 4) * 0.1), bytes_accessed=int((10 * MIB) * 0.1), transcendentals=0),
    )(place, lengths, residual, *quarters, gains, biases)


def up_kernel(place_ref, second_ref, *refs):
    buffers, (shift_ref, active_ref, slope_ref, held, sems) = refs[:8], refs[8:]
    tile = pl.program_id(0)

    @pl.when(tile == 0)
    def _():
        for number, buffer in enumerate(buffers):
            dx, dc, half = number // 4, number // 2 % 2, number % 2
            at = ((place_ref[0] ^ dx) * 2 + (place_ref[2] ^ dc)) * 2 + half
            for dy in range(2):
                pltpu.make_async_copy(
                    buffer.at[dy], held.at[at, :, place_ref[1] ^ dy], sems.at[at, dy]
                ).start()

    for dy in range(2):
        pltpu.make_async_copy(buffers[0].at[dy], held.at[tile, :, dy], sems.at[tile, dy]).wait()
    up_tile = square(held[tile])
    shift = shift_ref[pl.ds(tile, 1), :]
    for chunk in range(ROWS // CHUNK):
        rows = slice(chunk * CHUNK, (chunk + 1) * CHUNK)
        hidden = mul_nn(second_ref[rows, :], up_tile) + shift
        phi = 0.5 + 0.5 * lax.erf(hidden * math.sqrt(0.5))
        density = jnp.exp(hidden * hidden * -0.5) * (1.0 / math.sqrt(2.0 * math.pi))
        active_ref[0, rows, :] = (hidden * phi).astype(BF)
        slope_ref[0, rows, :] = (phi + hidden * density).astype(BF)


def up(place, second, parts, shift):
    tile_block = pl.BlockSpec((1, ROWS, TILE), lambda tile: (tile, 0, 0))
    return pl.pallas_call(
        up_kernel,
        grid=(TILES,),
        out_shape=(sds((TILES, ROWS, TILE), BF), sds((TILES, ROWS, TILE), BF)),
        in_specs=[SMEM_SPEC, whole_block((ROWS, D))]
        + [ANY_SPEC] * 8
        + [whole_block((TILES, TILE))],
        out_specs=(tile_block, tile_block),
        scratch_shapes=[
            pltpu.VMEM((TILES, 4, 2, D // 8, TILE), BF),
            pltpu.SemaphoreType.DMA((TILES, 2)),
        ],
        compiler_params=pltpu.CompilerParams(vmem_limit_bytes=60 * MIB),
        cost_estimate=pl.CostEstimate(flops=int((2 * ROWS * D * FF * 4) * 0.1), bytes_accessed=int((20 * MIB) * 0.1), transcendentals=0),
    )(place, second, *parts, shift)


def down_kernel(
    place_ref, middle_ref, active_ref, d0_ref, d1_ref, biases_ref, out_ref, held, rows, sems, row_sems
):
    tile = pl.program_id(0)

    @pl.when(tile == 0)
    def _():
        for at in range(TILES):
            for number, buffer in enumerate((d0_ref, d1_ref)):
                pltpu.make_async_copy(
                    buffer.at[at], held.at[at, place_ref[2] ^ number], sems.at[at, number]
                ).start()
            pltpu.make_async_copy(active_ref.at[at], rows.at[at], row_sems.at[at]).start()
        out_ref[...] = middle_ref[...] + biases_ref[5:6, :]

    for number in range(2):
        pltpu.make_async_copy(d0_ref.at[tile], held.at[tile, number], sems.at[tile, number]).wait()
    pltpu.make_async_copy(active_ref.at[0], rows.at[tile], row_sems.at[tile]).wait()
    out_ref[...] += mul_nn(rows[tile], square(held[tile]))


def down(place, middle, active, parts, biases):
    return pl.pallas_call(
        down_kernel,
        grid=(TILES,),
        out_shape=sds((ROWS, D), F32),
        in_specs=[
            SMEM_SPEC,
            whole_block((ROWS, D)),
            ANY_SPEC,
            ANY_SPEC,
            ANY_SPEC,
            whole_block((6, D)),
        ],
        out_specs=whole_block((ROWS, D)),
        scratch_shapes=[
            pltpu.VMEM((TILES, 2, TILE // 2, D), BF),
            pltpu.VMEM((TILES, ROWS, TILE), BF),
            pltpu.SemaphoreType.DMA((TILES, 2)),
            pltpu.SemaphoreType.DMA((TILES,)),
        ],
        compiler_params=pltpu.CompilerParams(vmem_limit_bytes=60 * MIB),
        cost_estimate=pl.CostEstimate(flops=int((2 * ROWS * D * FF) * 0.1), bytes_accessed=int((14 * MIB) * 0.1), transcendentals=0),
    )(place, middle, active, *parts, biases)


def head_kernel(
    residual_ref,
    targets_ref,
    masked_ref,
    weight_ref,
    shift_ref,
    gain_ref,
    move_ref,
    activations_ref,
    grad_ref,
    rounded_ref,
    small_ref,
):
    small_ref[...] = jnp.zeros_like(small_ref)
    lanes = lax.broadcasted_iota(jnp.int32, (1, 128), 1)

    def body(rows, carry):
        weight_grad, gain_grad, move_grad, shift_grad, stats = carry
        residual = residual_ref[rows, :]
        activations_ref[rows, :] = residual.astype(BF)
        normed, inverse = normalize(residual)
        final = (normed * gain_ref[...] + move_ref[...]).astype(BF)
        logits = mul_nn(final, weight_ref[...]) + shift_ref[...]
        top = jnp.max(logits, -1, keepdims=True)
        log_total = top + jnp.log(jnp.sum(jnp.exp(logits - top), -1, keepdims=True))
        onehot = (targets_ref[rows, :] == lanes).astype(F32)
        picked = jnp.sum(logits * onehot, -1, keepdims=True)
        mask = masked_ref[rows, :].astype(F32)
        loss = col_sum(mask * (log_total - picked))
        hits = col_sum(mask * jnp.exp(picked - log_total))
        count = col_sum(mask)
        stats = stats + (
            jnp.where(lanes == 0, loss, 0.0)
            + jnp.where(lanes == 1, hits, 0.0)
            + jnp.where(lanes == 2, count, 0.0)
        )
        grad_logits = (mask * (jnp.exp(logits - log_total) - onehot)).astype(BF)
        weight_grad = weight_grad + mul_tn(grad_logits, final)
        shift_grad = shift_grad + col_sum(grad_logits.astype(F32))
        grad_final = mul_nt(grad_logits, weight_ref[...])
        gain_grad = gain_grad + col_sum(grad_final * normed)
        move_grad = move_grad + col_sum(grad_final)
        grad = norm_back(grad_final * gain_ref[...], normed, inverse)
        grad_ref[rows, :] = grad
        rounded_ref[rows, :] = grad.astype(BF)
        return weight_grad, gain_grad, move_grad, shift_grad, stats

    row = jnp.zeros((1, D), F32)
    narrow = jnp.zeros((1, 128), F32)
    weight_grad, gain_grad, move_grad, shift_grad, stats = over_chunks(
        body, (jnp.zeros((128, D), F32), row, row, narrow, narrow)
    )
    small_ref[0:32, :] = weight_grad[0:32, :]
    small_ref[32:33, :] = gain_grad
    small_ref[33:34, :] = move_grad
    small_ref[34:35, 0:128] = shift_grad
    small_ref[35:36, 0:128] = stats


def head(residual, targets, masked, weight, shift, gain, move):
    return pl.pallas_call(
        head_kernel,
        out_shape=(
            sds((ROWS, D), BF),
            sds((ROWS, D), F32),
            sds((ROWS, D), BF),
            sds((40, D), F32),
        ),
        grid=(1,),
        in_specs=[
            whole_block((ROWS, D)),
            whole_block((ROWS, 1)),
            whole_block((ROWS, 1)),
            whole_block((D, 128)),
            whole_block((1, 128)),
            whole_block((1, D)),
            whole_block((1, D)),
        ],
        out_specs=(whole_block((ROWS, D)),) * 3 + (whole_block((40, D)),),
        compiler_params=pltpu.CompilerParams(vmem_limit_bytes=60 * MIB),
        cost_estimate=pl.CostEstimate(flops=int((2 * ROWS * D * 128 * 8) * 0.1), bytes_accessed=int((5 * MIB) * 0.1), transcendentals=0),
    )(residual, targets, masked, weight, shift, gain, move)


def down_back_kernel(
    place_ref, grad_ref, active_ref, pass_ref, stay_ref, keep_ref, turned, held, sems
):
    step = pl.program_id(0)

    @pl.when(step == 0)
    def _():
        for at in range(TILES):
            tile = (at % 4) * 2 + (place_ref[1] ^ (1 - at // 4))
            pltpu.make_async_copy(active_ref.at[tile], held.at[at], sems.at[at]).start()
        for half in range(2):
            turned[half] = grad_ref[:, half * (D // 2) : (half + 1) * (D // 2)].T

    pltpu.make_async_copy(active_ref.at[0], held.at[step], sems.at[step]).wait()
    c_at = place_ref[2]
    active = held[step]
    send = mul_nn(turned[1 - c_at], active).astype(BF)

    @pl.when(step < 4)
    def _():
        pass_ref[0] = send

    @pl.when(step >= 4)
    def _():
        stay_ref[0] = send

    keep_ref[0, 0] = mul_nn(turned[c_at], active).astype(BF)


def down_back(place, grad, active):
    half = (1, D // 2, TILE)
    out = sds((4, D // 2, TILE), BF)
    return pl.pallas_call(
        down_back_kernel,
        grid=(TILES,),
        in_specs=[SMEM_SPEC, whole_block((ROWS, D)), ANY_SPEC],
        out_specs=(
            pl.BlockSpec(half, lambda step: (jnp.minimum(step, 3), 0, 0)),
            pl.BlockSpec(half, lambda step: (jnp.maximum(step - 4, 0), 0, 0)),
            pl.BlockSpec((1, *half), lambda step: (1 - step // 4, step % 4, 0, 0)),
        ),
        scratch_shapes=[
            pltpu.VMEM((2, D // 2, ROWS), BF),
            pltpu.VMEM((TILES, ROWS, TILE), BF),
            pltpu.SemaphoreType.DMA((TILES,)),
        ],
        out_shape=(out, out, sds((2, 4, D // 2, TILE), BF)),
        compiler_params=pltpu.CompilerParams(vmem_limit_bytes=60 * MIB),
        cost_estimate=pl.CostEstimate(flops=int((2 * ROWS * D * FF) * 0.1), bytes_accessed=int((13 * MIB) * 0.1), transcendentals=0),
    )(place, grad, active)


def wide_back_tile(phase, step, place_ref):
    quarter = (place_ref[0] ^ (1 - step // 2)) * 2 + (place_ref[2] ^ (1 - phase))
    return quarter * 2 + step % 2


def wide_back_step(
    phase, step, place_ref, rounded_ref, second_ref, slope_ref, ups, downs, held_up, held_down,
    up_sems, down_sems, turned, shift_ref, store, total_ref, slopes, slope_sems
):
    y_at, c_at = place_ref[1], place_ref[2]

    @pl.when(step == 0)
    def _():
        for at in range(4):
            tile = wide_back_tile(phase, at, place_ref)
            for number, buffer in enumerate(downs):
                pltpu.make_async_copy(
                    buffer.at[tile], held_down.at[at, c_at ^ number], down_sems.at[at, number]
                ).start()
            for dy in range(2):
                pltpu.make_async_copy(
                    ups[(1 - at // 2) * 2 + at % 2].at[dy],
                    held_up.at[at, :, y_at ^ dy],
                    up_sems.at[at, dy],
                ).start()
            pltpu.make_async_copy(slope_ref.at[tile], slopes.at[at], slope_sems.at[at]).start()
        turned[...] = second_ref[...].T

    for number in range(2):
        pltpu.make_async_copy(
            downs[0].at[0], held_down.at[step, number], down_sems.at[step, number]
        ).wait()
    for dy in range(2):
        pltpu.make_async_copy(
            ups[0].at[dy], held_up.at[step, :, dy], up_sems.at[step, dy]
        ).wait()
    grad_active = mul_nt(rounded_ref[...], square(held_down[step]))
    pltpu.make_async_copy(slope_ref.at[0], slopes.at[step], slope_sems.at[step]).wait()
    grad_hidden = (grad_active * slopes[step].astype(F32)).astype(BF)
    shift_ref[pl.ds(step, 1), :] = col_sum(grad_hidden.astype(F32))
    total_ref[...] += mul_nt(grad_hidden, square(held_up[step]))
    store(mul_nn(turned[...], grad_hidden).reshape(4, 2, D // 8, TILE))


def wide_back_first_kernel(
    place_ref,
    rounded_ref,
    second_ref,
    slope_ref,
    u0_ref,
    u1_ref,
    u2_ref,
    u3_ref,
    d0_ref,
    d1_ref,
    pass_ref,
    stay_ref,
    shift_ref,
    total_ref,
    held_up,
    held_down,
    turned,
    up_sems,
    down_sems,
    slopes,
    slope_sems,
):
    step = pl.program_id(0)

    @pl.when(step == 0)
    def _():
        total_ref[...] = jnp.zeros_like(total_ref)

    def store(up_grad):
        def into(out_ref):
            for side in range(2):
                out_ref[side ^ place_ref[1], :, 0] = up_grad[:, side].astype(BF)

        @pl.when(step < 2)
        def _():
            into(pass_ref)

        @pl.when(step >= 2)
        def _():
            into(stay_ref)

    wide_back_step(
        0, step, place_ref, rounded_ref, second_ref, slope_ref,
        (u0_ref, u1_ref, u2_ref, u3_ref), (d0_ref, d1_ref),
        held_up, held_down, up_sems, down_sems, turned, shift_ref, store, total_ref, slopes, slope_sems
    )


def wide_back_last_kernel(
    place_ref,
    rounded_ref,
    second_ref,
    slope_ref,
    u0_ref,
    u1_ref,
    u2_ref,
    u3_ref,
    d0_ref,
    d1_ref,
    before_ref,
    grad_ref,
    middle_ref,
    gains_ref,
    got_pass_ref,
    got_keep_ref,
    pass_ref,
    keep_ref,
    shift_ref,
    middle_grad_ref,
    middle_rounded_ref,
    small_ref,
    held_up,
    held_down,
    turned,
    up_sems,
    down_sems,
    slopes,
    slope_sems,
    total,
):
    step = pl.program_id(0)

    @pl.when(step == 0)
    def _():
        total[...] = before_ref[...]

    def store(up_grad):
        def into(out_ref, got_ref):
            for side in range(2):
                at = side ^ place_ref[1]
                out_ref[at, :, 0] = (up_grad[:, side] + got_ref[at, :, 0].astype(F32)).astype(BF)

        @pl.when(step < 2)
        def _():
            into(pass_ref, got_pass_ref)

        @pl.when(step >= 2)
        def _():
            into(keep_ref, got_keep_ref)

    wide_back_step(
        1, step, place_ref, rounded_ref, second_ref, slope_ref,
        (u0_ref, u1_ref, u2_ref, u3_ref), (d0_ref, d1_ref),
        held_up, held_down, up_sems, down_sems, turned, shift_ref, store, total, slopes, slope_sems
    )

    @pl.when(step == 3)
    def _():
        def body(rows, carry):
            gain_sum, move_sum, out_sum, down_sum = carry
            normed, inverse = normalize(middle_ref[rows, :])
            grad_second = total[rows, :]
            grad = grad_ref[rows, :] + norm_back(grad_second * gains_ref[1:2, :], normed, inverse)
            rounded = grad.astype(BF)
            middle_grad_ref[rows, :] = grad
            middle_rounded_ref[rows, :] = rounded
            return (
                gain_sum + col_sum(grad_second * normed),
                move_sum + col_sum(grad_second),
                out_sum + col_sum(rounded.astype(F32)),
                down_sum + col_sum(rounded_ref[rows, :].astype(F32)),
            )

        row = jnp.zeros((1, D), F32)
        sums = over_chunks(body, (row, row, row, row))
        small_ref[...] = jnp.zeros_like(small_ref)
        for number in range(4):
            small_ref[number : number + 1, :] = sums[number]


def wide_back_call(kernel, in_specs, out_specs, out_shape, scratch, arrays):
    full = whole_block((ROWS, D))
    return pl.pallas_call(
        kernel,
        grid_spec=pltpu.PrefetchScalarGridSpec(
            num_scalar_prefetch=1,
            grid=(4,),
            in_specs=[full] * 2 + [ANY_SPEC] * 7 + in_specs,
            out_specs=out_specs,
            scratch_shapes=[
                pltpu.VMEM((4, 4, 2, D // 8, TILE), BF),
                pltpu.VMEM((4, 2, TILE // 2, D), BF),
                pltpu.VMEM((D, ROWS), BF),
                pltpu.SemaphoreType.DMA((4, 2)),
                pltpu.SemaphoreType.DMA((4, 2)),
                pltpu.VMEM((4, ROWS, TILE), BF),
                pltpu.SemaphoreType.DMA((4,)),
            ]
            + scratch,
        ),
        out_shape=out_shape,
        compiler_params=pltpu.CompilerParams(vmem_limit_bytes=60 * MIB),
        cost_estimate=pl.CostEstimate(flops=int((2 * ROWS * D * FF * 2) * 0.1), bytes_accessed=int((18 * MIB) * 0.1), transcendentals=0),
    )(*arrays)


def wide_back_blocks():
    block = (2, 4, 1, D // 8, TILE)
    return (
        pl.BlockSpec(block, lambda step, place_ref: (0, 0, jnp.minimum(step, 1), 0, 0)),
        pl.BlockSpec(block, lambda step, place_ref: (0, 0, jnp.maximum(step - 2, 0), 0, 0)),
    )


def wide_back_first(place, rounded, second, slope, up_parts, down_parts):
    out = sds((2, 4, 2, D // 8, TILE), BF)
    return wide_back_call(
        wide_back_first_kernel,
        [],
        (*wide_back_blocks(), whole_block((4, TILE)), whole_block((ROWS, D))),
        (out, out, sds((4, TILE), F32), sds((ROWS, D), F32)),
        [],
        (place, rounded, second, slope, *up_parts[2:4], *up_parts[6:8], *down_parts),
    )


def wide_back_last(
    place, rounded, second, slope, up_parts, down_parts, before, grad, middle, gains, *got
):
    full = whole_block((ROWS, D))
    out = sds((2, 4, 2, D // 8, TILE), BF)
    return wide_back_call(
        wide_back_last_kernel,
        [full] * 3 + [whole_block((2, D)), *wide_back_blocks()],
        (*wide_back_blocks(), whole_block((4, TILE)), full, full, whole_block((8, D))),
        (out, out, sds((4, TILE), F32), sds((ROWS, D), F32), sds((ROWS, D), BF), sds((8, D), F32)),
        [pltpu.VMEM((ROWS, D), F32)],
        (
            place, rounded, second, slope, *up_parts[0:2], *up_parts[4:6], *down_parts,
            before, grad, middle, gains, *got
        ),
    )


def mix_back_kernel(
    place_ref,
    lengths_ref,
    rounded_ref,
    middle_grad_ref,
    residual_ref,
    w0_ref,
    w1_ref,
    w2_ref,
    w3_ref,
    packed_ref,
    log_ref,
    mixed_ref,
    gains_ref,
    biases_ref,
    s00_ref,
    s01_ref,
    s10_ref,
    s11_ref,
    lefts_ref,
    rights_ref,
    grad_ref,
    grad_rounded_ref,
    small_ref,
    held,
    grad_mixed,
    total,
    sems,
):
    x_at, y_at, c_at = place_ref[0], place_ref[1], place_ref[2]
    copies = quarter_copies(place_ref, (w0_ref, w1_ref, w2_ref, w3_ref), held, sems)
    for copy in copies:
        copy.start()

    def send_grad(part):
        @pl.when(c_at ^ (part & 1) == 1)
        def _():
            left = lefts_ref[1 if part == 3 else 0]
            value = mul_nn(left, rights_ref[part]).astype(BF).reshape(4, 2, D // 8, D)
            for dx, out_refs in enumerate(((s00_ref, s01_ref), (s10_ref, s11_ref))):

                @pl.when(x_at ^ (part >> 1) == dx)
                def _():
                    for dy, out_ref in enumerate(out_refs):
                        out_ref[...] = jnp.where(y_at == dy, value[:, 0], value[:, 1])

    lefts_ref[1] = mixed_ref[...].T
    rights_ref[3] = rounded_ref[...]
    send_grad(3)

    def first(rows, carry):
        normed, inverse = normalize(residual_ref[rows, :].astype(F32))
        total[rows, :] = normed * gains_ref[0:1, :] + biases_ref[0:1, :]
        return carry

    over_chunks(first, 0)
    lefts_ref[0] = total[...].astype(BF).T
    for copy in copies:
        copy.wait()
    grad_mixed[...] = mul_nt(rounded_ref[...], square(held[3])).astype(BF)
    masks = head_masks()
    row_ids = lax.broadcasted_iota(jnp.int32, (LEN, 1), 0)
    scale = 1.0 / math.sqrt(HEAD_DIM)

    def one_sequence(seq, carry):
        rows = pl.ds(pl.multiple_of(seq * LEN, LEN), LEN)
        valid = row_ids < lengths_ref[seq]
        for group in range(GROUPS):
            at_query = slice(group * 128, (group + 1) * 128)
            at_key = slice(D + group * 128, D + (group + 1) * 128)
            at_value = slice(2 * D + group * 128, 2 * D + (group + 1) * 128)
            queries = stack_heads(packed_ref[rows, at_query], masks)
            key_rows = packed_ref[rows, at_key]
            value_rows = packed_ref[rows, at_value]
            grads = stack_heads(grad_mixed[rows, at_query], masks)
            scores = scores_of(key_rows, queries, valid)
            probs = jnp.exp(scores - log_ref[seq * GROUPS + group])
            grad_probs = mul_nt(value_rows, grads)
            inner = jnp.sum(grad_probs * probs, 0, keepdims=True)
            grad_scores = (probs * (grad_probs - inner)).astype(BF)
            rights_ref[2, rows, at_query] = mul_nn(probs.astype(BF), grads).astype(BF)
            rights_ref[1, rows, at_query] = (mul_nn(grad_scores, queries) * scale).astype(BF)
            grad_queries = unstack_heads(mul_tn(key_rows, grad_scores))
            rights_ref[0, rows, at_query] = (grad_queries * scale).astype(BF)
        return carry

    lax.fori_loop(0, SEQ_DEV, one_sequence, 0)
    for part in range(3):
        send_grad(part)
        result = mul_nt(rights_ref[part], square(held[part]))
        if part == 0:
            total[...] = result
        else:
            total[...] += result

    def body(rows, carry):
        gain_sum, move_sum, query_sum, value_sum = carry
        normed, inverse = normalize(residual_ref[rows, :].astype(F32))
        grad_pre = total[rows, :]
        grad = middle_grad_ref[rows, :] + norm_back(grad_pre * gains_ref[0:1, :], normed, inverse)
        grad_ref[rows, :] = grad
        grad_rounded_ref[rows, :] = grad.astype(BF)
        return (
            gain_sum + col_sum(grad_pre * normed),
            move_sum + col_sum(grad_pre),
            query_sum + col_sum(rights_ref[0, rows, :].astype(F32)),
            value_sum + col_sum(rights_ref[2, rows, :].astype(F32)),
        )

    row = jnp.zeros((1, D), F32)
    sums = over_chunks(body, (row, row, row, row))
    small_ref[...] = jnp.zeros_like(small_ref)
    for number in range(4):
        small_ref[number : number + 1, :] = sums[number]


def mix_back(
    place, lengths, rounded, middle_grad, residual, quarters, packed, logs, mixed, gains, biases
):
    out = sds((4, D // 8, D), BF)
    return pl.pallas_call(
        mix_back_kernel,
        out_shape=(
            *(out,) * 4,
            sds((2, D, ROWS), BF),
            sds((4, ROWS, D), BF),
            sds((ROWS, D), F32),
            sds((ROWS, D), BF),
            sds((8, D), F32),
        ),
        grid=(1,),
        in_specs=[SMEM_SPEC, SMEM_SPEC]
        + [whole_block((ROWS, D))] * 3
        + [ANY_SPEC] * 4
        + [
            whole_block((ROWS, 3 * D)),
            whole_block((SEQ_DEV * GROUPS, 1, PER_GROUP * LEN)),
            whole_block((ROWS, D)),
            whole_block((2, D)),
            whole_block((6, D)),
        ],
        out_specs=(
            *(whole_block((4, D // 8, D)),) * 4,
            whole_block((2, D, ROWS)),
            whole_block((4, ROWS, D)),
            whole_block((ROWS, D)),
            whole_block((ROWS, D)),
            whole_block((8, D)),
        ),
        scratch_shapes=[
            pltpu.VMEM((4, 4, 2, D // 8, D), BF),
            pltpu.VMEM((ROWS, D), BF),
            pltpu.VMEM((ROWS, D), F32),
            pltpu.SemaphoreType.DMA((8,)),
        ],
        compiler_params=pltpu.CompilerParams(vmem_limit_bytes=60 * MIB),
        cost_estimate=pl.CostEstimate(flops=int((2 * ROWS * D * 4 * D * 8) * 0.1), bytes_accessed=int((18 * MIB) * 0.1), transcendentals=0),
    )(
        place, lengths, rounded, middle_grad, residual, *quarters, packed, logs, mixed, gains, biases
    )


def mix_back_last_kernel(
    place_ref, left_ref, right_ref, g00_ref, g01_ref, g10_ref, g11_ref, pass_ref, keep_ref
):
    step = pl.program_id(0)
    y_at = place_ref[1]
    value = mul_nn(left_ref[0], right_ref[0]).reshape(4, 2, D // 8, D)

    def into(out_ref, *got_refs):
        for dy, got_ref in enumerate(got_refs):
            mine = jnp.where(y_at == dy, value[:, 0], value[:, 1])
            out_ref[dy] = (mine + got_ref[...].astype(F32)).astype(BF)

    @pl.when(step == 0)
    def _():
        into(pass_ref, g10_ref, g11_ref)

    @pl.when(step == 1)
    def _():
        into(keep_ref, g00_ref, g01_ref)


def mix_back_last(place, lefts, rights, *got):
    def part(step, place_ref):
        return (place_ref[0] ^ (1 - step)) * 2 + place_ref[2]

    out = sds((2, 4, D // 8, D), BF)
    return pl.pallas_call(
        mix_back_last_kernel,
        grid_spec=pltpu.PrefetchScalarGridSpec(
            num_scalar_prefetch=1,
            grid=(2,),
            in_specs=[
                pl.BlockSpec(
                    (1, D, ROWS), lambda step, place_ref: (part(step, place_ref) // 3, 0, 0)
                ),
                pl.BlockSpec((1, ROWS, D), lambda step, place_ref: (part(step, place_ref), 0, 0)),
                *(whole_block((4, D // 8, D)),) * 4,
            ],
            out_specs=(whole_block((2, 4, D // 8, D)),) * 2,
        ),
        out_shape=(out, out),
        compiler_params=pltpu.CompilerParams(vmem_limit_bytes=60 * MIB),
        cost_estimate=pl.CostEstimate(flops=int((2 * ROWS * D * 2 * D) * 0.1), bytes_accessed=int((6 * MIB) * 0.1), transcendentals=0),
    )(place, lefts, rights, *got)


def swap(value, axis, name="swap"):
    with jax.named_scope(name):
        return lax.ppermute(value, axis, [(0, 1), (1, 0)])


def after(value, *others):
    return lax.optimization_barrier((value, others))[0]


class Order:
    def __init__(self):
        self.last = None

    def hold(self, *arrays):
        if self.last is not None:
            arrays = lax.optimization_barrier((arrays, self.last))[0]
        return arrays

    def __call__(self, function, *arrays):
        results = function(*self.hold(*arrays))
        self.last = jax.tree.leaves(results)[0]
        return results


def wide_sum(*values):
    total = values[0].astype(F32)
    for value in values[1:]:
        total = total + value.astype(F32)
    return total


def rounded_sum(*values):
    return wide_sum(*values).astype(BF)


class Moves:
    def __init__(self, fsdp):
        self.z_size = fsdp // 2
        self.staged = fsdp == 8
        self.x_at = lax.axis_index("x")
        self.y_at = lax.axis_index("y")
        self.z_at = lax.axis_index("z")
        self.c_at = lax.axis_index("c")
        self.place = jnp.stack([self.x_at, self.y_at, self.c_at]).astype(jnp.int32)

    def hop(self, value, reach, name="hop"):
        with jax.named_scope(name):
            return lax.ppermute(value, "z", [(at, at ^ reach) for at in range(self.z_size)])

    def ordered(self, bit, own, other):
        return jnp.where(bit == 0, jnp.stack([own, other]), jnp.stack([other, own]))

    def by_side(self, value):
        value = value.reshape(4, 2, *value.shape[1:]).swapaxes(0, 1)
        return jnp.where(self.y_at == 0, value, value[::-1])

    def by_shard(self, value):
        value = jnp.where(self.y_at == 0, value, value[::-1]).swapaxes(0, 1)
        return value.reshape(8, *value.shape[2:])

    def own_quarter(self, flat):
        shard = flat.reshape(D // 8, -1, 128)
        step = shard.shape[1] // 4
        own = lax.dynamic_slice_in_dim(shard, (self.x_at * 2 + self.c_at) * step, step, 1)
        return own.reshape(D // 8, step // 5, 5, 128).swapaxes(0, 1).reshape(-1, D // 8, D)

    def gather_quarters(self, flat):
        whole = lax.all_gather(flat, ("z", "y"), axis=0, tiled=True)
        whole = whole.reshape(8, D // 8, 4, -1, D).transpose(2, 0, 3, 1, 4)
        parts = []
        for number in range(4):
            quarter = (self.x_at ^ (number >> 1)) * 2 + (self.c_at ^ (number & 1))
            parts.append(self.by_side(lax.dynamic_index_in_dim(whole, quarter, 0, False)))
        return tuple(parts)

    def high(self, own, other):
        return self.ordered(self.z_at // 2, own, other)

    def low(self, pair, other):
        return self.in_order(self.z_at % 2, pair, other)

    def both(self, line, other):
        return self.in_order(self.y_at, line, other)

    def in_order(self, bit, own, other):
        value = jnp.where(bit == 0, jnp.stack([own, other], 1), jnp.stack([other, own], 1))
        return value.reshape(-1, *own.shape[1:])

    def low_tiles(self, pair, other):
        line = self.low(pair, other)
        return tuple(line[:, tile] for tile in range(line.shape[1]))

    def part_near(self, *parts):
        total = wide_sum(*parts)
        total = total.reshape(2, 2, *total.shape[1:])
        near = self.z_at % 2
        return tuple(
            lax.dynamic_index_in_dim(total, at, 1, False).astype(BF) for at in (1 - near, near)
        )

    def part_far(self, *parts):
        total = wide_sum(*parts)
        far = self.z_at // 2
        return tuple(
            lax.dynamic_index_in_dim(total, at, 0, False).astype(BF) for at in (1 - far, far)
        )

    def gather_halves(self, flat):
        if not self.staged:
            whole = lax.all_gather(flat, ("z", "y"), axis=0, tiled=True).reshape(8, 2, TILE // 2, D)
            return tuple(
                lax.dynamic_index_in_dim(whole, self.c_at ^ number, 1, False) for number in range(2)
            )
        plane = lax.all_gather(self.own_half(flat), ("z", "y"), axis=0, tiled=False)
        return (plane, swap(plane, "c"))

    def own_half(self, flat):
        own = lax.dynamic_slice_in_dim(flat, self.c_at * (TILE // 2) * 5, (TILE // 2) * 5, 0)
        return own.reshape(TILE // 2, D)

    def sum_all(self, value):
        value = value + swap(value, "c")
        value = value + swap(value, "x")
        value = value + swap(value, "y")
        reach = 1
        while reach < self.z_size:
            value = value + self.hop(value, reach)
            reach *= 2
        return value

    def along_z(self, part):
        return lax.psum_scatter(part, "z", scatter_dimension=0, tiled=False)

    def quarters_flat(self, own, other):
        four = jnp.stack([own, other], 1)
        four = jnp.where(self.c_at == 0, four, four[:, ::-1])
        four = jnp.where(self.x_at == 0, four, four[::-1])
        return four.transpose(3, 0, 1, 2, 4).astype(F32).reshape(-1, 128)

    def halves_flat(self, own, other):
        both = self.ordered(self.c_at, own, other)
        return both.reshape(D, TILE).T.astype(F32).reshape(-1, 128)

    def plain_quarters(self, passed, keep):
        part = self.by_shard(rounded_sum(keep, swap(passed, "x")))
        part = part.transpose(0, 2, 1, 3).reshape(D, -1)
        part = lax.psum_scatter(part, ("z", "y"), scatter_dimension=0, tiled=True)
        parts = lax.all_gather(part, ("x", "c"), axis=0, tiled=False)
        return parts.swapaxes(0, 1).astype(F32).reshape(-1, 128)

    def plain_halves(self, part):
        part = self.by_shard(part).transpose(0, 2, 1)
        part = part.reshape(FF, D // 2)
        part = lax.psum_scatter(part, ("z", "y"), scatter_dimension=0, tiled=True).T
        part = rounded_sum(part, swap(part, "x"))
        return lax.all_gather(part, "c", axis=0, tiled=True).T.astype(F32).reshape(-1, 128)


def local(
    fsdp,
    inputs,
    targets,
    masked,
    lengths,
    attn_weight,
    up_weight,
    down_weight,
    norm_gains,
    layer_biases,
    up_bias,
    head_weight,
    final_gain,
    final_shift,
    head_bias,
):
    moves = Moves(fsdp)
    place = moves.place
    shifts = up_bias.reshape(LAYERS, TILES, TILE)
    saved = []

    def mix_on(layer, residual, quarters):
        return mix(place, lengths, residual, quarters, norm_gains[layer], layer_biases[layer])

    def prepared(targets, masked, head_weight, head_bias):
        wide_bias = head_bias.reshape(1, VOCAB)
        return (
            targets.reshape(ROWS, 1),
            masked.reshape(ROWS, 1),
            jnp.pad(head_weight, ((0, 0), (0, 128 - VOCAB))),
            jnp.pad(wide_bias, ((0, 0), (0, 128 - VOCAB)), constant_values=-1e30),
        )

    def up_on(layer, second, parts):
        return up(place, second, parts, shifts[layer])

    def down_on(layer, middle, active, parts):
        return down(place, middle, active, parts, layer_biases[layer])

    def two(own, other):
        return jnp.stack([own, other])

    run = Order()
    if moves.staged:
        a0 = run(moves.own_quarter, attn_weight[0])
        a0_far = moves.hop(a0, 2, "a0_far")
        u0 = run(moves.own_quarter, up_weight[0])
        u0_far = moves.hop(u0, 2, "u0_far")
        d0 = run(moves.own_half, down_weight[0])
        a0 = run(moves.high, a0, a0_far)
        a0_near = moves.hop(a0, 1, "a0_near")
        (d0,) = run.hold(d0)
        d0_far = moves.hop(d0, 2, "d0_far")
        u0 = run(moves.high, u0, u0_far)
        u0_near = moves.hop(u0, 1, "u0_near")
        (a0,) = run(moves.low_tiles, a0, a0_near)
        a0_y = swap(a0, "y", "a0_y")
        a1 = run(moves.own_quarter, attn_weight[1])
        a1_far = moves.hop(a1, 2, "a1_far")
        u1 = run(moves.own_quarter, up_weight[1])
        d1 = run(moves.own_half, down_weight[1])
        a0 = run(two, a0, a0_y)
        a0_x = swap(a0, "x", "a0_x")
        a0_c = swap(a0, "c", "a0_c")
        u00, u01 = run(moves.low_tiles, u0, u0_near)
        u00_y, u01_y = swap(u00, "y", "u00_y"), swap(u01, "y", "u01_y")
        d0 = run(moves.high, d0, d0_far)
        d0_near = moves.hop(d0, 1, "d0_near")
        a1 = run(moves.high, a1, a1_far)
        a1_near = moves.hop(a1, 1, "a1_near")
        ready = run(prepared, targets, masked, head_weight, head_bias)
        u00 = run(two, u00, u00_y)
        u00_x = swap(u00, "x", "u00_x")
        u00_c = swap(u00, "c", "u00_c")
        u01 = run(two, u01, u01_y)
        u01_x = swap(u01, "x", "u01_x")
        u01_c = swap(u01, "c", "u01_c")
        (a1,) = run(moves.low_tiles, a1, a1_near)
        a1_y = swap(a1, "y", "a1_y")
        (a0_x,) = run.hold(a0_x)
        a0_xc = swap(a0_x, "c", "a0_xc")
        quarters0 = (a0, a0_c, a0_x, a0_xc)
        mixed0 = run(lambda r, *q: mix_on(0, r, q), inputs, *quarters0)
        d0 = run(moves.low, d0, d0_near)
        d0_y = swap(d0, "y", "d0_y")
        (u1,) = run.hold(u1)
        u1_far = moves.hop(u1, 2, "u1_far")
        a1 = run(two, a1, a1_y)
        a1_x = swap(a1, "x", "a1_x")
        a1_c = swap(a1, "c", "a1_c")
        (u00_x,) = run.hold(u00_x)
        u00_xc = swap(u00_x, "c", "u00_xc")
        u1 = run(moves.high, u1, u1_far)
        u1_near = moves.hop(u1, 1, "u1_near")
        (d1,) = run.hold(d1)
        d1_far = moves.hop(d1, 2, "d1_far")
        (u01_x,) = run.hold(u01_x)
        u01_xc = swap(u01_x, "c", "u01_xc")
        ups0 = (u00, u01, u00_c, u01_c, u00_x, u01_x, u00_xc, u01_xc)
        wide0 = run(lambda m, *p: up_on(0, m, p), mixed0[4], *ups0)
        u10, u11 = run(moves.low_tiles, u1, u1_near)
        u10_y, u11_y = swap(u10, "y", "u10_y"), swap(u11, "y", "u11_y")
        d0 = run(moves.both, d0, d0_y)
        d0_c = swap(d0, "c", "d0_c")
        d1 = run(moves.high, d1, d1_far)
        d1_near = moves.hop(d1, 1, "d1_near")
        residual1 = run(lambda m, a, *p: down_on(0, m, a, p), mixed0[3], wide0[0], d0, d0_c)
        u10 = run(two, u10, u10_y)
        u10_x = swap(u10, "x", "u10_x")
        u10_c = swap(u10, "c", "u10_c")
        u11 = run(two, u11, u11_y)
        u11_x = swap(u11, "x", "u11_x")
        u11_c = swap(u11, "c", "u11_c")
        d1 = run(moves.low, d1, d1_near)
        d1_y = swap(d1, "y", "d1_y")
        (a1_x,) = run.hold(a1_x)
        a1_xc = swap(a1_x, "c", "a1_xc")
        quarters1 = (a1, a1_c, a1_x, a1_xc)
        mixed1 = run(lambda r, *q: mix_on(1, r, q), residual1, *quarters1)
        (u10_x,) = run.hold(u10_x)
        u10_xc = swap(u10_x, "c", "u10_xc")
        (u11_x,) = run.hold(u11_x)
        u11_xc = swap(u11_x, "c", "u11_xc")
        ups1 = (u10, u11, u10_c, u11_c, u10_x, u11_x, u10_xc, u11_xc)
        wide1 = run(lambda m, *p: up_on(1, m, p), mixed1[4], *ups1)
        d1 = run(moves.both, d1, d1_y)
        d1_c = swap(d1, "c", "d1_c")
        residual = run(lambda m, a, *p: down_on(1, m, a, p), mixed1[3], wide1[0], d1, d1_c)
        weights = [(quarters0, ups0, (d0, d0_c)), (quarters1, ups1, (d1, d1_c))]
        saved = [(inputs, *mixed0, *wide0), (residual1, *mixed1, *wide1)]
    else:
        weights = []
        for layer in range(LAYERS):
            attn_parts = moves.gather_quarters(attn_weight[layer])
            up_parts = moves.gather_quarters(up_weight[layer])
            weights.append(
                (
                    [part[:, :, 0] for part in attn_parts],
                    [up_parts[number][:, :, tile] for number in range(4) for tile in range(2)],
                    moves.gather_halves(down_weight[layer]),
                )
            )
        residual = inputs
        for layer in range(LAYERS):
            quarters, up_parts, down_parts = weights[layer]
            mixed = mix_on(layer, residual, quarters)
            wide = up_on(layer, mixed[4], up_parts)
            saved.append((residual, *mixed, *wide))
            residual = down_on(layer, mixed[3], wide[0], down_parts)
        ready = prepared(targets, masked, head_weight, head_bias)
    activations, grad, rounded, head_small = run(
        head, residual, *ready, final_gain.reshape(1, D), final_shift.reshape(1, D)
    )

    def down_at(layer, rounded):
        return down_back(place, rounded, saved[layer][6])

    def wide_first(layer, rounded):
        _, up_parts, down_parts = weights[layer]
        return wide_back_first(
            place, rounded, saved[layer][5], saved[layer][7], up_parts, down_parts
        )

    def wide_last(layer, rounded, before, grad, *got):
        _, up_parts, down_parts = weights[layer]
        _, _, _, _, middle, second, _, slope = saved[layer]
        return wide_back_last(
            place, rounded, second, slope, up_parts, down_parts, before, grad, middle, norm_gains[layer], *got
        )

    def mix_first(layer, rounded, middle_grad):
        residual, packed, logs, mixed, _, _, _, _ = saved[layer]
        return mix_back(
            place,
            lengths,
            rounded,
            middle_grad,
            residual,
            weights[layer][0],
            packed,
            logs,
            mixed,
            norm_gains[layer],
            layer_biases[layer],
        )

    def mix_last(lefts, rights, *got):
        return mix_back_last(place, lefts, rights, *got)

    def shift_rows(shift_send, shift_keep):
        send, keep = (part.reshape(2, 2, TILE)[::-1] for part in (shift_send, shift_keep))
        parts = moves.ordered(moves.c_at, keep, send).swapaxes(0, 1)
        return jnp.where(moves.x_at == 0, parts, parts[::-1]).reshape(TILES, TILE)

    def packed_small(head_small, *rest):
        small = [head_small]
        for layer in range(LAYERS):
            shift_send, shift_keep, wide_small, mix_small = rest[4 * layer : 4 * layer + 4]
            small += [shift_rows(shift_send, shift_keep), wide_small, mix_small]
        return jnp.concatenate(small, 0)

    def plus(own, other):
        return own + other

    def first_of(function, at):
        return lambda *a: rounded_sum(*(v[at] if n in function else v for n, v in enumerate(a)))

    if moves.staged:
        d1_pass, d1_stay, d1_keep = run(lambda g: down_at(1, g), rounded)
        d1_c1, d1_c0 = swap(d1_pass, "c", "d1_c1"), swap(d1_stay, "c", "d1_c0")
        u1_pass, u1_stay, *tail1 = run(lambda g: wide_first(1, g), rounded)
        u1_c1, u1_c0 = swap(u1_pass, "c", "u1_c1"), swap(u1_stay, "c", "u1_c0")
        d1_y = swap(run(first_of((0,), 1), d1_keep, d1_c1), "y", "d1_y")
        u1_pass, u1_keep, shift_keep1, middle_grad, middle_rounded, wide_small1 = run(
            lambda *a: wide_last(1, *a), rounded, tail1[1], grad, u1_c1, u1_c0
        )
        u1_x = swap(u1_pass, "x", "u1_x")
        *a1_send, lefts, rights, grad, rounded, mix_small1 = run(
            lambda *a: mix_first(1, *a), middle_rounded, middle_grad
        )
        a1_c = [swap(part, "c") for part in a1_send]
        d1 = moves.along_z(run(first_of((0,), 0), d1_keep, d1_c0, d1_y))
        a1_pass, a1_keep = run(mix_last, lefts, rights, *a1_c)
        a1_x = swap(a1_pass, "x", "a1_x")
        u1_y = swap(run(first_of((0, 1), 1), u1_keep, u1_x), "y", "u1_y")
        d0_pass, d0_stay, d0_keep = run(lambda g: down_at(0, g), rounded)
        d0_c1, d0_c0 = swap(d0_pass, "c", "d0_c1"), swap(d0_stay, "c", "d0_c0")
        u0_pass, u0_stay, *tail0 = run(lambda g: wide_first(0, g), rounded)
        u0_c1, u0_c0 = swap(u0_pass, "c", "u0_c1"), swap(u0_stay, "c", "u0_c0")
        a1_y = swap(run(first_of((0, 1), 1), a1_keep, a1_x), "y", "a1_y")
        d0_y = swap(run(first_of((0,), 1), d0_keep, d0_c1), "y", "d0_y")
        u1 = moves.along_z(run(first_of((0, 1), 0), u1_keep, u1_x, u1_y))
        u0_pass, u0_keep, shift_keep0, middle_grad, middle_rounded, wide_small0 = run(
            lambda *a: wide_last(0, *a), rounded, tail0[1], grad, u0_c1, u0_c0
        )
        u0_x = swap(u0_pass, "x", "u0_x")
        (d1,) = run.hold(d1)
        d1_x = swap(d1, "x", "d1_x")
        a1 = moves.along_z(run(first_of((0, 1), 0), a1_keep, a1_x, a1_y))
        *a0_send, lefts, rights, grad, rounded, mix_small0 = run(
            lambda *a: mix_first(0, *a), middle_rounded, middle_grad
        )
        a0_c = [swap(part, "c") for part in a0_send]
        small = run(
            packed_small,
            head_small,
            *(tail0[0], shift_keep0, wide_small0, mix_small0),
            *(tail1[0], shift_keep1, wide_small1, mix_small1),
        )
        small_next = swap(small, "c", "small_next")
        a0_pass, a0_keep = run(mix_last, lefts, rights, *a0_c)
        a0_x = swap(a0_pass, "x", "a0_x")
        d0 = moves.along_z(run(first_of((0,), 0), d0_keep, d0_c0, d0_y))
        small = run(plus, small, small_next)
        small_next = moves.hop(small, 2, "small_next")
        d1 = run(rounded_sum, d1, d1_x)
        d1_c = swap(d1, "c", "d1_c")
        u0_y = swap(run(first_of((0, 1), 1), u0_keep, u0_x), "y", "u0_y")
        last1 = run(lambda u, a: jnp.concatenate([u, a[None]]), u1, a1)
        last1_x = swap(last1, "x", "last1_x")
        small = run(plus, small, small_next)
        small_next = moves.hop(small, 1, "small_next")
        down_grad1 = run(moves.halves_flat, d1, d1_c)
        a0_y = swap(run(first_of((0, 1), 1), a0_keep, a0_x), "y", "a0_y")
        u0 = moves.along_z(run(first_of((0, 1), 0), u0_keep, u0_x, u0_y))
        last1 = run(two, last1, last1_x)
        last1_c = swap(last1, "c", "last1_c")
        small = run(plus, small, small_next)
        small_next = swap(small, "x", "small_next")
        a0_send, a0_stay = run(lambda k, x, y: moves.part_near(k[0], x[0], y), a0_keep, a0_x, a0_y)
        a0_near = moves.hop(a0_send, 1, "a0_near")
        up_grad1 = run(lambda *a: moves.quarters_flat(*(v[:, :2] for v in a)), last1, last1_c)
        (d0,) = run.hold(d0)
        d0_x = swap(d0, "x", "d0_x")
        a0_send, a0_stay = run(moves.part_far, a0_stay, a0_near)
        a0_far = moves.hop(a0_send, 2, "a0_far")
        small = run(plus, small, small_next)
        small_next = swap(small, "y", "small_next")
        attn_grad1 = run(lambda *a: moves.quarters_flat(*(v[:, 2:] for v in a)), last1, last1_c)
        last0 = run(lambda u, *a: jnp.concatenate([u, rounded_sum(*a)[None]]), u0, a0_stay, a0_far)
        last0_x = swap(last0, "x", "last0_x")
        d0 = run(rounded_sum, d0, d0_x)
        d0_c = swap(d0, "c", "d0_c")
        summed = run(plus, small, small_next)
        down_grad0 = run(moves.halves_flat, d0, d0_c)
        last0 = run(two, last0, last0_x)
        last0_c = swap(last0, "c", "last0_c")
        up_grad0 = run(lambda *a: moves.quarters_flat(*(v[:, :2] for v in a)), last0, last0_c)
        attn_grad0 = run(lambda *a: moves.quarters_flat(*(v[:, 2:] for v in a)), last0, last0_c)
        attn_grads = [attn_grad0, attn_grad1]
        up_grads = [up_grad0, up_grad1]
        down_grads = [down_grad0, down_grad1]
    else:
        attn_grads, up_grads, down_grads, smalls = ([None] * LAYERS for _ in range(4))
        for layer in reversed(range(LAYERS)):
            *send, keep = down_at(layer, rounded)
            got = jnp.stack([swap(part, "c") for part in send[::-1]])
            down_grads[layer] = moves.plain_halves(rounded_sum(keep, got))
            *send, shift_send, before = wide_first(layer, rounded)
            passed, keep, shift_keep, middle_grad, middle_rounded, wide_small = wide_last(
                layer, rounded, before, grad, *(swap(part, "c") for part in send)
            )
            up_grads[layer] = moves.plain_quarters(passed, keep)
            *send, lefts, rights, grad, rounded, mix_small = mix_first(
                layer, middle_rounded, middle_grad
            )
            passed, keep = mix_last(lefts, rights, *(swap(part, "c") for part in send))
            attn_grads[layer] = moves.plain_quarters(passed[:, :, None], keep[:, :, None])
            smalls[layer] = (shift_send, shift_keep, wide_small, mix_small)
        summed = moves.sum_all(packed_small(head_small, *smalls[0], *smalls[1]))

    gains_grad, biases_grad, shifts_grad = [], [], []
    for layer in range(LAYERS):
        base = 40 + 24 * layer
        shifts_grad.append(summed[base : base + 8].reshape(FF))
        wide_sums = summed[base + 8 : base + 16]
        mix_sums = summed[base + 16 : base + 24]
        gains_grad.append(jnp.stack([mix_sums[0], wide_sums[0]]))
        biases_grad.append(
            jnp.stack([mix_sums[1], wide_sums[1], mix_sums[2], mix_sums[3], wide_sums[2], wide_sums[3]])
        )
    totals = summed[35]
    return (
        activations,
        grad,
        jnp.stack(attn_grads),
        jnp.stack(up_grads),
        jnp.stack(down_grads),
        jnp.stack(gains_grad),
        jnp.stack(biases_grad),
        jnp.stack(shifts_grad),
        summed[:VOCAB].T,
        summed[32],
        summed[33],
        summed[34, :VOCAB],
        totals[0] / totals[2],
        totals[1] / totals[2],
        totals[2].astype(jnp.int32),
    )


def solution(mesh):
    fsdp, dp = mesh.shape["fsdp"], mesh.shape["dp"]
    fine = Mesh(mesh.devices.reshape(fsdp // 2, 2, dp // 2, 2), ("z", "y", "x", "c"))
    tokens = ("z", "y", "x", "c")
    flat = P(None, ("z", "y"), None)
    placed = (P(tokens, None), P(tokens), P(tokens), P(tokens), flat, flat, flat) + (P(),) * 7

    def run(*arrays):
        return local(fsdp, *arrays)

    return jax.shard_map(
        run,
        mesh=fine,
        in_specs=placed,
        out_specs=(P(tokens, None), P(tokens, None), flat, flat, flat) + (P(),) * 10,
        check_vma=False,
    )
```

```python
import math

import jax
import jax.numpy as jnp
from jax import lax
from jax.experimental import pallas as pl
from jax.experimental.pallas import tpu as pltpu
from jax.sharding import Mesh
from jax.sharding import PartitionSpec as P

D = 640
HEADS = 20
HEAD_DIM = 32
FF = 5120
VOCAB = 25
LAYERS = 2
LEN = 128
SEQ_DEV = 4
ROWS = SEQ_DEV * LEN
TILE = 640
TILES = FF // TILE
WIDE = 2 * TILE
STEPS = FF // WIDE
GROUPS = HEADS * HEAD_DIM // 128
PER_GROUP = 128 // HEAD_DIM
CHUNK = 128
CHUNKS = ROWS // CHUNK
SHARD = D // 8
HALF = TILE // 2
BF = jnp.bfloat16
F32 = jnp.float32
MIB = 2**20

SMEM_SPEC = pl.BlockSpec(memory_space=pltpu.SMEM)
ANY_SPEC = pl.BlockSpec(memory_space=pl.ANY)
KERNEL = dict(
    compiler_params=pltpu.CompilerParams(vmem_limit_bytes=60 * MIB),
    cost_estimate=pl.CostEstimate(flops=4 * 10**8, bytes_accessed=2 * MIB, transcendentals=0),
)


def dot(left, right, dims):
    return lax.dot_general(left, right, (dims, ((), ())), preferred_element_type=F32)


def mul_nn(left, right):
    return dot(left, right, ((1,), (0,)))


def mul_nt(left, right):
    return dot(left, right, ((1,), (1,)))


def mul_tn(left, right):
    return dot(left, right, ((0,), (0,)))


def normalize(values):
    centered = values - jnp.mean(values, -1, keepdims=True)
    inverse = lax.rsqrt(jnp.mean(centered * centered, -1, keepdims=True) + 1e-05)
    return (centered * inverse, inverse)


def norm_back(grad_normed, normed, inverse):
    return inverse * (
        grad_normed
        - jnp.mean(grad_normed, -1, keepdims=True)
        - normed * jnp.mean(grad_normed * normed, -1, keepdims=True)
    )


def col_sum(values):
    return jnp.sum(values, 0, keepdims=True)


def sds(shape, dtype):
    return jax.ShapeDtypeStruct(shape, dtype)


def whole_block(shape):
    zeros = (0,) * len(shape)
    return pl.BlockSpec(shape, lambda *_: zeros)


def semaphores(*shape):
    return pltpu.SemaphoreType.DMA(shape)


def copy(source, target, semaphore):
    return pltpu.make_async_copy(source, target, semaphore)


def chunk_rows(index):
    return slice(index * CHUNK, (index + 1) * CHUNK)


def over_chunks(body, start):
    def step(index, carry):
        return body(pl.ds(pl.multiple_of(index * CHUNK, CHUNK), CHUNK), carry)

    return lax.fori_loop(0, CHUNKS, step, start)


def quarter_copies(place_ref, buffers, held, sems):
    x_at, y_at, c_at = place_ref[0], place_ref[1], place_ref[2]
    copies = []
    for number, buffer in enumerate(buffers):
        dx, dc, dy = number // 4, number // 2 % 2, number % 2
        quarter = (x_at ^ dx) * 2 + (c_at ^ dc)
        lanes = pl.ds(pl.multiple_of(quarter * D, 128), D)
        copies.append(copy(buffer.at[:, 0], held.at[:, y_at ^ dy, :, lanes], sems.at[number]))
    return copies


def square(values):
    return values.reshape(D, values.shape[-1])


def head_masks():
    lanes = lax.broadcasted_iota(jnp.int32, (LEN, 128), 1) // HEAD_DIM
    return [(lanes == member) for member in range(PER_GROUP)]


def stack_heads(values, masks):
    zero = jnp.zeros_like(values)
    return jnp.concatenate([jnp.where(mask, values, zero) for mask in masks], 0)


def unstack_heads(values):
    parts = [
        values[HEAD_DIM * member : HEAD_DIM * (member + 1), LEN * member : LEN * (member + 1)]
        for member in range(PER_GROUP)
    ]
    return jnp.concatenate(parts, 0).T


def scores_of(keys, queries, valid):
    scores = mul_nt(keys, queries) * (1.0 / math.sqrt(HEAD_DIM))
    return jnp.where(valid, scores, -1e30)


def mix_kernel(place_ref, lengths_ref, residual_ref, *refs):
    buffers, refs = refs[:8], refs[8:]
    gains_ref, biases_ref, packed_out, log_ref, mixed_out, middle_out, second_out, *refs = refs
    held, pre, packed, mixed, middles, seconds, sems, out_sems, row_sems = refs
    copies = quarter_copies(place_ref, buffers, held, sems)
    for one in copies:
        one.start()

    def first(rows, carry):
        normed, inverse = normalize(residual_ref[rows, :].astype(F32))
        pre[rows, :] = (normed * gains_ref[0:1, :] + biases_ref[0:1, :]).astype(BF)
        return carry

    over_chunks(first, 0)
    for one in copies:
        one.wait()
    shifts = (biases_ref[2:3, :], 0.0, biases_ref[3:4, :])
    sent = []
    result = mul_nn(pre[...], square(held[:, :, :, : 3 * D]))
    for part in range(3):
        lanes = slice(part * D, (part + 1) * D)
        packed[:, lanes] = (result[:, lanes] + shifts[part]).astype(BF)
        sent.append(copy(packed.at[:, lanes], packed_out.at[:, lanes], out_sems.at[part]))
        sent[-1].start()
    masks = head_masks()
    row_ids = lax.broadcasted_iota(jnp.int32, (LEN, 1), 0)

    def one_sequence(seq, carry):
        rows = pl.ds(pl.multiple_of(seq * LEN, LEN), LEN)
        valid = row_ids < lengths_ref[seq]
        for group in range(GROUPS):
            lanes = slice(group * 128, (group + 1) * 128)
            queries = stack_heads(packed[rows, lanes], masks)
            key_rows = packed[rows, D + group * 128 : D + (group + 1) * 128]
            value_rows = packed[rows, 2 * D + group * 128 : 2 * D + (group + 1) * 128]
            scores = scores_of(key_rows, queries, valid)
            top = jnp.max(scores, 0, keepdims=True)
            expos = jnp.exp(scores - top)
            total = jnp.sum(expos, 0, keepdims=True)
            probs = (expos * (1.0 / total)).astype(BF)
            log_ref[seq * GROUPS + group] = top + jnp.log(total)
            mixed[rows, lanes] = unstack_heads(mul_tn(value_rows, probs)).astype(BF)
        return carry

    lax.fori_loop(0, SEQ_DEV, one_sequence, 0)
    sent.append(copy(mixed, mixed_out, out_sems.at[3]))
    sent[-1].start()
    middles[...] = mul_nn(mixed[...], square(held[:, :, :, 3 * D :])) + biases_ref[4:5, :]
    for index in range(CHUNKS):
        rows = chunk_rows(index)
        middle = middles[rows, :] + residual_ref[rows, :].astype(F32)
        middles[rows, :] = middle
        normed, inverse = normalize(middle)
        seconds[rows, :] = (normed * gains_ref[1:2, :] + biases_ref[1:2, :]).astype(BF)
        sent.append(copy(middles.at[rows, :], middle_out.at[rows, :], row_sems.at[index, 0]))
        sent[-1].start()
        sent.append(copy(seconds.at[rows, :], second_out.at[rows, :], row_sems.at[index, 1]))
        sent[-1].start()
    for one in sent:
        one.wait()


def mix(place, lengths, residual, quarters, gains, biases):
    logs = (SEQ_DEV * GROUPS, 1, PER_GROUP * LEN)
    return pl.pallas_call(
        mix_kernel,
        grid=(1,),
        out_shape=(
            sds((ROWS, 3 * D), BF),
            sds(logs, F32),
            sds((ROWS, D), BF),
            sds((ROWS, D), F32),
            sds((ROWS, D), BF),
        ),
        in_specs=[SMEM_SPEC, SMEM_SPEC, whole_block((ROWS, D))]
        + [ANY_SPEC] * 8
        + [whole_block((2, D)), whole_block((6, D))],
        out_specs=(ANY_SPEC, whole_block(logs), ANY_SPEC, ANY_SPEC, ANY_SPEC),
        scratch_shapes=[
            pltpu.VMEM((4, 2, SHARD, 4 * D), BF),
            pltpu.VMEM((ROWS, D), BF),
            pltpu.VMEM((ROWS, 3 * D), BF),
            pltpu.VMEM((ROWS, D), BF),
            pltpu.VMEM((ROWS, D), F32),
            pltpu.VMEM((ROWS, D), BF),
            semaphores(8),
            semaphores(4),
            semaphores(CHUNKS, 2),
        ],
        **KERNEL,
    )(place, lengths, residual, *quarters, gains, biases)


def up_kernel(place_ref, second_ref, *refs):
    buffers, refs = refs[:8], refs[8:]
    shift_ref, active_out, slope_out, held, actives, slopes, sems, out_sems = refs
    step = pl.program_id(0)

    @pl.when(step == 0)
    def _():
        for number, buffer in enumerate(buffers):
            dx, dc, dy = number // 4, number // 2 % 2, number % 2
            at = (place_ref[0] ^ dx) * 2 + (place_ref[2] ^ dc)
            for half in range(2):
                target = held.at[at, :, place_ref[1] ^ dy, :, half * TILE : (half + 1) * TILE]
                copy(buffer.at[:, half], target, sems.at[at, dy, half]).start()

    for dy in range(2):
        for half in range(2):
            target = held.at[step, :, dy, :, half * TILE : (half + 1) * TILE]
            copy(buffers[0].at[:, 0], target, sems.at[step, dy, half]).wait()
    up_tile = square(held[step])
    shift = shift_ref[pl.ds(step, 1), :]
    for index in range(2):
        rows = slice(index * 2 * CHUNK, (index + 1) * 2 * CHUNK)
        hidden = mul_nn(second_ref[rows, :], up_tile) + shift
        phi = 0.5 + 0.5 * lax.erf(hidden * math.sqrt(0.5))
        density = jnp.exp(hidden * hidden * -0.5) * (1.0 / math.sqrt(2.0 * math.pi))
        actives[step, rows, :] = (hidden * phi).astype(BF)
        slopes[step, rows, :] = (phi + hidden * density).astype(BF)
    copy(actives.at[step], active_out.at[step], out_sems.at[step, 0]).start()
    copy(slopes.at[step], slope_out.at[step], out_sems.at[step, 1]).start()

    @pl.when(step == STEPS - 1)
    def _():
        for at in range(STEPS):
            copy(actives.at[at], active_out.at[at], out_sems.at[at, 0]).wait()
            copy(slopes.at[at], slope_out.at[at], out_sems.at[at, 1]).wait()


def up(place, second, parts, shift):
    out = sds((STEPS, ROWS, WIDE), BF)
    return pl.pallas_call(
        up_kernel,
        grid=(STEPS,),
        out_shape=(out, out),
        in_specs=[SMEM_SPEC, whole_block((ROWS, D))]
        + [ANY_SPEC] * 8
        + [whole_block((STEPS, WIDE))],
        out_specs=(ANY_SPEC, ANY_SPEC),
        scratch_shapes=[
            pltpu.VMEM((STEPS, 4, 2, SHARD, WIDE), BF),
            pltpu.VMEM((STEPS, ROWS, WIDE), BF),
            pltpu.VMEM((STEPS, ROWS, WIDE), BF),
            semaphores(STEPS, 2, 2),
            semaphores(STEPS, 2),
        ],
        **KERNEL,
    )(place, second, *parts, shift)


def down_kernel(place_ref, middle_ref, active_ref, *refs):
    buffers, (biases_ref, out_ref, held, rows, sems, row_sems) = refs[:8], refs[8:]
    step = pl.program_id(0)

    @pl.when(step == 0)
    def _():
        for z_at in range(4):
            for number in range(4):
                dc, dy = number // 2, number % 2
                y_at, c_at = place_ref[1] ^ dy, place_ref[2] ^ dc
                buffer = buffers[dc * 4 + dy * 2 + z_at // 2].at[z_at % 2]
                copy(buffer, held.at[z_at, y_at, c_at], sems.at[z_at, y_at, c_at]).start()
            copy(active_ref.at[z_at], rows.at[z_at], row_sems.at[z_at]).start()
        out_ref[...] = middle_ref[...] + biases_ref[5:6, :]

    for y_at in range(2):
        for c_at in range(2):
            copy(buffers[0].at[0], held.at[step, y_at, c_at], sems.at[step, y_at, c_at]).wait()
    copy(active_ref.at[0], rows.at[step], row_sems.at[step]).wait()
    out_ref[...] += mul_nn(rows[step], held[step].reshape(WIDE, D))


def down(place, middle, active, parts, biases):
    return pl.pallas_call(
        down_kernel,
        grid=(STEPS,),
        out_shape=sds((ROWS, D), F32),
        in_specs=[SMEM_SPEC, whole_block((ROWS, D))] + [ANY_SPEC] * 9 + [whole_block((6, D))],
        out_specs=whole_block((ROWS, D)),
        scratch_shapes=[
            pltpu.VMEM((4, 2, 2, HALF, D), BF),
            pltpu.VMEM((STEPS, ROWS, WIDE), BF),
            semaphores(4, 2, 2),
            semaphores(STEPS),
        ],
        **KERNEL,
    )(place, middle, active, *parts, biases)


def head_kernel(
    residual_ref,
    targets_ref,
    masked_ref,
    weight_ref,
    shift_ref,
    gain_ref,
    move_ref,
    activations_ref,
    grad_ref,
    rounded_ref,
    small_ref,
):
    small_ref[...] = jnp.zeros_like(small_ref)
    lanes = lax.broadcasted_iota(jnp.int32, (1, 128), 1)

    def body(rows, carry):
        weight_grad, gain_grad, move_grad, shift_grad, stats = carry
        residual = residual_ref[rows, :]
        activations_ref[rows, :] = residual.astype(BF)
        normed, inverse = normalize(residual)
        final = (normed * gain_ref[...] + move_ref[...]).astype(BF)
        logits = mul_nn(final, weight_ref[...]) + shift_ref[...]
        top = jnp.max(logits, -1, keepdims=True)
        log_total = top + jnp.log(jnp.sum(jnp.exp(logits - top), -1, keepdims=True))
        onehot = (targets_ref[rows, :] == lanes).astype(F32)
        picked = jnp.sum(logits * onehot, -1, keepdims=True)
        mask = masked_ref[rows, :].astype(F32)
        loss = col_sum(mask * (log_total - picked))
        hits = col_sum(mask * jnp.exp(picked - log_total))
        count = col_sum(mask)
        stats = stats + (
            jnp.where(lanes == 0, loss, 0.0)
            + jnp.where(lanes == 1, hits, 0.0)
            + jnp.where(lanes == 2, count, 0.0)
        )
        grad_logits = (mask * (jnp.exp(logits - log_total) - onehot)).astype(BF)
        weight_grad = weight_grad + mul_tn(grad_logits, final)
        shift_grad = shift_grad + col_sum(grad_logits.astype(F32))
        grad_final = mul_nt(grad_logits, weight_ref[...])
        gain_grad = gain_grad + col_sum(grad_final * normed)
        move_grad = move_grad + col_sum(grad_final)
        grad = norm_back(grad_final * gain_ref[...], normed, inverse)
        grad_ref[rows, :] = grad
        rounded_ref[rows, :] = grad.astype(BF)
        return weight_grad, gain_grad, move_grad, shift_grad, stats

    row = jnp.zeros((1, D), F32)
    narrow = jnp.zeros((1, 128), F32)
    weight_grad, gain_grad, move_grad, shift_grad, stats = over_chunks(
        body, (jnp.zeros((128, D), F32), row, row, narrow, narrow)
    )
    small_ref[0:32, :] = weight_grad[0:32, :]
    small_ref[32:33, :] = gain_grad
    small_ref[33:34, :] = move_grad
    small_ref[34:35, 0:128] = shift_grad
    small_ref[35:36, 0:128] = stats


def head(residual, targets, masked, weight, shift, gain, move):
    full = whole_block((ROWS, D))
    return pl.pallas_call(
        head_kernel,
        out_shape=(
            sds((ROWS, D), BF),
            sds((ROWS, D), F32),
            sds((ROWS, D), BF),
            sds((40, D), F32),
        ),
        grid=(1,),
        in_specs=[full, whole_block((ROWS, 1)), whole_block((ROWS, 1)), whole_block((D, 128))]
        + [whole_block((1, 128)), whole_block((1, D)), whole_block((1, D))],
        out_specs=(full, full, full, whole_block((40, D))),
        **KERNEL,
    )(residual, targets, masked, weight, shift, gain, move)


def down_back_kernel(place_ref, grad_ref, active_ref, *refs):
    sends, (keep_out, held, grads, sems, out_sems) = refs[:8], refs[8:]
    step = pl.program_id(0)
    c_at = place_ref[2]

    @pl.when(step == 0)
    def _():
        for at in range(TILES):
            z_at, y_at = at % 4, place_ref[1] ^ (1 - at // 4)
            source = active_ref.at[z_at, :, pl.ds(pl.multiple_of(y_at * TILE, 128), TILE)]
            target = held.at[at // 2, :, at % 2 * TILE : (at % 2 + 1) * TILE]
            copy(source, target, sems.at[at]).start()

    for part in range(2):
        target = held.at[step, :, part * TILE : (part + 1) * TILE]
        copy(active_ref.at[0, :, :TILE], target, sems.at[2 * step + part]).wait()
    grads[step] = mul_tn(grad_ref[...], held[step]).astype(BF).reshape(2, HALF, WIDE)
    for at in range(TILES):

        @pl.when(step == at // 2)
        def _():
            lanes = slice(at % 2 * TILE, (at % 2 + 1) * TILE)
            copy(grads.at[at // 2, 1 - c_at, :, lanes], sends[at], out_sems.at[at, 0]).start()
            kept = grads.at[at // 2, c_at, :, lanes]
            copy(kept, keep_out.at[1 - at // 4, at % 4], out_sems.at[at, 1]).start()

    @pl.when(step == STEPS - 1)
    def _():
        for at in range(TILES):
            one = grads.at[0, 0, :, :TILE]
            copy(one, sends[at], out_sems.at[at, 0]).wait()
            copy(one, keep_out.at[0, 0], out_sems.at[at, 1]).wait()


def down_back(place, grad, active):
    part = sds((HALF, TILE), BF)
    return pl.pallas_call(
        down_back_kernel,
        grid=(STEPS,),
        in_specs=[SMEM_SPEC, whole_block((ROWS, D)), ANY_SPEC],
        out_specs=(ANY_SPEC,) * 9,
        out_shape=(part,) * 8 + (sds((2, 4, HALF, TILE), BF),),
        scratch_shapes=[
            pltpu.VMEM((STEPS, ROWS, WIDE), BF),
            pltpu.VMEM((STEPS, 2, HALF, WIDE), BF),
            semaphores(TILES),
            semaphores(TILES, 2),
        ],
        **KERNEL,
    )(place, grad, active)


def down_sum_kernel(side, others, keep_ref, *refs):
    parts, refs = refs[:4], refs[4:]
    other_refs, refs = refs[:others], refs[others:]
    out_ref, kept, got, other, total, sems, other_sems, out_sems = refs
    copies = []
    for at in range(4):
        copies.append(
            [
                copy(keep_ref.at[side, at], kept.at[at], sems.at[at, 0]),
                copy(parts[at], got.at[at], sems.at[at, 1]),
            ]
            + [copy(ref.at[at], other.at[at], other_sems.at[at]) for ref in other_refs]
        )
        for one in copies[-1]:
            one.start()
    for at in range(4):
        for one in copies[at]:
            one.wait()
        value = kept[at].astype(F32) + got[at].astype(F32)
        if others:
            value = value + other[at].astype(F32)
        total[at] = value.astype(BF)
        copy(total.at[at], out_ref.at[at], out_sems.at[at]).start()
    for at in range(4):
        copy(total.at[at], out_ref.at[at], out_sems.at[at]).wait()


def down_sum(side, keep, parts, *other):
    shape = (4, HALF, TILE)

    def kernel(*refs):
        down_sum_kernel(side, len(other), *refs)

    return pl.pallas_call(
        kernel,
        grid=(1,),
        in_specs=[ANY_SPEC] * (5 + len(other)),
        out_specs=ANY_SPEC,
        out_shape=sds(shape, BF),
        scratch_shapes=[pltpu.VMEM(shape, BF)] * 4
        + [semaphores(4, 2), semaphores(4), semaphores(4)],
        **KERNEL,
    )(keep, *parts, *other)


def wide_back_start(phase, place_ref, slope_ref, ups, downs, held, sems):
    x_at, y_at, c_at = place_ref[0], place_ref[1], place_ref[2]
    held_up, held_down, slopes = held
    up_sems, down_sems, slope_sems = sems
    for step in range(2):
        dx = 1 - step
        for number, buffer in enumerate(downs):
            dc, dy, z_high = number // 4, number // 2 % 2, number % 2

            @pl.when(x_at ^ dx == z_high)
            def _():
                y_to, c_to = y_at ^ dy, c_at ^ dc
                target = held_down.at[step, y_to, c_to]
                source = buffer.at[c_at ^ (1 - phase)]
                copy(source, target, down_sems.at[step, y_to, c_to]).start()

        quarter = (x_at ^ dx) * 2 + (c_at ^ (1 - phase))
        copy(slope_ref.at[quarter], slopes.at[step], slope_sems.at[step]).start()
        for dy in range(2):
            for half in range(2):
                target = held_up.at[step, :, y_at ^ dy, :, half * TILE : (half + 1) * TILE]
                source = ups[2 * dx + dy].at[:, half]
                copy(source, target, up_sems.at[step, dy, half]).start()


def wide_back_step(step, rounded_ref, second_ref, slope_ref, ups, downs, held, sems, shift_ref, total):
    held_up, held_down, slopes = held
    up_sems, down_sems, slope_sems = sems
    for y_at in range(2):
        for c_at in range(2):
            target = held_down.at[step, y_at, c_at]
            copy(downs[0].at[0], target, down_sems.at[step, y_at, c_at]).wait()
    grad_active = mul_nt(rounded_ref[...], held_down[step].reshape(WIDE, D))
    copy(slope_ref.at[0], slopes.at[step], slope_sems.at[step]).wait()
    grad_hidden = (grad_active * slopes[step].astype(F32)).astype(BF)
    shift_ref[pl.ds(step, 1), :] = col_sum(grad_hidden.astype(F32))
    for dy in range(2):
        for half in range(2):
            target = held_up.at[step, :, dy, :, half * TILE : (half + 1) * TILE]
            copy(ups[0].at[:, 0], target, up_sems.at[step, dy, half]).wait()
    total[...] += mul_nt(grad_hidden, square(held_up[step]))
    return mul_tn(second_ref[...], grad_hidden).reshape(4, 2, SHARD, WIDE)


def wide_back_scratch():
    return [
        pltpu.VMEM((2, 4, 2, SHARD, WIDE), BF),
        pltpu.VMEM((2, 2, 2, HALF, D), BF),
        pltpu.VMEM((2, ROWS, WIDE), BF),
        semaphores(2, 2, 2),
        semaphores(2, 2, 2),
        semaphores(2),
    ]


def wide_back_first_kernel(place_ref, rounded_ref, second_ref, slope_ref, *refs):
    ups, downs, refs = refs[:4], refs[4:12], refs[12:]
    sends, (shift_ref, total_ref, *refs) = refs[:8], refs[8:]
    held, sems, sent, out_sems = refs[:3], refs[3:6], refs[6], refs[7]
    step = pl.program_id(0)

    @pl.when(step == 0)
    def _():
        wide_back_start(0, place_ref, slope_ref, ups, downs, held, sems)
        total_ref[...] = jnp.zeros_like(total_ref)

    up_grad = wide_back_step(
        step, rounded_ref, second_ref, slope_ref, ups, downs, held, sems, shift_ref, total_ref
    )
    for side in range(2):
        sent[step, side ^ place_ref[1]] = up_grad[:, side].astype(BF)

    def out_copy(at, half, dy):
        lanes = slice(half * TILE, (half + 1) * TILE)
        number = 4 * at + 2 * half + dy
        return copy(sent.at[at, dy, :, :, lanes], sends[number], out_sems.at[at, half, dy])

    pieces = [(half, dy) for half in range(2) for dy in range(2)]
    for at in range(2):

        @pl.when(step == at)
        def _():
            for half, dy in pieces:
                out_copy(at, half, dy).start()

    @pl.when(step == 1)
    def _():
        for at in range(2):
            for half, dy in pieces:
                out_copy(at, half, dy).wait()


def wide_back_first(place, rounded, second, slope, up_parts, down_parts):
    full = whole_block((ROWS, D))
    return pl.pallas_call(
        wide_back_first_kernel,
        grid=(2,),
        in_specs=[SMEM_SPEC, full, full] + [ANY_SPEC] * 13,
        out_specs=(ANY_SPEC,) * 8 + (whole_block((2, WIDE)), full),
        out_shape=(sds((4, SHARD, TILE), BF),) * 8 + (sds((2, WIDE), F32), sds((ROWS, D), F32)),
        scratch_shapes=wide_back_scratch()
        + [pltpu.VMEM((2, 2, 4, SHARD, WIDE), BF), semaphores(2, 2, 2)],
        **KERNEL,
    )(place, rounded, second, slope, *up_parts[2:4], *up_parts[6:8], *down_parts)


def wide_back_last_kernel(place_ref, rounded_ref, second_ref, slope_ref, *refs):
    ups, downs, refs = refs[:4], refs[4:12], refs[12:]
    before_ref, grad_ref, middle_ref, gains_ref, *refs = refs
    gots, refs = refs[:8], refs[8:]
    outs, (shift_ref, grad_out, rounded_out, small_ref, *refs) = refs[:2], refs[2:]
    held, sems, refs = refs[:3], refs[3:6], refs[6:]
    kept, got, total, grads, middles, roundeds, got_sems, out_sems, in_sems, row_sems = refs
    step = pl.program_id(0)
    fetched = (
        copy(before_ref, total, in_sems.at[0]),
        copy(grad_ref, grads, in_sems.at[1]),
        copy(middle_ref, middles, in_sems.at[2]),
    )

    pieces = [(half, dy) for half in range(2) for dy in range(2)]

    def got_copy(at, half, dy):
        lanes = slice(half * TILE, (half + 1) * TILE)
        target = got.at[at, dy, :, :, lanes]
        return copy(gots[4 * at + 2 * half + dy], target, got_sems.at[at, half, dy])

    @pl.when(step == 0)
    def _():
        fetched[0].start()
        wide_back_start(1, place_ref, slope_ref, ups, downs, held, sems)
        for at in range(2):
            for half, dy in pieces:
                got_copy(at, half, dy).start()
        fetched[1].start()
        fetched[2].start()
        fetched[0].wait()

    up_grad = wide_back_step(
        step, rounded_ref, second_ref, slope_ref, ups, downs, held, sems, shift_ref, total
    )
    for half, dy in pieces:
        lanes = slice(half * TILE, (half + 1) * TILE)
        copy(gots[0], got.at[step, dy, :, :, lanes], got_sems.at[step, half, dy]).wait()
    for side in range(2):
        at_side = side ^ place_ref[1]
        kept[step, at_side] = (up_grad[:, side] + got[step, at_side].astype(F32)).astype(BF)

    def out_copy(at, half, dy):
        lanes = slice(half * TILE, (half + 1) * TILE)
        target = outs[at].at[dy, :, half]
        return copy(kept.at[at, dy, :, :, lanes], target, out_sems.at[at, half, dy])

    for at in range(2):

        @pl.when(step == at)
        def _():
            for half, dy in pieces:
                out_copy(at, half, dy).start()

    @pl.when(step == 1)
    def _():
        fetched[1].wait()
        fetched[2].wait()
        sums = [jnp.zeros((1, D), F32)] * 4
        sent = []
        for index in range(CHUNKS):
            rows = chunk_rows(index)
            normed, inverse = normalize(middles[rows, :])
            grad_second = total[rows, :]
            grad = grads[rows, :] + norm_back(grad_second * gains_ref[1:2, :], normed, inverse)
            rounded = grad.astype(BF)
            grads[rows, :] = grad
            roundeds[rows, :] = rounded
            sent.append(copy(grads.at[rows, :], grad_out.at[rows, :], row_sems.at[index, 0]))
            sent.append(copy(roundeds.at[rows, :], rounded_out.at[rows, :], row_sems.at[index, 1]))
            sent[-2].start()
            sent[-1].start()
            terms = (
                grad_second * normed,
                grad_second,
                rounded.astype(F32),
                rounded_ref[rows, :].astype(F32),
            )
            sums = [old + col_sum(term) for old, term in zip(sums, terms)]
        small_ref[...] = jnp.zeros_like(small_ref)
        for number in range(4):
            small_ref[number : number + 1, :] = sums[number]
        for at in range(2):
            for half, dy in pieces:
                out_copy(at, half, dy).wait()
        for one in sent:
            one.wait()


def wide_back_last(
    place, rounded, second, slope, up_parts, down_parts, before, grad, middle, gains, *got
):
    full = whole_block((ROWS, D))
    out = sds((2, 4, 2, SHARD, TILE), BF)
    return pl.pallas_call(
        wide_back_last_kernel,
        grid=(2,),
        in_specs=[SMEM_SPEC, full, full]
        + [ANY_SPEC] * 16
        + [whole_block((2, D))]
        + [ANY_SPEC] * 8,
        out_specs=(ANY_SPEC, ANY_SPEC, whole_block((2, WIDE)), ANY_SPEC, ANY_SPEC, whole_block((8, D))),
        out_shape=(
            out,
            out,
            sds((2, WIDE), F32),
            sds((ROWS, D), F32),
            sds((ROWS, D), BF),
            sds((8, D), F32),
        ),
        scratch_shapes=wide_back_scratch()
        + [
            pltpu.VMEM((2, 2, 4, SHARD, WIDE), BF),
            pltpu.VMEM((2, 2, 4, SHARD, WIDE), BF),
            pltpu.VMEM((ROWS, D), F32),
            pltpu.VMEM((ROWS, D), F32),
            pltpu.VMEM((ROWS, D), F32),
            pltpu.VMEM((ROWS, D), BF),
            semaphores(2, 2, 2),
            semaphores(2, 2, 2),
            semaphores(3),
            semaphores(CHUNKS, 2),
        ],
        **KERNEL,
    )(
        place, rounded, second, slope, *up_parts[0:2], *up_parts[4:6], *down_parts,
        before, grad, middle, gains, *got
    )


def mix_back_kernel(place_ref, lengths_ref, rounded_ref, grad_ref, residual_ref, *refs):
    buffers, (packed_ref, log_ref, mixed_ref, gains_ref, biases_ref, *refs) = refs[:8], refs[8:]
    sends, (pre_out, rights_out, grad_out, rounded_out, small_ref, *refs) = refs[:4], refs[4:]
    held, packed, sent, pre, rights, grad_mixed, total, grads, roundeds, *refs = refs
    sems, in_sems, send_sems, pre_sem, right_sems, row_sems = refs
    x_at, y_at, c_at = place_ref[0], place_ref[1], place_ref[2]
    copies = quarter_copies(place_ref, buffers, held, sems)
    for one in copies:
        one.start()
    fetched = [
        copy(packed_ref.at[chunk_rows(at), :], packed.at[chunk_rows(at), :], in_sems.at[at])
        for at in range(SEQ_DEV)
    ]
    fetched.append(copy(grad_ref, grads, in_sems.at[SEQ_DEV]))
    for one in fetched:
        one.start()

    def send_grad(part, right):
        @pl.when(c_at ^ (part & 1) == 1)
        def _():
            left = mixed_ref[...] if part == 3 else pre[...]
            value = mul_tn(left, right).astype(BF).reshape(4, 2, SHARD, D)
            for side in range(2):
                sent[x_at ^ (part >> 1), side ^ y_at] = value[:, side]

    send_grad(3, rounded_ref[...])

    def first(rows, carry):
        normed, inverse = normalize(residual_ref[rows, :].astype(F32))
        pre[rows, :] = (normed * gains_ref[0:1, :] + biases_ref[0:1, :]).astype(BF)
        return carry

    over_chunks(first, 0)
    pre_copy = copy(pre, pre_out, pre_sem.at[0])
    pre_copy.start()
    for one in copies:
        one.wait()
    grad_mixed[...] = mul_nt(rounded_ref[...], square(held[:, :, :, 3 * D :])).astype(BF)
    masks = head_masks()
    row_ids = lax.broadcasted_iota(jnp.int32, (LEN, 1), 0)
    scale = 1.0 / math.sqrt(HEAD_DIM)

    def right_copy(seq, part):
        rows = pl.ds(pl.multiple_of(seq * LEN, LEN), LEN)
        lanes = slice(part * D, (part + 1) * D)
        return copy(rights.at[rows, lanes], rights_out.at[part, rows, :], right_sems.at[seq, part])

    def one_sequence(seq, carry):
        rows = pl.ds(pl.multiple_of(seq * LEN, LEN), LEN)
        copy(packed_ref.at[chunk_rows(0), :], packed.at[rows, :], in_sems.at[seq]).wait()
        valid = row_ids < lengths_ref[seq]
        for group in range(GROUPS):
            at_query = slice(group * 128, (group + 1) * 128)
            queries = stack_heads(packed[rows, at_query], masks)
            key_rows = packed[rows, D + group * 128 : D + (group + 1) * 128]
            value_rows = packed[rows, 2 * D + group * 128 : 2 * D + (group + 1) * 128]
            mixed_grads = stack_heads(grad_mixed[rows, at_query], masks)
            scores = scores_of(key_rows, queries, valid)
            probs = jnp.exp(scores - log_ref[seq * GROUPS + group])
            grad_probs = mul_nt(value_rows, mixed_grads)
            inner = jnp.sum(grad_probs * probs, 0, keepdims=True)
            grad_scores = (probs * (grad_probs - inner)).astype(BF)
            rights[rows, 2 * D + group * 128 : 2 * D + (group + 1) * 128] = mul_nn(probs.astype(BF), mixed_grads).astype(BF)
            rights[rows, D + group * 128 : D + (group + 1) * 128] = (mul_nn(grad_scores, queries) * scale).astype(BF)
            grad_queries = unstack_heads(mul_tn(key_rows, grad_scores))
            rights[rows, at_query] = (grad_queries * scale).astype(BF)
        for part in range(3):
            right_copy(seq, part).start()
        return carry

    lax.fori_loop(0, SEQ_DEV, one_sequence, 0)
    for part in range(3):
        send_grad(part, rights[:, part * D : (part + 1) * D])
    for dx in range(2):
        for dy in range(2):
            copy(sent.at[dx, dy], sends[2 * dx + dy], send_sems.at[dx, dy]).start()
    total[...] = mul_nt(rights[...], square(held[:, :, :, : 3 * D]))
    fetched[-1].wait()
    sums = [jnp.zeros((1, D), F32)] * 4
    out_copies = []
    for index in range(CHUNKS):
        rows = chunk_rows(index)
        normed, inverse = normalize(residual_ref[rows, :].astype(F32))
        grad_pre = total[rows, :]
        grad = grads[rows, :] + norm_back(grad_pre * gains_ref[0:1, :], normed, inverse)
        grads[rows, :] = grad
        roundeds[rows, :] = grad.astype(BF)
        out_copies.append(copy(grads.at[rows, :], grad_out.at[rows, :], row_sems.at[index, 0]))
        out_copies.append(copy(roundeds.at[rows, :], rounded_out.at[rows, :], row_sems.at[index, 1]))
        out_copies[-2].start()
        out_copies[-1].start()
        terms = (
            grad_pre * normed,
            grad_pre,
            rights[rows, 0:D].astype(F32),
            rights[rows, 2 * D : 3 * D].astype(F32),
        )
        sums = [old + col_sum(term) for old, term in zip(sums, terms)]
    small_ref[...] = jnp.zeros_like(small_ref)
    for number in range(4):
        small_ref[number : number + 1, :] = sums[number]
    for seq in range(SEQ_DEV):
        for part in range(3):
            right_copy(seq, part).wait()
    for dx in range(2):
        for dy in range(2):
            copy(sent.at[dx, dy], sends[2 * dx + dy], send_sems.at[dx, dy]).wait()
    for one in [pre_copy] + out_copies:
        one.wait()


def mix_back(
    place, lengths, rounded, middle_grad, residual, quarters, packed, logs, mixed, gains, biases
):
    part = sds((4, SHARD, D), BF)
    full = whole_block((ROWS, D))
    return pl.pallas_call(
        mix_back_kernel,
        out_shape=(part,) * 4
        + (
            sds((ROWS, D), BF),
            sds((3, ROWS, D), BF),
            sds((ROWS, D), F32),
            sds((ROWS, D), BF),
            sds((8, D), F32),
        ),
        grid=(1,),
        in_specs=[SMEM_SPEC, SMEM_SPEC, full, ANY_SPEC, full]
        + [ANY_SPEC] * 9
        + [whole_block((SEQ_DEV * GROUPS, 1, PER_GROUP * LEN)), full]
        + [whole_block((2, D)), whole_block((6, D))],
        out_specs=(ANY_SPEC,) * 8 + (whole_block((8, D)),),
        scratch_shapes=[
            pltpu.VMEM((4, 2, SHARD, 4 * D), BF),
            pltpu.VMEM((ROWS, 3 * D), BF),
            pltpu.VMEM((2, 2, 4, SHARD, D), BF),
            pltpu.VMEM((ROWS, D), BF),
            pltpu.VMEM((ROWS, 3 * D), BF),
            pltpu.VMEM((ROWS, D), BF),
            pltpu.VMEM((ROWS, D), F32),
            pltpu.VMEM((ROWS, D), F32),
            pltpu.VMEM((ROWS, D), BF),
            semaphores(8),
            semaphores(SEQ_DEV + 1),
            semaphores(2, 2),
            semaphores(1),
            semaphores(SEQ_DEV, 3),
            semaphores(CHUNKS, 2),
        ],
        **KERNEL,
    )(
        place, lengths, rounded, middle_grad, residual, *quarters, packed, logs, mixed, gains, biases
    )


def mix_back_last_kernel(place_ref, pre_ref, mixed_ref, rights_ref, rounded_ref, *refs):
    gots, outs, (lefts, rights, got, kept, sems, out_sems) = refs[:4], refs[4:6], refs[6:]
    y_at, c_at = place_ref[1], place_ref[2]
    parts = [(place_ref[0] ^ dx) * 2 + c_at for dx in range(2)]
    for dx in (1, 0):

        @pl.when(parts[dx] == 3)
        def _():
            copy(mixed_ref, lefts.at[dx], sems.at[dx, 3]).start()
            copy(rounded_ref, rights.at[dx], sems.at[dx, 0]).start()

        @pl.when(parts[dx] != 3)
        def _():
            copy(pre_ref, lefts.at[dx], sems.at[dx, 3]).start()
            copy(rights_ref.at[jnp.minimum(parts[dx], 2)], rights.at[dx], sems.at[dx, 0]).start()

        for dy in range(2):
            copy(gots[2 * dx + dy], got.at[dx, dy], sems.at[dx, 1 + dy]).start()
    for dx in (1, 0):
        copy(pre_ref, lefts.at[dx], sems.at[dx, 3]).wait()
        copy(rounded_ref, rights.at[dx], sems.at[dx, 0]).wait()
        value = mul_tn(lefts[dx], rights[dx]).reshape(4, 2, SHARD, D)
        for dy in range(2):
            copy(gots[0], got.at[dx, dy], sems.at[dx, 1 + dy]).wait()
        for side in range(2):
            at = side ^ y_at
            kept[dx, at] = (value[:, side] + got[dx, at].astype(F32)).astype(BF)
        copy(kept.at[dx], outs[1 - dx], out_sems.at[dx]).start()
    for dx in range(2):
        copy(kept.at[dx], outs[1 - dx], out_sems.at[dx]).wait()


def mix_back_last(place, pre, mixed, rights, rounded, *got):
    out = sds((2, 4, SHARD, D), BF)
    return pl.pallas_call(
        mix_back_last_kernel,
        grid=(1,),
        in_specs=[SMEM_SPEC] + [ANY_SPEC] * 8,
        out_specs=(ANY_SPEC,) * 2,
        out_shape=(out, out),
        scratch_shapes=[
            pltpu.VMEM((2, ROWS, D), BF),
            pltpu.VMEM((2, ROWS, D), BF),
            pltpu.VMEM((2, 2, 4, SHARD, D), BF),
            pltpu.VMEM((2, 2, 4, SHARD, D), BF),
            semaphores(2, 4),
            semaphores(2),
        ],
        **KERNEL,
    )(place, pre, mixed, rights, rounded, *got)


def finish_kernel(layer, olds, place_ref, *refs):
    quarters, halves, outs = refs[:4], refs[4:8], refs[8 + olds : 11 + olds]
    attn, ups, downs, sems = refs[11 + olds :]
    x_at, c_at = place_ref[0], place_ref[2]
    values = [ref[...] for ref in quarters]
    pairs = [
        (jnp.where(c_at == 0, own, other), jnp.where(c_at == 0, other, own))
        for own, other in (values[:2], values[2:])
    ]
    ordered = [jnp.where(x_at == 0, own, other) for own, other in zip(*pairs)]
    ordered += [jnp.where(x_at == 0, other, own) for own, other in zip(*pairs)]
    for quarter, value in enumerate(ordered):
        for tile in range(3):
            target, first, stride = (
                (attn, quarter * 5, 20) if tile == 2 else (ups, quarter * 10 + tile * 5, 40)
            )
            for block in range(5):
                target[pl.ds(first + block, SHARD, stride=stride), :] = value[
                    tile, :, block * 128 : (block + 1) * 128
                ].astype(F32)
    copies = [
        copy(target, out.at[layer], sems.at[number])
        for number, (target, out) in enumerate(zip((attn, ups, downs), outs))
    ]
    copies[0].start()
    copies[1].start()
    own, other = (
        halves[at][...].astype(F32) + halves[at + 2][...].astype(F32) for at in range(2)
    )
    turned = jnp.concatenate(
        [jnp.where(c_at == 0, own, other), jnp.where(c_at == 0, other, own)], 0
    ).T
    for block in range(5):
        downs[pl.ds(block, TILE, stride=5), :] = turned[:, block * 128 : (block + 1) * 128]
    copies[2].start()
    for one in copies:
        one.wait()


def finish(layer, place, quarters, halves, *old):
    attn, wide = (D * 4 * D // 8 // 128, 128), (D * FF // 8 // 128, 128)

    def kernel(*refs):
        finish_kernel(layer, len(old), *refs)

    return pl.pallas_call(
        kernel,
        grid=(1,),
        in_specs=[SMEM_SPEC]
        + [whole_block((3, SHARD, D))] * 4
        + [whole_block((HALF, TILE))] * 4
        + [ANY_SPEC] * len(old),
        out_specs=(ANY_SPEC,) * 3,
        out_shape=tuple(sds((LAYERS, *shape), F32) for shape in (attn, wide, wide)),
        scratch_shapes=[pltpu.VMEM(shape, F32) for shape in (attn, wide, wide)] + [semaphores(3)],
        input_output_aliases={9 + number: number for number in range(len(old))},
        **KERNEL,
    )(place, *quarters, *halves, *old)


def swap(value, axis, name):
    with jax.named_scope(name):
        return lax.ppermute(value, axis, [(0, 1), (1, 0)])


def swaps(values, axis, name):
    return [swap(value, axis, name) for value in values]


class Order:
    def __init__(self):
        self.last = None

    def hold(self, *arrays):
        if self.last is not None:
            arrays = lax.optimization_barrier((arrays, self.last))[0]
        return arrays

    def __call__(self, function, *arrays):
        results = function(*self.hold(*arrays))
        self.last = jax.tree.leaves(results)[0]
        return results


def wide_sum(*values):
    total = values[0].astype(F32)
    for value in values[1:]:
        total = total + value.astype(F32)
    return total


def rounded_sum(*values):
    return wide_sum(*values).astype(BF)


def plus(own, other):
    return own + other


class Moves:
    def __init__(self, fsdp):
        self.z_size = fsdp // 2
        self.staged = fsdp == 8
        self.x_at = lax.axis_index("x")
        self.y_at = lax.axis_index("y")
        self.z_at = lax.axis_index("z")
        self.c_at = lax.axis_index("c")
        self.place = jnp.stack([self.x_at, self.y_at, self.c_at]).astype(jnp.int32)

    def hop(self, value, reach, name):
        with jax.named_scope(name):
            return lax.ppermute(value, "z", [(at, at ^ reach) for at in range(self.z_size)])

    def ordered(self, bit, own, other):
        return jnp.where(bit == 0, jnp.stack([own, other]), jnp.stack([other, own]))

    def by_side(self, value):
        value = value.reshape(4, 2, *value.shape[1:]).swapaxes(0, 1)
        return jnp.where(self.y_at == 0, value, value[::-1])

    def by_shard(self, value):
        value = jnp.where(self.y_at == 0, value, value[::-1]).swapaxes(0, 1)
        return value.reshape(8, *value.shape[2:])

    def own_quarter(self, flat):
        shard = flat.reshape(SHARD, -1, 128)
        step = shard.shape[1] // 4
        own = lax.dynamic_slice_in_dim(shard, (self.x_at * 2 + self.c_at) * step, step, 1)
        return own.reshape(SHARD, step // 5, 5, 128).swapaxes(0, 1).reshape(-1, SHARD, D)

    def own_half(self, flat):
        own = lax.dynamic_slice_in_dim(flat, self.c_at * HALF * 5, HALF * 5, 0)
        return own.reshape(1, HALF, D)

    def high(self, own, other):
        return self.ordered(self.z_at // 2, own, other)

    def low(self, pair, other):
        bit = self.z_at % 2
        line = jnp.where(bit == 0, jnp.stack([pair, other], 1), jnp.stack([other, pair], 1))
        return (line.reshape(4, *pair.shape[1:]),)

    def low_halves(self, pair, other):
        line = self.low(pair, other)[0][:, 0]
        return line[:2], line[2:]

    def part_near(self, *parts):
        total = wide_sum(*parts)
        total = total.reshape(2, 2, *total.shape[1:])
        near = self.z_at % 2
        return tuple(
            lax.dynamic_index_in_dim(total, at, 1, False).astype(BF) for at in (1 - near, near)
        )

    def part_far(self, *parts):
        total = wide_sum(*parts)
        far = self.z_at // 2
        return tuple(
            lax.dynamic_index_in_dim(total, at, 0, False).astype(BF) for at in (1 - far, far)
        )

    def along_z(self, part):
        return lax.psum_scatter(part, "z", scatter_dimension=0, tiled=False)

    def plain_quarters(self, flat):
        whole = lax.all_gather(flat, ("z", "y"), axis=0, tiled=True)
        whole = whole.reshape(8, SHARD, 4, -1, D).transpose(2, 0, 3, 1, 4)
        lines = []
        for number in range(4):
            quarter = (self.x_at ^ (number >> 1)) * 2 + (self.c_at ^ (number & 1))
            part = self.by_side(lax.dynamic_index_in_dim(whole, quarter, 0, False))
            lines += [part[dy] for dy in range(2)]
        return lines

    def plain_halves(self, flat):
        whole = lax.all_gather(flat, ("z", "y"), axis=0, tiled=True).reshape(8, 2, HALF, D)
        pairs = []
        for number in range(2):
            part = self.by_side(lax.dynamic_index_in_dim(whole, self.c_at ^ number, 1, False))
            pairs += [part[dy, 2 * at : 2 * at + 2] for dy in range(2) for at in range(2)]
        return pairs

    def plain_quarters_back(self, passed, keep):
        part = self.by_shard(rounded_sum(keep, swap(passed, "x", "quarters")))
        part = part.transpose(0, 2, 1, 3).reshape(D, -1)
        part = lax.psum_scatter(part, ("z", "y"), scatter_dimension=0, tiled=True)
        parts = lax.all_gather(part, ("x", "c"), axis=0, tiled=False)
        return parts.swapaxes(0, 1).astype(F32).reshape(-1, 128)

    def plain_halves_back(self, part):
        part = self.by_shard(part).transpose(0, 2, 1).reshape(FF, HALF)
        part = lax.psum_scatter(part, ("z", "y"), scatter_dimension=0, tiled=True).T
        part = rounded_sum(part, swap(part, "x", "halves"))
        return lax.all_gather(part, "c", axis=0, tiled=True).T.astype(F32).reshape(-1, 128)

    def sum_all(self, value):
        for axis in ("c", "x", "y"):
            value = value + swap(value, axis, "small")
        reach = 1
        while reach < self.z_size:
            value = value + self.hop(value, reach, "small")
            reach *= 2
        return value


def local(
    fsdp,
    inputs,
    targets,
    masked,
    lengths,
    attn_weight,
    up_weight,
    down_weight,
    norm_gains,
    layer_biases,
    up_bias,
    head_weight,
    final_gain,
    final_shift,
    head_bias,
):
    moves = Moves(fsdp)
    place = moves.place
    shifts = up_bias.reshape(LAYERS, STEPS, WIDE)
    run = Order()

    def mix_on(layer):
        return lambda r, *q: mix(place, lengths, r, q, norm_gains[layer], layer_biases[layer])

    def up_on(layer):
        return lambda second, *parts: up(place, second, parts, shifts[layer])

    def down_on(layer):
        return lambda m, active, *parts: down(place, m, active, parts, layer_biases[layer])

    def prepared(targets, masked, head_weight, head_bias):
        wide_bias = head_bias.reshape(1, VOCAB)
        return (
            targets.reshape(ROWS, 1),
            masked.reshape(ROWS, 1),
            jnp.pad(head_weight, ((0, 0), (0, 128 - VOCAB))),
            jnp.pad(wide_bias, ((0, 0), (0, 128 - VOCAB)), constant_values=-1e30),
        )

    def fan(lines, name):
        return [swaps(lines, axis, name + "_" + axis) for axis in "yxc"]

    def fan_y(y, name):
        return [swaps(y, axis, name + "_y" + axis) for axis in "xc"]

    def fan_x(x, yx, name):
        return swaps(x, "c", name + "_xc"), swaps(yx, "c", name + "_yxc")

    def in_place(own, y, x, c, yx, yc, xc, yxc):
        return [part[0] for part in (own, y, c, yc, x, yx, xc, yxc)]

    if moves.staged:
        a0 = run(moves.own_quarter, attn_weight[0])
        a0_far = moves.hop(a0, 2, "a0_far")
        u0 = run(moves.own_quarter, up_weight[0])
        u0_far = moves.hop(u0, 2, "u0_far")
        d0 = run(moves.own_half, down_weight[0])
        a0 = run(moves.high, a0, a0_far)
        a0_near = moves.hop(a0, 1, "a0_near")
        u0 = run(moves.high, u0, u0_far)
        u0_near = moves.hop(u0, 1, "u0_near")
        (d0,) = run.hold(d0)
        d0_far = moves.hop(d0, 2, "d0_far")
        a1 = run(moves.own_quarter, attn_weight[1])
        a0 = run(moves.low, a0, a0_near)
        a0_y, a0_x, a0_c = fan(a0, "a0")
        u1 = run(moves.own_quarter, up_weight[1])
        d1 = run(moves.own_half, down_weight[1])
        a0_y = run.hold(*a0_y)
        a0_yx, a0_yc = fan_y(a0_y, "a0")
        u0 = run(moves.low, u0, u0_near)
        u0_y, u0_x, u0_c = fan(u0, "u0")
        d0 = run(moves.high, d0, d0_far)
        d0_near = moves.hop(d0, 1, "d0_near")
        ready = run(prepared, targets, masked, head_weight, head_bias)
        a0_x, a0_yx = run.hold(a0_x, a0_yx)
        a0_xc, a0_yxc = fan_x(a0_x, a0_yx, "a0")
        quarters0 = in_place(a0, a0_y, a0_x, a0_c, a0_yx, a0_yc, a0_xc, a0_yxc)
        mixed0 = run(mix_on(0), inputs, *quarters0)
        u0_y = run.hold(*u0_y)
        u0_yx, u0_yc = fan_y(u0_y, "u0")
        d0 = run(moves.low_halves, d0, d0_near)
        d0_y, d0_c = swaps(d0, "y", "d0_y"), swaps(d0, "c", "d0_c")
        a1, u1, d1 = run.hold(a1, u1, d1)
        a1_far = moves.hop(a1, 2, "a1_far")
        u1_far = moves.hop(u1, 2, "u1_far")
        a1 = run(moves.high, a1, a1_far)
        a1_near = moves.hop(a1, 1, "a1_near")
        u1 = run(moves.high, u1, u1_far)
        u1_near = moves.hop(u1, 1, "u1_near")
        u0_x, u0_yx = run.hold(u0_x, u0_yx)
        u0_xc, u0_yxc = fan_x(u0_x, u0_yx, "u0")
        a1 = run(moves.low, a1, a1_near)
        a1_y, a1_x, a1_c = fan(a1, "a1")
        d1_far = moves.hop(d1, 2, "d1_far")
        ups0 = in_place(u0, u0_y, u0_x, u0_c, u0_yx, u0_yc, u0_xc, u0_yxc)
        wide0 = run(up_on(0), mixed0[4], *ups0)
        u1 = run(moves.low, u1, u1_near)
        u1_y, u1_x, u1_c = fan(u1, "u1")
        d1 = run(moves.high, d1, d1_far)
        d1_near = moves.hop(d1, 1, "d1_near")
        d0_y = run.hold(*d0_y)
        d0_yc = swaps(d0_y, "c", "d0_yc")
        downs0 = (*d0, *d0_y, *d0_c, *d0_yc)
        residual1 = run(down_on(0), mixed0[3], wide0[0], *downs0)
        a1_y = run.hold(*a1_y)
        a1_yx, a1_yc = fan_y(a1_y, "a1")
        d1 = run(moves.low_halves, d1, d1_near)
        d1_y, d1_c = swaps(d1, "y", "d1_y"), swaps(d1, "c", "d1_c")
        a1_x, a1_yx = run.hold(a1_x, a1_yx)
        a1_xc, a1_yxc = fan_x(a1_x, a1_yx, "a1")
        u1_y = run.hold(*u1_y)
        u1_yx, u1_yc = fan_y(u1_y, "u1")
        quarters1 = in_place(a1, a1_y, a1_x, a1_c, a1_yx, a1_yc, a1_xc, a1_yxc)
        mixed1 = run(mix_on(1), residual1, *quarters1)
        u1_x, u1_yx = run.hold(u1_x, u1_yx)
        u1_xc, u1_yxc = fan_x(u1_x, u1_yx, "u1")
        ups1 = in_place(u1, u1_y, u1_x, u1_c, u1_yx, u1_yc, u1_xc, u1_yxc)
        wide1 = run(up_on(1), mixed1[4], *ups1)
        d1_y = run.hold(*d1_y)
        d1_yc = swaps(d1_y, "c", "d1_yc")
        downs1 = (*d1, *d1_y, *d1_c, *d1_yc)
        residual = run(down_on(1), mixed1[3], wide1[0], *downs1)
        weights = [(quarters0, ups0, downs0), (quarters1, ups1, downs1)]
        saved = [(inputs, *mixed0, *wide0), (residual1, *mixed1, *wide1)]
    else:
        weights, saved = [], []
        residual = inputs
        for layer in range(LAYERS):
            quarters = moves.plain_quarters(attn_weight[layer])
            ups = moves.plain_quarters(up_weight[layer])
            downs = moves.plain_halves(down_weight[layer])
            weights.append((quarters, ups, downs))
            mixed = mix_on(layer)(residual, *quarters)
            wide = up_on(layer)(mixed[4], *ups)
            saved.append((residual, *mixed, *wide))
            residual = down_on(layer)(mixed[3], wide[0], *downs)
        ready = prepared(targets, masked, head_weight, head_bias)
    activations, grad, rounded, head_small = run(
        head, residual, *ready, final_gain.reshape(1, D), final_shift.reshape(1, D)
    )

    def down_at(layer):
        return lambda rounded: down_back(place, rounded, saved[layer][6])

    def wide_first(layer):
        _, ups, downs = weights[layer]
        _, _, _, _, _, second, _, slope = saved[layer]
        return lambda rounded: wide_back_first(place, rounded, second, slope, ups, downs)

    def wide_last(layer):
        _, ups, downs = weights[layer]
        _, _, _, _, middle, second, _, slope = saved[layer]
        return lambda rounded, before, grad, *got: wide_back_last(
            place, rounded, second, slope, ups, downs, before, grad, middle, norm_gains[layer], *got
        )

    def mix_first(layer):
        residual, packed, logs, mixed, _, _, _, _ = saved[layer]
        quarters = weights[layer][0]
        gains, biases = norm_gains[layer], layer_biases[layer]
        return lambda rounded, grad: mix_back(
            place, lengths, rounded, grad, residual, quarters, packed, logs, mixed, gains, biases
        )

    def mix_last(*arrays):
        return mix_back_last(place, *arrays)

    def shift_rows(shift_send, shift_keep):
        send, keep = (part.reshape(2, 2, TILE)[::-1] for part in (shift_send, shift_keep))
        parts = moves.ordered(moves.c_at, keep, send).swapaxes(0, 1)
        return jnp.where(moves.x_at == 0, parts, parts[::-1]).reshape(TILES, TILE)

    def packed_small(head_small, *rest):
        small = [head_small]
        for layer in range(LAYERS):
            shift_send, shift_keep, wide_small, mix_small = rest[4 * layer : 4 * layer + 4]
            small += [shift_rows(shift_send, shift_keep), wide_small, mix_small]
        return jnp.concatenate(small, 0)

    def sum_at(at):
        return lambda keep, got, *rest: rounded_sum(keep[at], got[at], *rest)

    if moves.staged:
        *d1_send, d1_keep = run(down_at(1), rounded)
        d1_c = swaps(d1_send, "c", "d1_c")
        *u1_send, shift_send1, before = run(wide_first(1), rounded)
        u1_c = swaps(u1_send, "c", "u1_c")
        d1_y = swap(run(lambda k, *c: down_sum(1, k, c), d1_keep, *d1_c[:4]), "y", "d1_y")
        u1_pass, u1_keep, shift_keep1, grad, rounded1, wide_small1 = run(
            wide_last(1), rounded, before, grad, *u1_c
        )
        u1_x = swap(u1_pass, "x", "u1_x")
        *a1_send, pre1, rights1, grad, rounded, mix_small1 = run(mix_first(1), rounded1, grad)
        a1_c = swaps(a1_send, "c", "a1_c")
        *d0_send, d0_keep = run(down_at(0), rounded)
        d0_c = swaps(d0_send, "c", "d0_c")
        a1_pass, a1_keep = run(mix_last, pre1, saved[1][3], rights1, rounded1, *a1_c)
        a1_x = swap(a1_pass, "x", "a1_x")
        d1 = run(lambda k, y, *c: down_sum(0, k, c, y), d1_keep, d1_y, *d1_c[4:])
        d1 = moves.along_z(d1)
        d0_y = swap(run(lambda k, *c: down_sum(1, k, c), d0_keep, *d0_c[:4]), "y", "d0_y")
        *u0_send, shift_send0, before = run(wide_first(0), rounded)
        u0_c = swaps(u0_send, "c", "u0_c")
        u1_y = swap(run(sum_at(1), u1_keep, u1_x), "y", "u1_y")
        a1_y = swap(run(sum_at(1), a1_keep, a1_x), "y", "a1_y")
        u0_pass, u0_keep, shift_keep0, grad, rounded0, wide_small0 = run(
            wide_last(0), rounded, before, grad, *u0_c
        )
        u0_x = swap(u0_pass, "x", "u0_x")
        d0 = run(lambda k, y, *c: down_sum(0, k, c, y), d0_keep, d0_y, *d0_c[4:])
        d0 = moves.along_z(d0)
        (d1,) = run.hold(d1)
        d1_x, d1_c = swap(d1, "x", "d1_x"), swap(d1, "c", "d1_c")

        def last_sums(u, ux, uy, a, ax, ay):
            both = (wide_sum(u[0], ux[0], uy), wide_sum(a[0], ax[0], ay)[:, None])
            return moves.part_near(jnp.concatenate(both, 1))

        *a0_send, pre0, rights0, grad, rounded, mix_small0 = run(mix_first(0), rounded0, grad)
        a0_c = swaps(a0_send, "c", "a0_c")
        j1_send, j1_stay = run(last_sums, u1_keep, u1_x, u1_y, a1_keep, a1_x, a1_y)
        j1_near = moves.hop(j1_send, 1, "j1_near")
        a0_pass, a0_keep = run(mix_last, pre0, saved[0][3], rights0, rounded0, *a0_c)
        a0_x = swap(a0_pass, "x", "a0_x")
        small = run(
            packed_small,
            head_small,
            *(shift_send0, shift_keep0, wide_small0, mix_small0),
            *(shift_send1, shift_keep1, wide_small1, mix_small1),
        )
        small_c = swap(small, "c", "small_c")
        (d1_x,) = run.hold(d1_x)
        d1_xc = swap(d1_x, "c", "d1_xc")
        u0_y = swap(run(sum_at(1), u0_keep, u0_x), "y", "u0_y")
        small = run(plus, small, small_c)
        small_far = moves.hop(small, 2, "small_far")
        j1_send, j1_stay = run(moves.part_far, j1_stay, j1_near)
        j1_far = moves.hop(j1_send, 2, "j1_far")
        (d0,) = run.hold(d0)
        d0_x, d0_c = swap(d0, "x", "d0_x"), swap(d0, "c", "d0_c")
        small = run(plus, small, small_far)
        small_near = moves.hop(small, 1, "small_near")
        a0_y = swap(run(sum_at(1), a0_keep, a0_x), "y", "a0_y")
        u0 = moves.along_z(run(sum_at(0), u0_keep, u0_x, u0_y))
        j1 = run(rounded_sum, j1_stay, j1_far)
        j1_x, j1_c = swap(j1, "x", "j1_x"), swap(j1, "c", "j1_c")
        small = run(plus, small, small_near)
        small_x = swap(small, "x", "small_x")
        (d0_x,) = run.hold(d0_x)
        d0_xc = swap(d0_x, "c", "d0_xc")
        a0_send, a0_stay = run(lambda k, x, y: moves.part_near(k[0], x[0], y), a0_keep, a0_x, a0_y)
        a0_near = moves.hop(a0_send, 1, "a0_near")
        small = run(plus, small, small_x)
        small_y = swap(small, "y", "small_y")
        (j1_x,) = run.hold(j1_x)
        j1_xc = swap(j1_x, "c", "j1_xc")
        a0_send, a0_stay = run(moves.part_far, a0_stay, a0_near)
        a0_far = moves.hop(a0_send, 2, "a0_far")
        summed = run(plus, small, small_y)
        j0 = run(lambda u, *a: jnp.concatenate([u, rounded_sum(*a)[None]]), u0, a0_stay, a0_far)
        j0_x, j0_c = swap(j0, "x", "j0_x"), swap(j0, "c", "j0_c")
        done = run(
            lambda *v: finish(1, place, v[:4], v[4:]),
            *(j1, j1_c, j1_x, j1_xc, d1, d1_c, d1_x, d1_xc),
        )
        (j0_x,) = run.hold(j0_x)
        j0_xc = swap(j0_x, "c", "j0_xc")
        matrix_grads = run(
            lambda *v: finish(0, place, v[:4], v[4:8], *v[8:]),
            *(j0, j0_c, j0_x, j0_xc, d0, d0_c, d0_x, d0_xc, *done),
        )
    else:
        flats, smalls = [None] * LAYERS, [None] * LAYERS
        for layer in reversed(range(LAYERS)):
            *send, keep = down_at(layer)(rounded)
            got = swaps(send, "c", "down")
            got = jnp.stack([jnp.stack(got[4:]), jnp.stack(got[:4])])
            down_grad = moves.plain_halves_back(rounded_sum(keep, got))
            *send, shift_send, before = wide_first(layer)(rounded)
            passed, keep, shift_keep, grad, rounded, wide_small = wide_last(layer)(
                rounded, before, grad, *swaps(send, "c", "up")
            )
            up_grad = moves.plain_quarters_back(passed, keep)
            middle_rounded = rounded
            *send, pre, rights, grad, rounded, mix_small = mix_first(layer)(rounded, grad)
            got = swaps(send, "c", "attn")
            passed, keep = mix_last(pre, saved[layer][3], rights, middle_rounded, *got)
            attn_grad = moves.plain_quarters_back(passed[:, :, None], keep[:, :, None])
            flats[layer] = (attn_grad, up_grad, down_grad)
            smalls[layer] = (shift_send, shift_keep, wide_small, mix_small)
        summed = moves.sum_all(packed_small(head_small, *smalls[0], *smalls[1]))
        matrix_grads = [jnp.stack(pair) for pair in zip(*flats)]

    gains_grad, biases_grad, shifts_grad = [], [], []
    for layer in range(LAYERS):
        base = 40 + 24 * layer
        shifts_grad.append(summed[base : base + 8].reshape(FF))
        wide_sums = summed[base + 8 : base + 16]
        mix_sums = summed[base + 16 : base + 24]
        gains_grad.append(jnp.stack([mix_sums[0], wide_sums[0]]))
        biases_grad.append(
            jnp.stack([mix_sums[1], wide_sums[1], mix_sums[2], mix_sums[3], wide_sums[2], wide_sums[3]])
        )
    totals = summed[35]
    return (
        activations,
        grad,
        *matrix_grads,
        jnp.stack(gains_grad),
        jnp.stack(biases_grad),
        jnp.stack(shifts_grad),
        summed[:VOCAB].T,
        summed[32],
        summed[33],
        summed[34, :VOCAB],
        totals[0] / totals[2],
        totals[1] / totals[2],
        totals[2].astype(jnp.int32),
    )


def solution(mesh):
    fsdp, dp = mesh.shape["fsdp"], mesh.shape["dp"]
    fine = Mesh(mesh.devices.reshape(fsdp // 2, 2, dp // 2, 2), ("z", "y", "x", "c"))
    tokens = ("z", "y", "x", "c")
    flat = P(None, ("z", "y"), None)
    placed = (P(tokens, None), P(tokens), P(tokens), P(tokens), flat, flat, flat) + (P(),) * 7

    def run(*arrays):
        return local(fsdp, *arrays)

    return jax.shard_map(
        run,
        mesh=fine,
        in_specs=placed,
        out_specs=(P(tokens, None), P(tokens, None), flat, flat, flat) + (P(),) * 10,
        check_vma=False,
    )
```

```python
import math

import jax
import jax.numpy as jnp
from jax import lax
from jax.experimental import pallas as pl
from jax.experimental.pallas import tpu as pltpu
from jax.sharding import Mesh
from jax.sharding import PartitionSpec as P

D = 640
HEADS = 20
HEAD_DIM = 32
FF = 5120
VOCAB = 25
LAYERS = 2
LEN = 128
SEQ_DEV = 4
ROWS = SEQ_DEV * LEN
TILE = 640
TILES = FF // TILE
WIDE = 2 * TILE
STEPS = FF // WIDE
GROUPS = HEADS * HEAD_DIM // 128
PER_GROUP = 128 // HEAD_DIM
CHUNK = 128
CHUNKS = ROWS // CHUNK
SHARD = D // 8
HALF = TILE // 2
BF = jnp.bfloat16
F32 = jnp.float32
MIB = 2**20

SMEM_SPEC = pl.BlockSpec(memory_space=pltpu.SMEM)
ANY_SPEC = pl.BlockSpec(memory_space=pl.ANY)
KERNEL = dict(
    compiler_params=pltpu.CompilerParams(vmem_limit_bytes=60 * MIB),
    cost_estimate=pl.CostEstimate(flops=4 * 10**8, bytes_accessed=2 * MIB, transcendentals=0),
)


def dot(left, right, dims):
    return lax.dot_general(left, right, (dims, ((), ())), preferred_element_type=F32)


def mul_nn(left, right):
    return dot(left, right, ((1,), (0,)))


def mul_nt(left, right):
    return dot(left, right, ((1,), (1,)))


def mul_tn(left, right):
    return dot(left, right, ((0,), (0,)))


def normalize(values):
    centered = values - jnp.mean(values, -1, keepdims=True)
    inverse = lax.rsqrt(jnp.mean(centered * centered, -1, keepdims=True) + 1e-05)
    return (centered * inverse, inverse)


def norm_back(grad_normed, normed, inverse):
    return inverse * (
        grad_normed
        - jnp.mean(grad_normed, -1, keepdims=True)
        - normed * jnp.mean(grad_normed * normed, -1, keepdims=True)
    )


def col_sum(values):
    return jnp.sum(values, 0, keepdims=True)


def sds(shape, dtype):
    return jax.ShapeDtypeStruct(shape, dtype)


def whole_block(shape):
    zeros = (0,) * len(shape)
    return pl.BlockSpec(shape, lambda *_: zeros)


def semaphores(*shape):
    return pltpu.SemaphoreType.DMA(shape)


def copy(source, target, semaphore):
    return pltpu.make_async_copy(source, target, semaphore)


def chunk_rows(index):
    return slice(index * CHUNK, (index + 1) * CHUNK)


def over_chunks(body, start):
    def step(index, carry):
        return body(pl.ds(pl.multiple_of(index * CHUNK, CHUNK), CHUNK), carry)

    return lax.fori_loop(0, CHUNKS, step, start)


def quarter_copies(place_ref, buffers, held, sems):
    x_at, y_at, c_at = place_ref[0], place_ref[1], place_ref[2]
    copies = []
    for number, buffer in enumerate(buffers):
        dx, dc, dy = number // 4, number // 2 % 2, number % 2
        quarter = (x_at ^ dx) * 2 + (c_at ^ dc)
        lanes = pl.ds(pl.multiple_of(quarter * D, 128), D)
        copies.append(copy(buffer.at[:, 0], held.at[:, y_at ^ dy, :, lanes], sems.at[number]))
    return copies


def tiles_from(line):
    return line.shape[1] - 2


def square(values):
    return values.reshape(D, values.shape[-1])


def head_masks():
    lanes = lax.broadcasted_iota(jnp.int32, (LEN, 128), 1) // HEAD_DIM
    return [(lanes == member) for member in range(PER_GROUP)]


def stack_heads(values, masks):
    zero = jnp.zeros_like(values)
    return jnp.concatenate([jnp.where(mask, values, zero) for mask in masks], 0)


def unstack_heads(values):
    parts = [
        values[HEAD_DIM * member : HEAD_DIM * (member + 1), LEN * member : LEN * (member + 1)]
        for member in range(PER_GROUP)
    ]
    return jnp.concatenate(parts, 0).T


def scores_of(keys, queries, valid):
    scores = mul_nt(keys, queries) * (1.0 / math.sqrt(HEAD_DIM))
    return jnp.where(valid, scores, -1e30)


def mix_kernel(place_ref, lengths_ref, residual_ref, *refs):
    buffers, refs = refs[:8], refs[8:]
    gains_ref, biases_ref, packed_out, log_ref, mixed_out, middle_out, second_out, *refs = refs
    held, pre, packed, mixed, middles, seconds, sems, out_sems, row_sems = refs
    copies = quarter_copies(place_ref, buffers, held, sems)
    for one in copies:
        one.start()

    def first(rows, carry):
        normed, inverse = normalize(residual_ref[rows, :].astype(F32))
        pre[rows, :] = (normed * gains_ref[0:1, :] + biases_ref[0:1, :]).astype(BF)
        return carry

    over_chunks(first, 0)
    for one in copies:
        one.wait()
    shifts = (biases_ref[2:3, :], 0.0, biases_ref[3:4, :])
    sent = []
    result = mul_nn(pre[...], square(held[:, :, :, : 3 * D]))
    for part in range(3):
        lanes = slice(part * D, (part + 1) * D)
        packed[:, lanes] = (result[:, lanes] + shifts[part]).astype(BF)
        sent.append(copy(packed.at[:, lanes], packed_out.at[:, lanes], out_sems.at[part]))
        sent[-1].start()
    masks = head_masks()
    row_ids = lax.broadcasted_iota(jnp.int32, (LEN, 1), 0)

    def one_sequence(seq, carry):
        rows = pl.ds(pl.multiple_of(seq * LEN, LEN), LEN)
        valid = row_ids < lengths_ref[seq]
        for group in range(GROUPS):
            lanes = slice(group * 128, (group + 1) * 128)
            queries = stack_heads(packed[rows, lanes], masks)
            key_rows = packed[rows, D + group * 128 : D + (group + 1) * 128]
            value_rows = packed[rows, 2 * D + group * 128 : 2 * D + (group + 1) * 128]
            scores = scores_of(key_rows, queries, valid)
            top = jnp.max(scores, 0, keepdims=True)
            expos = jnp.exp(scores - top)
            total = jnp.sum(expos, 0, keepdims=True)
            probs = (expos * (1.0 / total)).astype(BF)
            log_ref[seq * GROUPS + group] = top + jnp.log(total)
            mixed[rows, lanes] = unstack_heads(mul_tn(value_rows, probs)).astype(BF)
        return carry

    lax.fori_loop(0, SEQ_DEV, one_sequence, 0)
    sent.append(copy(mixed, mixed_out, out_sems.at[3]))
    sent[-1].start()
    middles[...] = mul_nn(mixed[...], square(held[:, :, :, 3 * D :])) + biases_ref[4:5, :]
    for index in range(CHUNKS):
        rows = chunk_rows(index)
        middle = middles[rows, :] + residual_ref[rows, :].astype(F32)
        middles[rows, :] = middle
        normed, inverse = normalize(middle)
        seconds[rows, :] = (normed * gains_ref[1:2, :] + biases_ref[1:2, :]).astype(BF)
        sent.append(copy(middles.at[rows, :], middle_out.at[rows, :], row_sems.at[index, 0]))
        sent[-1].start()
        sent.append(copy(seconds.at[rows, :], second_out.at[rows, :], row_sems.at[index, 1]))
        sent[-1].start()
    for one in sent:
        one.wait()


def mix(place, lengths, residual, quarters, gains, biases):
    logs = (SEQ_DEV * GROUPS, 1, PER_GROUP * LEN)
    return pl.pallas_call(
        mix_kernel,
        grid=(1,),
        out_shape=(
            sds((ROWS, 3 * D), BF),
            sds(logs, F32),
            sds((ROWS, D), BF),
            sds((ROWS, D), F32),
            sds((ROWS, D), BF),
        ),
        in_specs=[SMEM_SPEC, SMEM_SPEC, whole_block((ROWS, D))]
        + [ANY_SPEC] * 8
        + [whole_block((2, D)), whole_block((6, D))],
        out_specs=(ANY_SPEC, whole_block(logs), ANY_SPEC, ANY_SPEC, ANY_SPEC),
        scratch_shapes=[
            pltpu.VMEM((4, 2, SHARD, 4 * D), BF),
            pltpu.VMEM((ROWS, D), BF),
            pltpu.VMEM((ROWS, 3 * D), BF),
            pltpu.VMEM((ROWS, D), BF),
            pltpu.VMEM((ROWS, D), F32),
            pltpu.VMEM((ROWS, D), BF),
            semaphores(8),
            semaphores(4),
            semaphores(CHUNKS, 2),
        ],
        **KERNEL,
    )(place, lengths, residual, *quarters, gains, biases)


def up_kernel(place_ref, second_ref, *refs):
    buffers, refs = refs[:8], refs[8:]
    shift_ref, active_out, slope_out, held, actives, slopes, sems, out_sems = refs
    step = pl.program_id(0)

    @pl.when(step == 0)
    def _():
        for number, buffer in enumerate(buffers):
            dx, dc, dy = number // 4, number // 2 % 2, number % 2
            at = (place_ref[0] ^ dx) * 2 + (place_ref[2] ^ dc)
            for half in range(2):
                target = held.at[at, :, place_ref[1] ^ dy, :, half * TILE : (half + 1) * TILE]
                copy(buffer.at[:, tiles_from(buffer) + half], target, sems.at[at, dy, half]).start()

    for dy in range(2):
        for half in range(2):
            target = held.at[step, :, dy, :, half * TILE : (half + 1) * TILE]
            copy(buffers[0].at[:, 0], target, sems.at[step, dy, half]).wait()
    up_tile = square(held[step])
    shift = shift_ref[pl.ds(step, 1), :]
    for index in range(2):
        rows = slice(index * 2 * CHUNK, (index + 1) * 2 * CHUNK)
        hidden = mul_nn(second_ref[rows, :], up_tile) + shift
        phi = 0.5 + 0.5 * lax.erf(hidden * math.sqrt(0.5))
        density = jnp.exp(hidden * hidden * -0.5) * (1.0 / math.sqrt(2.0 * math.pi))
        actives[step, rows, :] = (hidden * phi).astype(BF)
        slopes[step, rows, :] = (phi + hidden * density).astype(BF)
    copy(actives.at[step], active_out.at[step], out_sems.at[step, 0]).start()
    copy(slopes.at[step], slope_out.at[step], out_sems.at[step, 1]).start()

    @pl.when(step == STEPS - 1)
    def _():
        for at in range(STEPS):
            copy(actives.at[at], active_out.at[at], out_sems.at[at, 0]).wait()
            copy(slopes.at[at], slope_out.at[at], out_sems.at[at, 1]).wait()


def up(place, second, parts, shift):
    out = sds((STEPS, ROWS, WIDE), BF)
    return pl.pallas_call(
        up_kernel,
        grid=(STEPS,),
        out_shape=(out, out),
        in_specs=[SMEM_SPEC, whole_block((ROWS, D))]
        + [ANY_SPEC] * 8
        + [whole_block((STEPS, WIDE))],
        out_specs=(ANY_SPEC, ANY_SPEC),
        scratch_shapes=[
            pltpu.VMEM((STEPS, 4, 2, SHARD, WIDE), BF),
            pltpu.VMEM((STEPS, ROWS, WIDE), BF),
            pltpu.VMEM((STEPS, ROWS, WIDE), BF),
            semaphores(STEPS, 2, 2),
            semaphores(STEPS, 2),
        ],
        **KERNEL,
    )(place, second, *parts, shift)


def down_kernel(place_ref, middle_ref, active_ref, *refs):
    buffers, (biases_ref, out_ref, held, rows, sems, row_sems) = refs[:8], refs[8:]
    step = pl.program_id(0)

    @pl.when(step == 0)
    def _():
        for z_at in range(4):
            for number in range(4):
                dc, dy = number // 2, number % 2
                y_at, c_at = place_ref[1] ^ dy, place_ref[2] ^ dc
                buffer = buffers[dc * 4 + dy * 2 + z_at // 2].at[z_at % 2]
                copy(buffer, held.at[z_at, y_at, c_at], sems.at[z_at, y_at, c_at]).start()
            copy(active_ref.at[z_at], rows.at[z_at], row_sems.at[z_at]).start()
        out_ref[...] = middle_ref[...] + biases_ref[5:6, :]

    for y_at in range(2):
        for c_at in range(2):
            copy(buffers[0].at[0], held.at[step, y_at, c_at], sems.at[step, y_at, c_at]).wait()
    copy(active_ref.at[0], rows.at[step], row_sems.at[step]).wait()
    out_ref[...] += mul_nn(rows[step], held[step].reshape(WIDE, D))


def down(place, middle, active, parts, biases):
    return pl.pallas_call(
        down_kernel,
        grid=(STEPS,),
        out_shape=sds((ROWS, D), F32),
        in_specs=[SMEM_SPEC, whole_block((ROWS, D))] + [ANY_SPEC] * 9 + [whole_block((6, D))],
        out_specs=whole_block((ROWS, D)),
        scratch_shapes=[
            pltpu.VMEM((4, 2, 2, HALF, D), BF),
            pltpu.VMEM((STEPS, ROWS, WIDE), BF),
            semaphores(4, 2, 2),
            semaphores(STEPS),
        ],
        **KERNEL,
    )(place, middle, active, *parts, biases)


def head_kernel(
    residual_ref,
    targets_ref,
    masked_ref,
    weight_ref,
    shift_ref,
    gain_ref,
    move_ref,
    activations_ref,
    grad_ref,
    rounded_ref,
    small_ref,
):
    small_ref[...] = jnp.zeros_like(small_ref)
    lanes = lax.broadcasted_iota(jnp.int32, (1, 128), 1)

    def body(rows, carry):
        weight_grad, gain_grad, move_grad, shift_grad, stats = carry
        residual = residual_ref[rows, :]
        activations_ref[rows, :] = residual.astype(BF)
        normed, inverse = normalize(residual)
        final = (normed * gain_ref[...] + move_ref[...]).astype(BF)
        logits = mul_nn(final, weight_ref[...]) + shift_ref[...]
        top = jnp.max(logits, -1, keepdims=True)
        log_total = top + jnp.log(jnp.sum(jnp.exp(logits - top), -1, keepdims=True))
        onehot = (targets_ref[rows, :] == lanes).astype(F32)
        picked = jnp.sum(logits * onehot, -1, keepdims=True)
        mask = masked_ref[rows, :].astype(F32)
        loss = col_sum(mask * (log_total - picked))
        hits = col_sum(mask * jnp.exp(picked - log_total))
        count = col_sum(mask)
        stats = stats + (
            jnp.where(lanes == 0, loss, 0.0)
            + jnp.where(lanes == 1, hits, 0.0)
            + jnp.where(lanes == 2, count, 0.0)
        )
        grad_logits = (mask * (jnp.exp(logits - log_total) - onehot)).astype(BF)
        weight_grad = weight_grad + mul_tn(grad_logits, final)
        shift_grad = shift_grad + col_sum(grad_logits.astype(F32))
        grad_final = mul_nt(grad_logits, weight_ref[...])
        gain_grad = gain_grad + col_sum(grad_final * normed)
        move_grad = move_grad + col_sum(grad_final)
        grad = norm_back(grad_final * gain_ref[...], normed, inverse)
        grad_ref[rows, :] = grad
        rounded_ref[rows, :] = grad.astype(BF)
        return weight_grad, gain_grad, move_grad, shift_grad, stats

    row = jnp.zeros((1, D), F32)
    narrow = jnp.zeros((1, 128), F32)
    weight_grad, gain_grad, move_grad, shift_grad, stats = over_chunks(
        body, (jnp.zeros((128, D), F32), row, row, narrow, narrow)
    )
    small_ref[0:32, :] = weight_grad[0:32, :]
    small_ref[32:33, :] = gain_grad
    small_ref[33:34, :] = move_grad
    small_ref[34:35, 0:128] = shift_grad
    small_ref[35:36, 0:128] = stats


def head(residual, targets, masked, weight, shift, gain, move):
    full = whole_block((ROWS, D))
    return pl.pallas_call(
        head_kernel,
        out_shape=(
            sds((ROWS, D), BF),
            sds((ROWS, D), F32),
            sds((ROWS, D), BF),
            sds((40, D), F32),
        ),
        grid=(1,),
        in_specs=[full, whole_block((ROWS, 1)), whole_block((ROWS, 1)), whole_block((D, 128))]
        + [whole_block((1, 128)), whole_block((1, D)), whole_block((1, D))],
        out_specs=(full, full, full, whole_block((40, D))),
        **KERNEL,
    )(residual, targets, masked, weight, shift, gain, move)


def down_back_kernel(place_ref, grad_ref, active_ref, *refs):
    sends, (keep_out, held, grads, sems, out_sems) = refs[:8], refs[8:]
    step = pl.program_id(0)
    c_at = place_ref[2]

    @pl.when(step == 0)
    def _():
        for at in range(TILES):
            z_at, y_at = at % 4, place_ref[1] ^ (1 - at // 4)
            source = active_ref.at[z_at, :, pl.ds(pl.multiple_of(y_at * TILE, 128), TILE)]
            target = held.at[at // 2, :, at % 2 * TILE : (at % 2 + 1) * TILE]
            copy(source, target, sems.at[at]).start()

    for part in range(2):
        target = held.at[step, :, part * TILE : (part + 1) * TILE]
        copy(active_ref.at[0, :, :TILE], target, sems.at[2 * step + part]).wait()
    grads[step] = mul_tn(grad_ref[...], held[step]).astype(BF).reshape(2, HALF, WIDE)
    for at in range(TILES):

        @pl.when(step == at // 2)
        def _():
            lanes = slice(at % 2 * TILE, (at % 2 + 1) * TILE)
            copy(grads.at[at // 2, 1 - c_at, :, lanes], sends[at], out_sems.at[at, 0]).start()
            kept = grads.at[at // 2, c_at, :, lanes]
            copy(kept, keep_out.at[1 - at // 4, at % 4], out_sems.at[at, 1]).start()

    @pl.when(step == STEPS - 1)
    def _():
        for at in range(TILES):
            one = grads.at[0, 0, :, :TILE]
            copy(one, sends[at], out_sems.at[at, 0]).wait()
            copy(one, keep_out.at[0, 0], out_sems.at[at, 1]).wait()


def down_back(place, grad, active):
    part = sds((HALF, TILE), BF)
    return pl.pallas_call(
        down_back_kernel,
        grid=(STEPS,),
        in_specs=[SMEM_SPEC, whole_block((ROWS, D)), ANY_SPEC],
        out_specs=(ANY_SPEC,) * 9,
        out_shape=(part,) * 8 + (sds((2, 4, HALF, TILE), BF),),
        scratch_shapes=[
            pltpu.VMEM((STEPS, ROWS, WIDE), BF),
            pltpu.VMEM((STEPS, 2, HALF, WIDE), BF),
            semaphores(TILES),
            semaphores(TILES, 2),
        ],
        **KERNEL,
    )(place, grad, active)


def down_sum_kernel(side, others, keep_ref, *refs):
    parts, refs = refs[:4], refs[4:]
    other_refs, refs = refs[:others], refs[others:]
    out_ref, kept, got, other, total, sems, other_sems, out_sems = refs
    copies = []
    for at in range(4):
        copies.append(
            [
                copy(keep_ref.at[side, at], kept.at[at], sems.at[at, 0]),
                copy(parts[at], got.at[at], sems.at[at, 1]),
            ]
            + [copy(ref.at[at], other.at[at], other_sems.at[at]) for ref in other_refs]
        )
        for one in copies[-1]:
            one.start()
    for at in range(4):
        for one in copies[at]:
            one.wait()
        value = kept[at].astype(F32) + got[at].astype(F32)
        if others:
            value = value + other[at].astype(F32)
        total[at] = value.astype(BF)
        copy(total.at[at], out_ref.at[at], out_sems.at[at]).start()
    for at in range(4):
        copy(total.at[at], out_ref.at[at], out_sems.at[at]).wait()


def down_sum(side, keep, parts, *other):
    shape = (4, HALF, TILE)

    def kernel(*refs):
        down_sum_kernel(side, len(other), *refs)

    return pl.pallas_call(
        kernel,
        grid=(1,),
        in_specs=[ANY_SPEC] * (5 + len(other)),
        out_specs=ANY_SPEC,
        out_shape=sds(shape, BF),
        scratch_shapes=[pltpu.VMEM(shape, BF)] * 4
        + [semaphores(4, 2), semaphores(4), semaphores(4)],
        **KERNEL,
    )(keep, *parts, *other)


def wide_back_start(phase, place_ref, slope_ref, ups, downs, held, sems):
    x_at, y_at, c_at = place_ref[0], place_ref[1], place_ref[2]
    held_up, held_down, slopes = held
    up_sems, down_sems, slope_sems = sems
    for step in range(2):
        dx = 1 - step
        for number, buffer in enumerate(downs):
            dc, dy, z_high = number // 4, number // 2 % 2, number % 2

            @pl.when(x_at ^ dx == z_high)
            def _():
                y_to, c_to = y_at ^ dy, c_at ^ dc
                target = held_down.at[step, y_to, c_to]
                source = buffer.at[c_at ^ (1 - phase)]
                copy(source, target, down_sems.at[step, y_to, c_to]).start()

        quarter = (x_at ^ dx) * 2 + (c_at ^ (1 - phase))
        copy(slope_ref.at[quarter], slopes.at[step], slope_sems.at[step]).start()
        for dy in range(2):
            for half in range(2):
                target = held_up.at[step, :, y_at ^ dy, :, half * TILE : (half + 1) * TILE]
                source = ups[2 * dx + dy].at[:, tiles_from(ups[0]) + half]
                copy(source, target, up_sems.at[step, dy, half]).start()


def wide_back_step(step, rounded_ref, second_ref, slope_ref, ups, downs, held, sems, shift_ref, total):
    held_up, held_down, slopes = held
    up_sems, down_sems, slope_sems = sems
    for y_at in range(2):
        for c_at in range(2):
            target = held_down.at[step, y_at, c_at]
            copy(downs[0].at[0], target, down_sems.at[step, y_at, c_at]).wait()
    grad_active = mul_nt(rounded_ref[...], held_down[step].reshape(WIDE, D))
    copy(slope_ref.at[0], slopes.at[step], slope_sems.at[step]).wait()
    grad_hidden = (grad_active * slopes[step].astype(F32)).astype(BF)
    shift_ref[pl.ds(step, 1), :] = col_sum(grad_hidden.astype(F32))
    for dy in range(2):
        for half in range(2):
            target = held_up.at[step, :, dy, :, half * TILE : (half + 1) * TILE]
            copy(ups[0].at[:, 0], target, up_sems.at[step, dy, half]).wait()
    total[...] += mul_nt(grad_hidden, square(held_up[step]))
    return mul_tn(second_ref[...], grad_hidden).reshape(4, 2, SHARD, WIDE)


def wide_back_scratch():
    return [
        pltpu.VMEM((2, 4, 2, SHARD, WIDE), BF),
        pltpu.VMEM((2, 2, 2, HALF, D), BF),
        pltpu.VMEM((2, ROWS, WIDE), BF),
        semaphores(2, 2, 2),
        semaphores(2, 2, 2),
        semaphores(2),
    ]


def wide_back_first_kernel(place_ref, rounded_ref, second_ref, slope_ref, *refs):
    ups, downs, refs = refs[:4], refs[4:12], refs[12:]
    sends, (shift_ref, total_ref, *refs) = refs[:8], refs[8:]
    held, sems, sent, out_sems = refs[:3], refs[3:6], refs[6], refs[7]
    step = pl.program_id(0)

    @pl.when(step == 0)
    def _():
        wide_back_start(0, place_ref, slope_ref, ups, downs, held, sems)
        total_ref[...] = jnp.zeros_like(total_ref)

    up_grad = wide_back_step(
        step, rounded_ref, second_ref, slope_ref, ups, downs, held, sems, shift_ref, total_ref
    )
    for side in range(2):
        sent[step, side ^ place_ref[1]] = up_grad[:, side].astype(BF)

    def out_copy(at, half, dy):
        lanes = slice(half * TILE, (half + 1) * TILE)
        number = 4 * at + 2 * half + dy
        return copy(sent.at[at, dy, :, :, lanes], sends[number], out_sems.at[at, half, dy])

    pieces = [(half, dy) for half in range(2) for dy in range(2)]
    for at in range(2):

        @pl.when(step == at)
        def _():
            for half, dy in pieces:
                out_copy(at, half, dy).start()

    @pl.when(step == 1)
    def _():
        for at in range(2):
            for half, dy in pieces:
                out_copy(at, half, dy).wait()


def wide_back_first(place, rounded, second, slope, up_parts, down_parts):
    full = whole_block((ROWS, D))
    return pl.pallas_call(
        wide_back_first_kernel,
        grid=(2,),
        in_specs=[SMEM_SPEC, full, full] + [ANY_SPEC] * 13,
        out_specs=(ANY_SPEC,) * 8 + (whole_block((2, WIDE)), full),
        out_shape=(sds((4, SHARD, TILE), BF),) * 8 + (sds((2, WIDE), F32), sds((ROWS, D), F32)),
        scratch_shapes=wide_back_scratch()
        + [pltpu.VMEM((2, 2, 4, SHARD, WIDE), BF), semaphores(2, 2, 2)],
        **KERNEL,
    )(place, rounded, second, slope, *up_parts[2:4], *up_parts[6:8], *down_parts)


def wide_back_last_kernel(place_ref, rounded_ref, second_ref, slope_ref, *refs):
    ups, downs, refs = refs[:4], refs[4:12], refs[12:]
    before_ref, grad_ref, middle_ref, gains_ref, *refs = refs
    gots, refs = refs[:8], refs[8:]
    outs, (shift_ref, grad_out, rounded_out, small_ref, *refs) = refs[:2], refs[2:]
    held, sems, refs = refs[:3], refs[3:6], refs[6:]
    kept, got, total, grads, middles, roundeds, got_sems, out_sems, in_sems, row_sems = refs
    step = pl.program_id(0)
    fetched = (
        copy(before_ref, total, in_sems.at[0]),
        copy(grad_ref, grads, in_sems.at[1]),
        copy(middle_ref, middles, in_sems.at[2]),
    )

    pieces = [(half, dy) for half in range(2) for dy in range(2)]

    def got_copy(at, half, dy):
        lanes = slice(half * TILE, (half + 1) * TILE)
        target = got.at[at, dy, :, :, lanes]
        return copy(gots[4 * at + 2 * half + dy], target, got_sems.at[at, half, dy])

    @pl.when(step == 0)
    def _():
        fetched[0].start()
        wide_back_start(1, place_ref, slope_ref, ups, downs, held, sems)
        for at in range(2):
            for half, dy in pieces:
                got_copy(at, half, dy).start()
        fetched[1].start()
        fetched[2].start()
        fetched[0].wait()

    up_grad = wide_back_step(
        step, rounded_ref, second_ref, slope_ref, ups, downs, held, sems, shift_ref, total
    )
    for half, dy in pieces:
        lanes = slice(half * TILE, (half + 1) * TILE)
        copy(gots[0], got.at[step, dy, :, :, lanes], got_sems.at[step, half, dy]).wait()
    for side in range(2):
        at_side = side ^ place_ref[1]
        kept[step, at_side] = (up_grad[:, side] + got[step, at_side].astype(F32)).astype(BF)

    def out_copy(at, half, dy):
        lanes = slice(half * TILE, (half + 1) * TILE)
        target = outs[at].at[dy, :, half]
        return copy(kept.at[at, dy, :, :, lanes], target, out_sems.at[at, half, dy])

    for at in range(2):

        @pl.when(step == at)
        def _():
            for half, dy in pieces:
                out_copy(at, half, dy).start()

    @pl.when(step == 1)
    def _():
        fetched[1].wait()
        fetched[2].wait()
        sums = [jnp.zeros((1, D), F32)] * 4
        sent = []
        for index in range(CHUNKS):
            rows = chunk_rows(index)
            normed, inverse = normalize(middles[rows, :])
            grad_second = total[rows, :]
            grad = grads[rows, :] + norm_back(grad_second * gains_ref[1:2, :], normed, inverse)
            rounded = grad.astype(BF)
            grads[rows, :] = grad
            roundeds[rows, :] = rounded
            sent.append(copy(grads.at[rows, :], grad_out.at[rows, :], row_sems.at[index, 0]))
            sent.append(copy(roundeds.at[rows, :], rounded_out.at[rows, :], row_sems.at[index, 1]))
            sent[-2].start()
            sent[-1].start()
            terms = (
                grad_second * normed,
                grad_second,
                rounded.astype(F32),
                rounded_ref[rows, :].astype(F32),
            )
            sums = [old + col_sum(term) for old, term in zip(sums, terms)]
        small_ref[...] = jnp.zeros_like(small_ref)
        for number in range(4):
            small_ref[number : number + 1, :] = sums[number]
        for at in range(2):
            for half, dy in pieces:
                out_copy(at, half, dy).wait()
        for one in sent:
            one.wait()


def wide_back_last(
    place, rounded, second, slope, up_parts, down_parts, before, grad, middle, gains, *got
):
    full = whole_block((ROWS, D))
    out = sds((2, 4, 2, SHARD, TILE), BF)
    return pl.pallas_call(
        wide_back_last_kernel,
        grid=(2,),
        in_specs=[SMEM_SPEC, full, full]
        + [ANY_SPEC] * 16
        + [whole_block((2, D))]
        + [ANY_SPEC] * 8,
        out_specs=(ANY_SPEC, ANY_SPEC, whole_block((2, WIDE)), ANY_SPEC, ANY_SPEC, whole_block((8, D))),
        out_shape=(
            out,
            out,
            sds((2, WIDE), F32),
            sds((ROWS, D), F32),
            sds((ROWS, D), BF),
            sds((8, D), F32),
        ),
        scratch_shapes=wide_back_scratch()
        + [
            pltpu.VMEM((2, 2, 4, SHARD, WIDE), BF),
            pltpu.VMEM((2, 2, 4, SHARD, WIDE), BF),
            pltpu.VMEM((ROWS, D), F32),
            pltpu.VMEM((ROWS, D), F32),
            pltpu.VMEM((ROWS, D), F32),
            pltpu.VMEM((ROWS, D), BF),
            semaphores(2, 2, 2),
            semaphores(2, 2, 2),
            semaphores(3),
            semaphores(CHUNKS, 2),
        ],
        **KERNEL,
    )(
        place, rounded, second, slope, *up_parts[0:2], *up_parts[4:6], *down_parts,
        before, grad, middle, gains, *got
    )


def mix_back_kernel(place_ref, lengths_ref, rounded_ref, grad_ref, residual_ref, *refs):
    buffers, (packed_ref, log_ref, mixed_ref, gains_ref, biases_ref, *refs) = refs[:8], refs[8:]
    sends, (pre_out, rights_out, grad_out, rounded_out, small_ref, *refs) = refs[:4], refs[4:]
    held, packed, sent, pre, rights, grad_mixed, total, grads, roundeds, *refs = refs
    sems, in_sems, send_sems, pre_sem, right_sems, row_sems = refs
    x_at, y_at, c_at = place_ref[0], place_ref[1], place_ref[2]
    copies = quarter_copies(place_ref, buffers, held, sems)
    for one in copies:
        one.start()
    fetched = [
        copy(packed_ref.at[chunk_rows(at), :], packed.at[chunk_rows(at), :], in_sems.at[at])
        for at in range(SEQ_DEV)
    ]
    fetched.append(copy(grad_ref, grads, in_sems.at[SEQ_DEV]))
    for one in fetched:
        one.start()

    def send_grad(part, right):
        @pl.when(c_at ^ (part & 1) == 1)
        def _():
            left = mixed_ref[...] if part == 3 else pre[...]
            value = mul_tn(left, right).astype(BF).reshape(4, 2, SHARD, D)
            for side in range(2):
                sent[x_at ^ (part >> 1), side ^ y_at] = value[:, side]

    send_grad(3, rounded_ref[...])

    def first(rows, carry):
        normed, inverse = normalize(residual_ref[rows, :].astype(F32))
        pre[rows, :] = (normed * gains_ref[0:1, :] + biases_ref[0:1, :]).astype(BF)
        return carry

    over_chunks(first, 0)
    pre_copy = copy(pre, pre_out, pre_sem.at[0])
    pre_copy.start()
    for one in copies:
        one.wait()
    grad_mixed[...] = mul_nt(rounded_ref[...], square(held[:, :, :, 3 * D :])).astype(BF)
    masks = head_masks()
    row_ids = lax.broadcasted_iota(jnp.int32, (LEN, 1), 0)
    scale = 1.0 / math.sqrt(HEAD_DIM)

    def right_copy(seq, part):
        rows = pl.ds(pl.multiple_of(seq * LEN, LEN), LEN)
        lanes = slice(part * D, (part + 1) * D)
        return copy(rights.at[rows, lanes], rights_out.at[part, rows, :], right_sems.at[seq, part])

    def one_sequence(seq, carry):
        rows = pl.ds(pl.multiple_of(seq * LEN, LEN), LEN)
        copy(packed_ref.at[chunk_rows(0), :], packed.at[rows, :], in_sems.at[seq]).wait()
        valid = row_ids < lengths_ref[seq]
        for group in range(GROUPS):
            at_query = slice(group * 128, (group + 1) * 128)
            queries = stack_heads(packed[rows, at_query], masks)
            key_rows = packed[rows, D + group * 128 : D + (group + 1) * 128]
            value_rows = packed[rows, 2 * D + group * 128 : 2 * D + (group + 1) * 128]
            mixed_grads = stack_heads(grad_mixed[rows, at_query], masks)
            scores = scores_of(key_rows, queries, valid)
            probs = jnp.exp(scores - log_ref[seq * GROUPS + group])
            grad_probs = mul_nt(value_rows, mixed_grads)
            inner = jnp.sum(grad_probs * probs, 0, keepdims=True)
            grad_scores = (probs * (grad_probs - inner)).astype(BF)
            rights[rows, 2 * D + group * 128 : 2 * D + (group + 1) * 128] = mul_nn(probs.astype(BF), mixed_grads).astype(BF)
            rights[rows, D + group * 128 : D + (group + 1) * 128] = (mul_nn(grad_scores, queries) * scale).astype(BF)
            grad_queries = unstack_heads(mul_tn(key_rows, grad_scores))
            rights[rows, at_query] = (grad_queries * scale).astype(BF)
        for part in range(3):
            right_copy(seq, part).start()
        return carry

    lax.fori_loop(0, SEQ_DEV, one_sequence, 0)
    for part in range(3):
        send_grad(part, rights[:, part * D : (part + 1) * D])
    for dx in range(2):
        for dy in range(2):
            copy(sent.at[dx, dy], sends[2 * dx + dy], send_sems.at[dx, dy]).start()
    total[...] = mul_nt(rights[...], square(held[:, :, :, : 3 * D]))
    fetched[-1].wait()
    sums = [jnp.zeros((1, D), F32)] * 4
    out_copies = []
    for index in range(CHUNKS):
        rows = chunk_rows(index)
        normed, inverse = normalize(residual_ref[rows, :].astype(F32))
        grad_pre = total[rows, :]
        grad = grads[rows, :] + norm_back(grad_pre * gains_ref[0:1, :], normed, inverse)
        grads[rows, :] = grad
        roundeds[rows, :] = grad.astype(BF)
        out_copies.append(copy(grads.at[rows, :], grad_out.at[rows, :], row_sems.at[index, 0]))
        out_copies.append(copy(roundeds.at[rows, :], rounded_out.at[rows, :], row_sems.at[index, 1]))
        out_copies[-2].start()
        out_copies[-1].start()
        terms = (
            grad_pre * normed,
            grad_pre,
            rights[rows, 0:D].astype(F32),
            rights[rows, 2 * D : 3 * D].astype(F32),
        )
        sums = [old + col_sum(term) for old, term in zip(sums, terms)]
    small_ref[...] = jnp.zeros_like(small_ref)
    for number in range(4):
        small_ref[number : number + 1, :] = sums[number]
    for seq in range(SEQ_DEV):
        for part in range(3):
            right_copy(seq, part).wait()
    for dx in range(2):
        for dy in range(2):
            copy(sent.at[dx, dy], sends[2 * dx + dy], send_sems.at[dx, dy]).wait()
    for one in [pre_copy] + out_copies:
        one.wait()


def mix_back(
    place, lengths, rounded, middle_grad, residual, quarters, packed, logs, mixed, gains, biases
):
    part = sds((4, SHARD, D), BF)
    full = whole_block((ROWS, D))
    return pl.pallas_call(
        mix_back_kernel,
        out_shape=(part,) * 4
        + (
            sds((ROWS, D), BF),
            sds((3, ROWS, D), BF),
            sds((ROWS, D), F32),
            sds((ROWS, D), BF),
            sds((8, D), F32),
        ),
        grid=(1,),
        in_specs=[SMEM_SPEC, SMEM_SPEC, full, ANY_SPEC, full]
        + [ANY_SPEC] * 9
        + [whole_block((SEQ_DEV * GROUPS, 1, PER_GROUP * LEN)), full]
        + [whole_block((2, D)), whole_block((6, D))],
        out_specs=(ANY_SPEC,) * 8 + (whole_block((8, D)),),
        scratch_shapes=[
            pltpu.VMEM((4, 2, SHARD, 4 * D), BF),
            pltpu.VMEM((ROWS, 3 * D), BF),
            pltpu.VMEM((2, 2, 4, SHARD, D), BF),
            pltpu.VMEM((ROWS, D), BF),
            pltpu.VMEM((ROWS, 3 * D), BF),
            pltpu.VMEM((ROWS, D), BF),
            pltpu.VMEM((ROWS, D), F32),
            pltpu.VMEM((ROWS, D), F32),
            pltpu.VMEM((ROWS, D), BF),
            semaphores(8),
            semaphores(SEQ_DEV + 1),
            semaphores(2, 2),
            semaphores(1),
            semaphores(SEQ_DEV, 3),
            semaphores(CHUNKS, 2),
        ],
        **KERNEL,
    )(
        place, lengths, rounded, middle_grad, residual, *quarters, packed, logs, mixed, gains, biases
    )


def mix_back_last_kernel(place_ref, pre_ref, mixed_ref, rights_ref, rounded_ref, *refs):
    gots, outs, (lefts, rights, got, kept, sems, out_sems) = refs[:4], refs[4:6], refs[6:]
    y_at, c_at = place_ref[1], place_ref[2]
    parts = [(place_ref[0] ^ dx) * 2 + c_at for dx in range(2)]
    for dx in (1, 0):

        @pl.when(parts[dx] == 3)
        def _():
            copy(mixed_ref, lefts.at[dx], sems.at[dx, 3]).start()
            copy(rounded_ref, rights.at[dx], sems.at[dx, 0]).start()

        @pl.when(parts[dx] != 3)
        def _():
            copy(pre_ref, lefts.at[dx], sems.at[dx, 3]).start()
            copy(rights_ref.at[jnp.minimum(parts[dx], 2)], rights.at[dx], sems.at[dx, 0]).start()

        for dy in range(2):
            copy(gots[2 * dx + dy], got.at[dx, dy], sems.at[dx, 1 + dy]).start()
    for dx in (1, 0):
        copy(pre_ref, lefts.at[dx], sems.at[dx, 3]).wait()
        copy(rounded_ref, rights.at[dx], sems.at[dx, 0]).wait()
        value = mul_tn(lefts[dx], rights[dx]).reshape(4, 2, SHARD, D)
        for dy in range(2):
            copy(gots[0], got.at[dx, dy], sems.at[dx, 1 + dy]).wait()
        for side in range(2):
            at = side ^ y_at
            kept[dx, at] = (value[:, side] + got[dx, at].astype(F32)).astype(BF)
        copy(kept.at[dx], outs[1 - dx], out_sems.at[dx]).start()
    for dx in range(2):
        copy(kept.at[dx], outs[1 - dx], out_sems.at[dx]).wait()


def mix_back_last(place, pre, mixed, rights, rounded, *got):
    out = sds((2, 4, SHARD, D), BF)
    return pl.pallas_call(
        mix_back_last_kernel,
        grid=(1,),
        in_specs=[SMEM_SPEC] + [ANY_SPEC] * 8,
        out_specs=(ANY_SPEC,) * 2,
        out_shape=(out, out),
        scratch_shapes=[
            pltpu.VMEM((2, ROWS, D), BF),
            pltpu.VMEM((2, ROWS, D), BF),
            pltpu.VMEM((2, 2, 4, SHARD, D), BF),
            pltpu.VMEM((2, 2, 4, SHARD, D), BF),
            semaphores(2, 4),
            semaphores(2),
        ],
        **KERNEL,
    )(place, pre, mixed, rights, rounded, *got)


def finish_kernel(layer, olds, place_ref, *refs):
    quarters, halves, outs = refs[:4], refs[4:8], refs[8 + olds : 11 + olds]
    attn, ups, downs, sems = refs[11 + olds :]
    x_at, c_at = place_ref[0], place_ref[2]
    values = [ref[...] for ref in quarters]
    pairs = [
        (jnp.where(c_at == 0, own, other), jnp.where(c_at == 0, other, own))
        for own, other in (values[:2], values[2:])
    ]
    ordered = [jnp.where(x_at == 0, own, other) for own, other in zip(*pairs)]
    ordered += [jnp.where(x_at == 0, other, own) for own, other in zip(*pairs)]
    for quarter, value in enumerate(ordered):
        for tile in range(3):
            target, first, stride = (
                (attn, quarter * 5, 20) if tile == 2 else (ups, quarter * 10 + tile * 5, 40)
            )
            for block in range(5):
                target[pl.ds(first + block, SHARD, stride=stride), :] = value[
                    tile, :, block * 128 : (block + 1) * 128
                ].astype(F32)
    copies = [
        copy(target, out.at[layer], sems.at[number])
        for number, (target, out) in enumerate(zip((attn, ups, downs), outs))
    ]
    copies[0].start()
    copies[1].start()
    own, other = (
        halves[at][...].astype(F32) + halves[at + 2][...].astype(F32) for at in range(2)
    )
    turned = jnp.concatenate(
        [jnp.where(c_at == 0, own, other), jnp.where(c_at == 0, other, own)], 0
    ).T
    for block in range(5):
        downs[pl.ds(block, TILE, stride=5), :] = turned[:, block * 128 : (block + 1) * 128]
    copies[2].start()
    for one in copies:
        one.wait()


def finish(layer, place, quarters, halves, *old):
    attn, wide = (D * 4 * D // 8 // 128, 128), (D * FF // 8 // 128, 128)

    def kernel(*refs):
        finish_kernel(layer, len(old), *refs)

    return pl.pallas_call(
        kernel,
        grid=(1,),
        in_specs=[SMEM_SPEC]
        + [whole_block((3, SHARD, D))] * 4
        + [whole_block((HALF, TILE))] * 4
        + [ANY_SPEC] * len(old),
        out_specs=(ANY_SPEC,) * 3,
        out_shape=tuple(sds((LAYERS, *shape), F32) for shape in (attn, wide, wide)),
        scratch_shapes=[pltpu.VMEM(shape, F32) for shape in (attn, wide, wide)] + [semaphores(3)],
        input_output_aliases={9 + number: number for number in range(len(old))},
        **KERNEL,
    )(place, *quarters, *halves, *old)


def swap(value, axis, name):
    with jax.named_scope(name):
        return lax.ppermute(value, axis, [(0, 1), (1, 0)])


def swaps(values, axis, name):
    return [swap(value, axis, name) for value in values]


class Order:
    def __init__(self):
        self.last = None

    def hold(self, *arrays):
        if self.last is not None:
            arrays = lax.optimization_barrier((arrays, self.last))[0]
        return arrays

    def __call__(self, function, *arrays):
        results = function(*self.hold(*arrays))
        self.last = jax.tree.leaves(results)[0]
        return results


def wide_sum(*values):
    total = values[0].astype(F32)
    for value in values[1:]:
        total = total + value.astype(F32)
    return total


def rounded_sum(*values):
    return wide_sum(*values).astype(BF)


def plus(own, other):
    return own + other


class Moves:
    def __init__(self, fsdp):
        self.z_size = fsdp // 2
        self.staged = fsdp == 8
        self.x_at = lax.axis_index("x")
        self.y_at = lax.axis_index("y")
        self.z_at = lax.axis_index("z")
        self.c_at = lax.axis_index("c")
        self.place = jnp.stack([self.x_at, self.y_at, self.c_at]).astype(jnp.int32)

    def hop(self, value, reach, name):
        with jax.named_scope(name):
            return lax.ppermute(value, "z", [(at, at ^ reach) for at in range(self.z_size)])

    def ordered(self, bit, own, other):
        return jnp.where(bit == 0, jnp.stack([own, other]), jnp.stack([other, own]))

    def by_side(self, value):
        value = value.reshape(4, 2, *value.shape[1:]).swapaxes(0, 1)
        return jnp.where(self.y_at == 0, value, value[::-1])

    def by_shard(self, value):
        value = jnp.where(self.y_at == 0, value, value[::-1]).swapaxes(0, 1)
        return value.reshape(8, *value.shape[2:])

    def own_quarter(self, flat):
        shard = flat.reshape(SHARD, -1, 128)
        step = shard.shape[1] // 4
        own = lax.dynamic_slice_in_dim(shard, (self.x_at * 2 + self.c_at) * step, step, 1)
        return own.reshape(SHARD, step // 5, 5, 128).swapaxes(0, 1).reshape(-1, SHARD, D)

    def own_half(self, flat):
        own = lax.dynamic_slice_in_dim(flat, self.c_at * HALF * 5, HALF * 5, 0)
        return own.reshape(1, HALF, D)

    def high(self, own, other):
        return self.ordered(self.z_at // 2, own, other)

    def low(self, pair, other):
        bit = self.z_at % 2
        line = jnp.where(bit == 0, jnp.stack([pair, other], 1), jnp.stack([other, pair], 1))
        return (line.reshape(4, *pair.shape[1:]),)

    def low_halves(self, pair, other):
        line = self.low(pair, other)[0][:, 0]
        return line[:2], line[2:]

    def part_near(self, *parts):
        total = wide_sum(*parts)
        total = total.reshape(2, 2, *total.shape[1:])
        near = self.z_at % 2
        return tuple(
            lax.dynamic_index_in_dim(total, at, 1, False).astype(BF) for at in (1 - near, near)
        )

    def part_far(self, *parts):
        total = wide_sum(*parts)
        far = self.z_at // 2
        return tuple(
            lax.dynamic_index_in_dim(total, at, 0, False).astype(BF) for at in (1 - far, far)
        )

    def along_z(self, part):
        return lax.psum_scatter(part, "z", scatter_dimension=0, tiled=False)

    def plain_quarters(self, flat):
        whole = lax.all_gather(flat, ("z", "y"), axis=0, tiled=True)
        whole = whole.reshape(8, SHARD, 4, -1, D).transpose(2, 0, 3, 1, 4)
        lines = []
        for number in range(4):
            quarter = (self.x_at ^ (number >> 1)) * 2 + (self.c_at ^ (number & 1))
            part = self.by_side(lax.dynamic_index_in_dim(whole, quarter, 0, False))
            lines += [part[dy] for dy in range(2)]
        return lines

    def plain_halves(self, flat):
        whole = lax.all_gather(flat, ("z", "y"), axis=0, tiled=True).reshape(8, 2, HALF, D)
        pairs = []
        for number in range(2):
            part = self.by_side(lax.dynamic_index_in_dim(whole, self.c_at ^ number, 1, False))
            pairs += [part[dy, 2 * at : 2 * at + 2] for dy in range(2) for at in range(2)]
        return pairs

    def plain_quarters_back(self, passed, keep):
        part = self.by_shard(rounded_sum(keep, swap(passed, "x", "quarters")))
        part = part.transpose(0, 2, 1, 3).reshape(D, -1)
        part = lax.psum_scatter(part, ("z", "y"), scatter_dimension=0, tiled=True)
        parts = lax.all_gather(part, ("x", "c"), axis=0, tiled=False)
        return parts.swapaxes(0, 1).astype(F32).reshape(-1, 128)

    def plain_halves_back(self, part):
        part = self.by_shard(part).transpose(0, 2, 1).reshape(FF, HALF)
        part = lax.psum_scatter(part, ("z", "y"), scatter_dimension=0, tiled=True).T
        part = rounded_sum(part, swap(part, "x", "halves"))
        return lax.all_gather(part, "c", axis=0, tiled=True).T.astype(F32).reshape(-1, 128)

    def sum_all(self, value):
        for axis in ("c", "x", "y"):
            value = value + swap(value, axis, "small")
        reach = 1
        while reach < self.z_size:
            value = value + self.hop(value, reach, "small")
            reach *= 2
        return value


def local(
    fsdp,
    inputs,
    targets,
    masked,
    lengths,
    attn_weight,
    up_weight,
    down_weight,
    norm_gains,
    layer_biases,
    up_bias,
    head_weight,
    final_gain,
    final_shift,
    head_bias,
):
    moves = Moves(fsdp)
    place = moves.place
    shifts = up_bias.reshape(LAYERS, STEPS, WIDE)
    run = Order()

    def mix_on(layer):
        return lambda r, *q: mix(place, lengths, r, q, norm_gains[layer], layer_biases[layer])

    def up_on(layer):
        return lambda second, *parts: up(place, second, parts, shifts[layer])

    def down_on(layer):
        return lambda m, active, *parts: down(place, m, active, parts, layer_biases[layer])

    def prepared(targets, masked, head_weight, head_bias):
        wide_bias = head_bias.reshape(1, VOCAB)
        return (
            targets.reshape(ROWS, 1),
            masked.reshape(ROWS, 1),
            jnp.pad(head_weight, ((0, 0), (0, 128 - VOCAB))),
            jnp.pad(wide_bias, ((0, 0), (0, 128 - VOCAB)), constant_values=-1e30),
        )

    def fan(lines, name):
        return [swaps(lines, axis, name + "_" + axis) for axis in "yxc"]

    def fan_y(y, name):
        return [swaps(y, axis, name + "_y" + axis) for axis in "xc"]

    def fan_x(x, yx, name):
        return swaps(x, "c", name + "_xc"), swaps(yx, "c", name + "_yxc")

    def in_place(own, y, x, c, yx, yc, xc, yxc):
        return [part[0] for part in (own, y, c, yc, x, yx, xc, yxc)]

    if moves.staged:
        a0 = run(moves.own_quarter, attn_weight[0])
        a0_far = moves.hop(a0, 2, "a0_far")
        u0 = run(moves.own_quarter, up_weight[0])
        u0_far = moves.hop(u0, 2, "u0_far")
        d0 = run(moves.own_half, down_weight[0])
        a0 = run(moves.high, a0, a0_far)
        a0_near = moves.hop(a0, 1, "a0_near")
        u0 = run(moves.high, u0, u0_far)
        u0_near = moves.hop(u0, 1, "u0_near")
        (d0,) = run.hold(d0)
        d0_far = moves.hop(d0, 2, "d0_far")
        a0 = run(moves.low, a0, a0_near)
        a0_y, a0_x, a0_c = fan(a0, "a0")
        j1 = run(
            lambda a, u: jnp.concatenate([moves.own_quarter(a), moves.own_quarter(u)]),
            *(attn_weight[1], up_weight[1]),
        )
        d1 = run(moves.own_half, down_weight[1])
        a0_y = run.hold(*a0_y)
        a0_yx, a0_yc = fan_y(a0_y, "a0")
        u0 = run(moves.low, u0, u0_near)
        u0_y, u0_x, u0_c = fan(u0, "u0")
        d0 = run(moves.high, d0, d0_far)
        d0_near = moves.hop(d0, 1, "d0_near")
        ready = run(prepared, targets, masked, head_weight, head_bias)
        a0_x, a0_yx = run.hold(a0_x, a0_yx)
        a0_xc, a0_yxc = fan_x(a0_x, a0_yx, "a0")
        quarters0 = in_place(a0, a0_y, a0_x, a0_c, a0_yx, a0_yc, a0_xc, a0_yxc)
        mixed0 = run(mix_on(0), inputs, *quarters0)
        u0_y = run.hold(*u0_y)
        u0_yx, u0_yc = fan_y(u0_y, "u0")
        d0 = run(moves.low_halves, d0, d0_near)
        d0_y, d0_c = swaps(d0, "y", "d0_y"), swaps(d0, "c", "d0_c")
        j1, d1 = run.hold(j1, d1)
        j1_far = moves.hop(j1, 2, "j1_far")
        u0_x = run.hold(*u0_x)
        u0_xc = swaps(u0_x, "c", "u0_xc")
        j1 = run(moves.high, j1, j1_far)
        j1_near = moves.hop(j1, 1, "j1_near")
        d0_y[0:1] = run.hold(d0_y[0])
        d0_yc = swaps(d0_y[:1], "c", "d0_yc")
        u0_yx = run.hold(*u0_yx)
        u0_yxc = swaps(u0_yx, "c", "u0_yxc")
        j1 = run(moves.low, j1, j1_near)
        j1_y, j1_x, j1_c = fan(j1, "j1")
        d0_y[1:2] = run.hold(d0_y[1])
        d0_yc += swaps(d0_y[1:], "c", "d0_yc")
        ups0 = in_place(u0, u0_y, u0_x, u0_c, u0_yx, u0_yc, u0_xc, u0_yxc)
        wide0 = run(up_on(0), mixed0[4], *ups0)
        (d1,) = run.hold(d1)
        d1_far = moves.hop(d1, 2, "d1_far")
        downs0 = (*d0, *d0_y, *d0_c, *d0_yc)
        residual1 = run(down_on(0), mixed0[3], wide0[0], *downs0)
        j1_x = run.hold(*j1_x)
        j1_xc = swaps(j1_x, "c", "j1_xc")
        j1_y = run.hold(*j1_y)
        j1_yx, j1_yc = fan_y(j1_y, "j1")
        d1 = run(moves.high, d1, d1_far)
        d1_near = moves.hop(d1, 1, "d1_near")
        d1 = run(moves.low_halves, d1, d1_near)
        d1_y, d1_c = swaps(d1, "y", "d1_y"), swaps(d1, "c", "d1_c")
        j1_yx = run.hold(*j1_yx)
        j1_yxc = swaps(j1_yx, "c", "j1_yxc")
        ups1 = in_place(j1, j1_y, j1_x, j1_c, j1_yx, j1_yc, j1_xc, j1_yxc)
        quarters1 = ups1
        mixed1 = run(mix_on(1), residual1, *quarters1)
        d1_y[0:1] = run.hold(d1_y[0])
        d1_yc = swaps(d1_y[:1], "c", "d1_yc")
        wide1 = run(up_on(1), mixed1[4], *ups1)
        d1_y[1:2] = run.hold(d1_y[1])
        d1_yc += swaps(d1_y[1:], "c", "d1_yc")
        downs1 = (*d1, *d1_y, *d1_c, *d1_yc)
        residual = run(down_on(1), mixed1[3], wide1[0], *downs1)
        weights = [(quarters0, ups0, downs0), (quarters1, ups1, downs1)]
        saved = [(inputs, *mixed0, *wide0), (residual1, *mixed1, *wide1)]
    else:
        weights, saved = [], []
        residual = inputs
        for layer in range(LAYERS):
            quarters = moves.plain_quarters(attn_weight[layer])
            ups = moves.plain_quarters(up_weight[layer])
            downs = moves.plain_halves(down_weight[layer])
            weights.append((quarters, ups, downs))
            mixed = mix_on(layer)(residual, *quarters)
            wide = up_on(layer)(mixed[4], *ups)
            saved.append((residual, *mixed, *wide))
            residual = down_on(layer)(mixed[3], wide[0], *downs)
        ready = prepared(targets, masked, head_weight, head_bias)
    activations, grad, rounded, head_small = run(
        head, residual, *ready, final_gain.reshape(1, D), final_shift.reshape(1, D)
    )

    def down_at(layer):
        return lambda rounded: down_back(place, rounded, saved[layer][6])

    def wide_first(layer):
        _, ups, downs = weights[layer]
        _, _, _, _, _, second, _, slope = saved[layer]
        return lambda rounded: wide_back_first(place, rounded, second, slope, ups, downs)

    def wide_last(layer):
        _, ups, downs = weights[layer]
        _, _, _, _, middle, second, _, slope = saved[layer]
        return lambda rounded, before, grad, *got: wide_back_last(
            place, rounded, second, slope, ups, downs, before, grad, middle, norm_gains[layer], *got
        )

    def mix_first(layer):
        residual, packed, logs, mixed, _, _, _, _ = saved[layer]
        quarters = weights[layer][0]
        gains, biases = norm_gains[layer], layer_biases[layer]
        return lambda rounded, grad: mix_back(
            place, lengths, rounded, grad, residual, quarters, packed, logs, mixed, gains, biases
        )

    def mix_last(*arrays):
        return mix_back_last(place, *arrays)

    def shift_rows(shift_send, shift_keep):
        send, keep = (part.reshape(2, 2, TILE)[::-1] for part in (shift_send, shift_keep))
        parts = moves.ordered(moves.c_at, keep, send).swapaxes(0, 1)
        return jnp.where(moves.x_at == 0, parts, parts[::-1]).reshape(TILES, TILE)

    def packed_small(head_small, *rest):
        small = [head_small]
        for layer in range(LAYERS):
            shift_send, shift_keep, wide_small, mix_small = rest[4 * layer : 4 * layer + 4]
            small += [shift_rows(shift_send, shift_keep), wide_small, mix_small]
        return jnp.concatenate(small, 0)

    def sum_at(at):
        return lambda keep, got, *rest: rounded_sum(keep[at], got[at], *rest)

    if moves.staged:
        *d1_send, d1_keep = run(down_at(1), rounded)
        d1_c = swaps(d1_send, "c", "d1_c")
        *u1_send, shift_send1, before = run(wide_first(1), rounded)
        u1_c = swaps(u1_send, "c", "u1_c")
        d1_y = swap(run(lambda k, *c: down_sum(1, k, c), d1_keep, *d1_c[:4]), "y", "d1_y")
        u1_pass, u1_keep, shift_keep1, grad, rounded1, wide_small1 = run(
            wide_last(1), rounded, before, grad, *u1_c
        )
        u1_x = swap(u1_pass, "x", "u1_x")
        *a1_send, pre1, rights1, grad, rounded, mix_small1 = run(mix_first(1), rounded1, grad)
        a1_c = swaps(a1_send, "c", "a1_c")
        *d0_send, d0_keep = run(down_at(0), rounded)
        d0_c = swaps(d0_send, "c", "d0_c")
        a1_pass, a1_keep = run(mix_last, pre1, saved[1][3], rights1, rounded1, *a1_c)
        a1_x = swap(a1_pass, "x", "a1_x")
        d1 = run(lambda k, y, *c: down_sum(0, k, c, y), d1_keep, d1_y, *d1_c[4:])
        d1 = moves.along_z(d1)
        d0_y = swap(run(lambda k, *c: down_sum(1, k, c), d0_keep, *d0_c[:4]), "y", "d0_y")
        *u0_send, shift_send0, before = run(wide_first(0), rounded)
        u0_c = swaps(u0_send, "c", "u0_c")
        u1_y = swap(run(sum_at(1), u1_keep, u1_x), "y", "u1_y")
        a1_y = swap(run(sum_at(1), a1_keep, a1_x), "y", "a1_y")
        u0_pass, u0_keep, shift_keep0, grad, rounded0, wide_small0 = run(
            wide_last(0), rounded, before, grad, *u0_c
        )
        u0_x = swap(u0_pass, "x", "u0_x")
        d0 = run(lambda k, y, *c: down_sum(0, k, c, y), d0_keep, d0_y, *d0_c[4:])
        d0 = moves.along_z(d0)
        (d1,) = run.hold(d1)
        d1_x, d1_c = swap(d1, "x", "d1_x"), swap(d1, "c", "d1_c")

        def last_sums(u, ux, uy, a, ax, ay):
            both = (wide_sum(u[0], ux[0], uy), wide_sum(a[0], ax[0], ay)[:, None])
            return moves.part_near(jnp.concatenate(both, 1))

        *a0_send, pre0, rights0, grad, rounded, mix_small0 = run(mix_first(0), rounded0, grad)
        a0_c = swaps(a0_send, "c", "a0_c")
        j1_send, j1_stay = run(last_sums, u1_keep, u1_x, u1_y, a1_keep, a1_x, a1_y)
        j1_near = moves.hop(j1_send, 1, "j1_near")
        a0_pass, a0_keep = run(mix_last, pre0, saved[0][3], rights0, rounded0, *a0_c)
        a0_x = swap(a0_pass, "x", "a0_x")
        small = run(
            packed_small,
            head_small,
            *(shift_send0, shift_keep0, wide_small0, mix_small0),
            *(shift_send1, shift_keep1, wide_small1, mix_small1),
        )
        small_c = swap(small, "c", "small_c")
        (d1_x,) = run.hold(d1_x)
        d1_xc = swap(d1_x, "c", "d1_xc")
        u0_y = swap(run(sum_at(1), u0_keep, u0_x), "y", "u0_y")
        small = run(plus, small, small_c)
        small_far = moves.hop(small, 2, "small_far")
        j1_send, j1_stay = run(moves.part_far, j1_stay, j1_near)
        j1_far = moves.hop(j1_send, 2, "j1_far")
        (d0,) = run.hold(d0)
        d0_x, d0_c = swap(d0, "x", "d0_x"), swap(d0, "c", "d0_c")
        small = run(plus, small, small_far)
        small_near = moves.hop(small, 1, "small_near")
        a0_y = swap(run(sum_at(1), a0_keep, a0_x), "y", "a0_y")
        u0 = moves.along_z(run(sum_at(0), u0_keep, u0_x, u0_y))
        j1 = run(rounded_sum, j1_stay, j1_far)
        j1_x, j1_c = swap(j1, "x", "j1_x"), swap(j1, "c", "j1_c")
        small = run(plus, small, small_near)
        small_x = swap(small, "x", "small_x")
        (d0_x,) = run.hold(d0_x)
        d0_xc = swap(d0_x, "c", "d0_xc")
        a0_send, a0_stay = run(lambda k, x, y: moves.part_near(k[0], x[0], y), a0_keep, a0_x, a0_y)
        a0_near = moves.hop(a0_send, 1, "a0_near")
        small = run(plus, small, small_x)
        small_y = swap(small, "y", "small_y")
        (j1_x,) = run.hold(j1_x)
        j1_xc = swap(j1_x, "c", "j1_xc")
        a0_send, a0_stay = run(moves.part_far, a0_stay, a0_near)
        a0_far = moves.hop(a0_send, 2, "a0_far")
        summed = run(plus, small, small_y)
        j0 = run(lambda u, *a: jnp.concatenate([u, rounded_sum(*a)[None]]), u0, a0_stay, a0_far)
        j0_x, j0_c = swap(j0, "x", "j0_x"), swap(j0, "c", "j0_c")
        done = run(
            lambda *v: finish(1, place, v[:4], v[4:]),
            *(j1, j1_c, j1_x, j1_xc, d1, d1_c, d1_x, d1_xc),
        )
        (j0_x,) = run.hold(j0_x)
        j0_xc = swap(j0_x, "c", "j0_xc")
        matrix_grads = run(
            lambda *v: finish(0, place, v[:4], v[4:8], *v[8:]),
            *(j0, j0_c, j0_x, j0_xc, d0, d0_c, d0_x, d0_xc, *done),
        )
    else:
        flats, smalls = [None] * LAYERS, [None] * LAYERS
        for layer in reversed(range(LAYERS)):
            *send, keep = down_at(layer)(rounded)
            got = swaps(send, "c", "down")
            got = jnp.stack([jnp.stack(got[4:]), jnp.stack(got[:4])])
            down_grad = moves.plain_halves_back(rounded_sum(keep, got))
            *send, shift_send, before = wide_first(layer)(rounded)
            passed, keep, shift_keep, grad, rounded, wide_small = wide_last(layer)(
                rounded, before, grad, *swaps(send, "c", "up")
            )
            up_grad = moves.plain_quarters_back(passed, keep)
            middle_rounded = rounded
            *send, pre, rights, grad, rounded, mix_small = mix_first(layer)(rounded, grad)
            got = swaps(send, "c", "attn")
            passed, keep = mix_last(pre, saved[layer][3], rights, middle_rounded, *got)
            attn_grad = moves.plain_quarters_back(passed[:, :, None], keep[:, :, None])
            flats[layer] = (attn_grad, up_grad, down_grad)
            smalls[layer] = (shift_send, shift_keep, wide_small, mix_small)
        summed = moves.sum_all(packed_small(head_small, *smalls[0], *smalls[1]))
        matrix_grads = [jnp.stack(pair) for pair in zip(*flats)]

    gains_grad, biases_grad, shifts_grad = [], [], []
    for layer in range(LAYERS):
        base = 40 + 24 * layer
        shifts_grad.append(summed[base : base + 8].reshape(FF))
        wide_sums = summed[base + 8 : base + 16]
        mix_sums = summed[base + 16 : base + 24]
        gains_grad.append(jnp.stack([mix_sums[0], wide_sums[0]]))
        biases_grad.append(
            jnp.stack([mix_sums[1], wide_sums[1], mix_sums[2], mix_sums[3], wide_sums[2], wide_sums[3]])
        )
    totals = summed[35]
    return (
        activations,
        grad,
        *matrix_grads,
        jnp.stack(gains_grad),
        jnp.stack(biases_grad),
        jnp.stack(shifts_grad),
        summed[:VOCAB].T,
        summed[32],
        summed[33],
        summed[34, :VOCAB],
        totals[0] / totals[2],
        totals[1] / totals[2],
        totals[2].astype(jnp.int32),
    )


def solution(mesh):
    fsdp, dp = mesh.shape["fsdp"], mesh.shape["dp"]
    fine = Mesh(mesh.devices.reshape(fsdp // 2, 2, dp // 2, 2), ("z", "y", "x", "c"))
    tokens = ("z", "y", "x", "c")
    flat = P(None, ("z", "y"), None)
    placed = (P(tokens, None), P(tokens), P(tokens), P(tokens), flat, flat, flat) + (P(),) * 7

    def run(*arrays):
        return local(fsdp, *arrays)

    return jax.shard_map(
        run,
        mesh=fine,
        in_specs=placed,
        out_specs=(P(tokens, None), P(tokens, None), flat, flat, flat) + (P(),) * 10,
        check_vma=False,
    )
```

```python
import math

import jax
import jax.numpy as jnp
from jax import lax
from jax.experimental import pallas as pl
from jax.experimental.pallas import tpu as pltpu
from jax.sharding import Mesh
from jax.sharding import PartitionSpec as P

D = 640
HEADS = 20
HEAD_DIM = 32
FF = 5120
VOCAB = 25
LAYERS = 2
LEN = 128
SEQ_DEV = 4
ROWS = SEQ_DEV * LEN
TILE = 640
TILES = FF // TILE
WIDE = 2 * TILE
STEPS = FF // WIDE
GROUPS = HEADS * HEAD_DIM // 128
PER_GROUP = 128 // HEAD_DIM
CHUNK = 128
CHUNKS = ROWS // CHUNK
SHARD = D // 8
HALF = TILE // 2
BF = jnp.bfloat16
F32 = jnp.float32
MIB = 2**20

SMEM_SPEC = pl.BlockSpec(memory_space=pltpu.SMEM)
ANY_SPEC = pl.BlockSpec(memory_space=pl.ANY)
KERNEL = dict(
    compiler_params=pltpu.CompilerParams(vmem_limit_bytes=60 * MIB),
    cost_estimate=pl.CostEstimate(flops=4 * 10**8, bytes_accessed=2 * MIB, transcendentals=0),
)


def dot(left, right, dims):
    return lax.dot_general(left, right, (dims, ((), ())), preferred_element_type=F32)


def mul_nn(left, right):
    return dot(left, right, ((1,), (0,)))


def mul_nt(left, right):
    return dot(left, right, ((1,), (1,)))


def mul_tn(left, right):
    return dot(left, right, ((0,), (0,)))


def normalize(values):
    centered = values - jnp.mean(values, -1, keepdims=True)
    inverse = lax.rsqrt(jnp.mean(centered * centered, -1, keepdims=True) + 1e-05)
    return (centered * inverse, inverse)


def norm_back(grad_normed, normed, inverse):
    return inverse * (
        grad_normed
        - jnp.mean(grad_normed, -1, keepdims=True)
        - normed * jnp.mean(grad_normed * normed, -1, keepdims=True)
    )


def col_sum(values):
    return jnp.sum(values, 0, keepdims=True)


def sds(shape, dtype):
    return jax.ShapeDtypeStruct(shape, dtype)


def whole_block(shape):
    zeros = (0,) * len(shape)
    return pl.BlockSpec(shape, lambda *_: zeros)


def semaphores(*shape):
    return pltpu.SemaphoreType.DMA(shape)


def copy(source, target, semaphore):
    return pltpu.make_async_copy(source, target, semaphore)


def chunk_rows(index):
    return slice(index * CHUNK, (index + 1) * CHUNK)


def over_chunks(body, start):
    def step(index, carry):
        return body(pl.ds(pl.multiple_of(index * CHUNK, CHUNK), CHUNK), carry)

    return lax.fori_loop(0, CHUNKS, step, start)


def quarter_copies(place_ref, buffers, held, sems):
    x_at, y_at, c_at = place_ref[0], place_ref[1], place_ref[2]
    copies = []
    for number, buffer in enumerate(buffers):
        dx, dc, dy = number // 4, number // 2 % 2, number % 2
        quarter = (x_at ^ dx) * 2 + (c_at ^ dc)
        lanes = pl.ds(pl.multiple_of(quarter * D, 128), D)
        copies.append(copy(buffer.at[:, 0], held.at[:, y_at ^ dy, :, lanes], sems.at[number]))
    return copies


def tiles_from(line):
    return line.shape[1] - 2


def square(values):
    return values.reshape(D, values.shape[-1])


def head_masks():
    lanes = lax.broadcasted_iota(jnp.int32, (LEN, 128), 1) // HEAD_DIM
    return [(lanes == member) for member in range(PER_GROUP)]


def stack_heads(values, masks):
    zero = jnp.zeros_like(values)
    return jnp.concatenate([jnp.where(mask, values, zero) for mask in masks], 0)


def unstack_heads(values):
    parts = [
        values[HEAD_DIM * member : HEAD_DIM * (member + 1), LEN * member : LEN * (member + 1)]
        for member in range(PER_GROUP)
    ]
    return jnp.concatenate(parts, 0).T


def scores_of(keys, queries, valid):
    scores = mul_nt(keys, queries) * (1.0 / math.sqrt(HEAD_DIM))
    return jnp.where(valid, scores, -1e30)


def mix_kernel(place_ref, lengths_ref, residual_ref, *refs):
    buffers, refs = refs[:8], refs[8:]
    gains_ref, biases_ref, packed_out, log_ref, mixed_out, middle_out, second_out, *refs = refs
    held, pre, packed, mixed, middles, seconds, sems, out_sems, row_sems = refs
    copies = quarter_copies(place_ref, buffers, held, sems)
    for one in copies:
        one.start()

    def first(rows, carry):
        normed, inverse = normalize(residual_ref[rows, :].astype(F32))
        pre[rows, :] = (normed * gains_ref[0:1, :] + biases_ref[0:1, :]).astype(BF)
        return carry

    over_chunks(first, 0)
    for one in copies:
        one.wait()
    shifts = (biases_ref[2:3, :], 0.0, biases_ref[3:4, :])
    sent = []
    result = mul_nn(pre[...], square(held[:, :, :, : 3 * D]))
    for part in range(3):
        lanes = slice(part * D, (part + 1) * D)
        packed[:, lanes] = (result[:, lanes] + shifts[part]).astype(BF)
        sent.append(copy(packed.at[:, lanes], packed_out.at[:, lanes], out_sems.at[part]))
        sent[-1].start()
    masks = head_masks()
    row_ids = lax.broadcasted_iota(jnp.int32, (LEN, 1), 0)

    def one_sequence(seq, carry):
        rows = pl.ds(pl.multiple_of(seq * LEN, LEN), LEN)
        valid = row_ids < lengths_ref[seq]
        for group in range(GROUPS):
            lanes = slice(group * 128, (group + 1) * 128)
            queries = stack_heads(packed[rows, lanes], masks)
            key_rows = packed[rows, D + group * 128 : D + (group + 1) * 128]
            value_rows = packed[rows, 2 * D + group * 128 : 2 * D + (group + 1) * 128]
            scores = scores_of(key_rows, queries, valid)
            top = jnp.max(scores, 0, keepdims=True)
            expos = jnp.exp(scores - top)
            total = jnp.sum(expos, 0, keepdims=True)
            probs = (expos * (1.0 / total)).astype(BF)
            log_ref[seq * GROUPS + group] = top + jnp.log(total)
            mixed[rows, lanes] = unstack_heads(mul_tn(value_rows, probs)).astype(BF)
        return carry

    lax.fori_loop(0, SEQ_DEV, one_sequence, 0)
    sent.append(copy(mixed, mixed_out, out_sems.at[3]))
    sent[-1].start()
    middles[...] = mul_nn(mixed[...], square(held[:, :, :, 3 * D :])) + biases_ref[4:5, :]
    for index in range(CHUNKS):
        rows = chunk_rows(index)
        middle = middles[rows, :] + residual_ref[rows, :].astype(F32)
        middles[rows, :] = middle
        normed, inverse = normalize(middle)
        seconds[rows, :] = (normed * gains_ref[1:2, :] + biases_ref[1:2, :]).astype(BF)
        sent.append(copy(middles.at[rows, :], middle_out.at[rows, :], row_sems.at[index, 0]))
        sent[-1].start()
        sent.append(copy(seconds.at[rows, :], second_out.at[rows, :], row_sems.at[index, 1]))
        sent[-1].start()
    for one in sent:
        one.wait()


def mix(place, lengths, residual, quarters, gains, biases):
    logs = (SEQ_DEV * GROUPS, 1, PER_GROUP * LEN)
    return pl.pallas_call(
        mix_kernel,
        grid=(1,),
        out_shape=(
            sds((ROWS, 3 * D), BF),
            sds(logs, F32),
            sds((ROWS, D), BF),
            sds((ROWS, D), F32),
            sds((ROWS, D), BF),
        ),
        in_specs=[SMEM_SPEC, SMEM_SPEC, whole_block((ROWS, D))]
        + [ANY_SPEC] * 8
        + [whole_block((2, D)), whole_block((6, D))],
        out_specs=(ANY_SPEC, whole_block(logs), ANY_SPEC, ANY_SPEC, ANY_SPEC),
        scratch_shapes=[
            pltpu.VMEM((4, 2, SHARD, 4 * D), BF),
            pltpu.VMEM((ROWS, D), BF),
            pltpu.VMEM((ROWS, 3 * D), BF),
            pltpu.VMEM((ROWS, D), BF),
            pltpu.VMEM((ROWS, D), F32),
            pltpu.VMEM((ROWS, D), BF),
            semaphores(8),
            semaphores(4),
            semaphores(CHUNKS, 2),
        ],
        **KERNEL,
    )(place, lengths, residual, *quarters, gains, biases)


def up_kernel(place_ref, second_ref, *refs):
    buffers, refs = refs[:8], refs[8:]
    shift_ref, active_out, slope_out, held, actives, slopes, sems, out_sems = refs
    step = pl.program_id(0)

    @pl.when(step == 0)
    def _():
        for number, buffer in enumerate(buffers):
            dx, dc, dy = number // 4, number // 2 % 2, number % 2
            at = (place_ref[0] ^ dx) * 2 + (place_ref[2] ^ dc)
            for half in range(2):
                target = held.at[at, :, place_ref[1] ^ dy, :, half * TILE : (half + 1) * TILE]
                copy(buffer.at[:, tiles_from(buffer) + half], target, sems.at[at, dy, half]).start()

    for dy in range(2):
        for half in range(2):
            target = held.at[step, :, dy, :, half * TILE : (half + 1) * TILE]
            copy(buffers[0].at[:, 0], target, sems.at[step, dy, half]).wait()
    up_tile = square(held[step])
    shift = shift_ref[pl.ds(step, 1), :]
    for index in range(2):
        rows = slice(index * 2 * CHUNK, (index + 1) * 2 * CHUNK)
        hidden = mul_nn(second_ref[rows, :], up_tile) + shift
        phi = 0.5 + 0.5 * lax.erf(hidden * math.sqrt(0.5))
        density = jnp.exp(hidden * hidden * -0.5) * (1.0 / math.sqrt(2.0 * math.pi))
        actives[step, rows, :] = (hidden * phi).astype(BF)
        slopes[step, rows, :] = (phi + hidden * density).astype(BF)
    copy(actives.at[step], active_out.at[step], out_sems.at[step, 0]).start()
    copy(slopes.at[step], slope_out.at[step], out_sems.at[step, 1]).start()

    @pl.when(step == STEPS - 1)
    def _():
        for at in range(STEPS):
            copy(actives.at[at], active_out.at[at], out_sems.at[at, 0]).wait()
            copy(slopes.at[at], slope_out.at[at], out_sems.at[at, 1]).wait()


def up(place, second, parts, shift):
    out = sds((STEPS, ROWS, WIDE), BF)
    return pl.pallas_call(
        up_kernel,
        grid=(STEPS,),
        out_shape=(out, out),
        in_specs=[SMEM_SPEC, whole_block((ROWS, D))]
        + [ANY_SPEC] * 8
        + [whole_block((STEPS, WIDE))],
        out_specs=(ANY_SPEC, ANY_SPEC),
        scratch_shapes=[
            pltpu.VMEM((STEPS, 4, 2, SHARD, WIDE), BF),
            pltpu.VMEM((STEPS, ROWS, WIDE), BF),
            pltpu.VMEM((STEPS, ROWS, WIDE), BF),
            semaphores(STEPS, 2, 2),
            semaphores(STEPS, 2),
        ],
        **KERNEL,
    )(place, second, *parts, shift)


def down_kernel(place_ref, middle_ref, active_ref, *refs):
    buffers, (biases_ref, out_ref, held, rows, sems, row_sems) = refs[:8], refs[8:]
    step = pl.program_id(0)

    @pl.when(step == 0)
    def _():
        for z_at in range(4):
            for number in range(4):
                dc, dy = number // 2, number % 2
                y_at, c_at = place_ref[1] ^ dy, place_ref[2] ^ dc
                buffer = buffers[dc * 4 + dy * 2 + z_at // 2].at[z_at % 2]
                copy(buffer, held.at[z_at, y_at, c_at], sems.at[z_at, y_at, c_at]).start()
            copy(active_ref.at[z_at], rows.at[z_at], row_sems.at[z_at]).start()
        out_ref[...] = middle_ref[...] + biases_ref[5:6, :]

    for y_at in range(2):
        for c_at in range(2):
            copy(buffers[0].at[0], held.at[step, y_at, c_at], sems.at[step, y_at, c_at]).wait()
    copy(active_ref.at[0], rows.at[step], row_sems.at[step]).wait()
    out_ref[...] += mul_nn(rows[step], held[step].reshape(WIDE, D))


def down(place, middle, active, parts, biases):
    return pl.pallas_call(
        down_kernel,
        grid=(STEPS,),
        out_shape=sds((ROWS, D), F32),
        in_specs=[SMEM_SPEC, whole_block((ROWS, D))] + [ANY_SPEC] * 9 + [whole_block((6, D))],
        out_specs=whole_block((ROWS, D)),
        scratch_shapes=[
            pltpu.VMEM((4, 2, 2, HALF, D), BF),
            pltpu.VMEM((STEPS, ROWS, WIDE), BF),
            semaphores(4, 2, 2),
            semaphores(STEPS),
        ],
        **KERNEL,
    )(place, middle, active, *parts, biases)


def head_kernel(
    residual_ref,
    targets_ref,
    masked_ref,
    weight_ref,
    shift_ref,
    gain_ref,
    move_ref,
    activations_ref,
    grad_ref,
    rounded_ref,
    small_ref,
):
    small_ref[...] = jnp.zeros_like(small_ref)
    lanes = lax.broadcasted_iota(jnp.int32, (1, 128), 1)

    def body(rows, carry):
        weight_grad, gain_grad, move_grad, shift_grad, stats = carry
        residual = residual_ref[rows, :]
        activations_ref[rows, :] = residual.astype(BF)
        normed, inverse = normalize(residual)
        final = (normed * gain_ref[...] + move_ref[...]).astype(BF)
        logits = mul_nn(final, weight_ref[...]) + shift_ref[...]
        top = jnp.max(logits, -1, keepdims=True)
        log_total = top + jnp.log(jnp.sum(jnp.exp(logits - top), -1, keepdims=True))
        onehot = (targets_ref[rows, :] == lanes).astype(F32)
        picked = jnp.sum(logits * onehot, -1, keepdims=True)
        mask = masked_ref[rows, :].astype(F32)
        loss = col_sum(mask * (log_total - picked))
        hits = col_sum(mask * jnp.exp(picked - log_total))
        count = col_sum(mask)
        stats = stats + (
            jnp.where(lanes == 0, loss, 0.0)
            + jnp.where(lanes == 1, hits, 0.0)
            + jnp.where(lanes == 2, count, 0.0)
        )
        grad_logits = (mask * (jnp.exp(logits - log_total) - onehot)).astype(BF)
        weight_grad = weight_grad + mul_tn(grad_logits, final)
        shift_grad = shift_grad + col_sum(grad_logits.astype(F32))
        grad_final = mul_nt(grad_logits, weight_ref[...])
        gain_grad = gain_grad + col_sum(grad_final * normed)
        move_grad = move_grad + col_sum(grad_final)
        grad = norm_back(grad_final * gain_ref[...], normed, inverse)
        grad_ref[rows, :] = grad
        rounded_ref[rows, :] = grad.astype(BF)
        return weight_grad, gain_grad, move_grad, shift_grad, stats

    row = jnp.zeros((1, D), F32)
    narrow = jnp.zeros((1, 128), F32)
    weight_grad, gain_grad, move_grad, shift_grad, stats = over_chunks(
        body, (jnp.zeros((128, D), F32), row, row, narrow, narrow)
    )
    small_ref[0:32, :] = weight_grad[0:32, :]
    small_ref[32:33, :] = gain_grad
    small_ref[33:34, :] = move_grad
    small_ref[34:35, 0:128] = shift_grad
    small_ref[35:36, 0:128] = stats


def head(residual, targets, masked, weight, shift, gain, move):
    full = whole_block((ROWS, D))
    return pl.pallas_call(
        head_kernel,
        out_shape=(
            sds((ROWS, D), BF),
            sds((ROWS, D), F32),
            sds((ROWS, D), BF),
            sds((40, D), F32),
        ),
        grid=(1,),
        in_specs=[full, whole_block((ROWS, 1)), whole_block((ROWS, 1)), whole_block((D, 128))]
        + [whole_block((1, 128)), whole_block((1, D)), whole_block((1, D))],
        out_specs=(full, full, full, whole_block((40, D))),
        **KERNEL,
    )(residual, targets, masked, weight, shift, gain, move)


def down_back_kernel(place_ref, grad_ref, active_ref, *refs):
    sends, (keep_out, held, grads, sems, out_sems) = refs[:8], refs[8:]
    step = pl.program_id(0)
    c_at = place_ref[2]

    @pl.when(step == 0)
    def _():
        for at in range(TILES):
            z_at, y_at = at % 4, place_ref[1] ^ (1 - at // 4)
            source = active_ref.at[z_at, :, pl.ds(pl.multiple_of(y_at * TILE, 128), TILE)]
            target = held.at[at // 2, :, at % 2 * TILE : (at % 2 + 1) * TILE]
            copy(source, target, sems.at[at]).start()

    for part in range(2):
        target = held.at[step, :, part * TILE : (part + 1) * TILE]
        copy(active_ref.at[0, :, :TILE], target, sems.at[2 * step + part]).wait()
    grads[step] = mul_tn(grad_ref[...], held[step]).astype(BF).reshape(2, HALF, WIDE)
    for at in range(TILES):

        @pl.when(step == at // 2)
        def _():
            lanes = slice(at % 2 * TILE, (at % 2 + 1) * TILE)
            copy(grads.at[at // 2, 1 - c_at, :, lanes], sends[at], out_sems.at[at, 0]).start()
            kept = grads.at[at // 2, c_at, :, lanes]
            copy(kept, keep_out.at[1 - at // 4, at % 4], out_sems.at[at, 1]).start()

    @pl.when(step == STEPS - 1)
    def _():
        for at in range(TILES):
            one = grads.at[0, 0, :, :TILE]
            copy(one, sends[at], out_sems.at[at, 0]).wait()
            copy(one, keep_out.at[0, 0], out_sems.at[at, 1]).wait()


def down_back(place, grad, active):
    part = sds((HALF, TILE), BF)
    return pl.pallas_call(
        down_back_kernel,
        grid=(STEPS,),
        in_specs=[SMEM_SPEC, whole_block((ROWS, D)), ANY_SPEC],
        out_specs=(ANY_SPEC,) * 9,
        out_shape=(part,) * 8 + (sds((2, 4, HALF, TILE), BF),),
        scratch_shapes=[
            pltpu.VMEM((STEPS, ROWS, WIDE), BF),
            pltpu.VMEM((STEPS, 2, HALF, WIDE), BF),
            semaphores(TILES),
            semaphores(TILES, 2),
        ],
        **KERNEL,
    )(place, grad, active)


def down_sum_kernel(side, others, keep_ref, *refs):
    parts, refs = refs[:4], refs[4:]
    other_refs, refs = refs[:others], refs[others:]
    out_ref, kept, got, other, total, sems, other_sems, out_sems = refs
    copies = []
    for at in range(4):
        copies.append(
            [
                copy(keep_ref.at[side, at], kept.at[at], sems.at[at, 0]),
                copy(parts[at], got.at[at], sems.at[at, 1]),
            ]
            + [copy(ref.at[at], other.at[at], other_sems.at[at]) for ref in other_refs]
        )
        for one in copies[-1]:
            one.start()
    for at in range(4):
        for one in copies[at]:
            one.wait()
        value = kept[at].astype(F32) + got[at].astype(F32)
        if others:
            value = value + other[at].astype(F32)
        total[at] = value.astype(BF)
        copy(total.at[at], out_ref.at[at], out_sems.at[at]).start()
    for at in range(4):
        copy(total.at[at], out_ref.at[at], out_sems.at[at]).wait()


def down_sum(side, keep, parts, *other):
    shape = (4, HALF, TILE)

    def kernel(*refs):
        down_sum_kernel(side, len(other), *refs)

    return pl.pallas_call(
        kernel,
        grid=(1,),
        in_specs=[ANY_SPEC] * (5 + len(other)),
        out_specs=ANY_SPEC,
        out_shape=sds(shape, BF),
        scratch_shapes=[pltpu.VMEM(shape, BF)] * 4
        + [semaphores(4, 2), semaphores(4), semaphores(4)],
        **KERNEL,
    )(keep, *parts, *other)


def wide_back_start(phase, place_ref, slope_ref, ups, downs, held, sems):
    x_at, y_at, c_at = place_ref[0], place_ref[1], place_ref[2]
    held_up, held_down, slopes = held
    up_sems, down_sems, slope_sems = sems
    for step in range(2):
        dx = 1 - step
        for number, buffer in enumerate(downs):
            dc, dy, z_high = number // 4, number // 2 % 2, number % 2

            @pl.when(x_at ^ dx == z_high)
            def _():
                y_to, c_to = y_at ^ dy, c_at ^ dc
                target = held_down.at[step, y_to, c_to]
                source = buffer.at[c_at ^ (1 - phase)]
                copy(source, target, down_sems.at[step, y_to, c_to]).start()

        quarter = (x_at ^ dx) * 2 + (c_at ^ (1 - phase))
        copy(slope_ref.at[quarter], slopes.at[step], slope_sems.at[step]).start()
        for dy in range(2):
            for half in range(2):
                target = held_up.at[step, :, y_at ^ dy, :, half * TILE : (half + 1) * TILE]
                source = ups[2 * dx + dy].at[:, tiles_from(ups[0]) + half]
                copy(source, target, up_sems.at[step, dy, half]).start()


def wide_back_step(step, rounded_ref, second_ref, slope_ref, ups, downs, held, sems, shift_ref, total):
    held_up, held_down, slopes = held
    up_sems, down_sems, slope_sems = sems
    for y_at in range(2):
        for c_at in range(2):
            target = held_down.at[step, y_at, c_at]
            copy(downs[0].at[0], target, down_sems.at[step, y_at, c_at]).wait()
    grad_active = mul_nt(rounded_ref[...], held_down[step].reshape(WIDE, D))
    copy(slope_ref.at[0], slopes.at[step], slope_sems.at[step]).wait()
    grad_hidden = (grad_active * slopes[step].astype(F32)).astype(BF)
    shift_ref[pl.ds(step, 1), :] = col_sum(grad_hidden.astype(F32))
    for dy in range(2):
        for half in range(2):
            target = held_up.at[step, :, dy, :, half * TILE : (half + 1) * TILE]
            copy(ups[0].at[:, 0], target, up_sems.at[step, dy, half]).wait()
    total[...] += mul_nt(grad_hidden, square(held_up[step]))
    return mul_tn(second_ref[...], grad_hidden).reshape(4, 2, SHARD, WIDE)


def wide_back_scratch():
    return [
        pltpu.VMEM((2, 4, 2, SHARD, WIDE), BF),
        pltpu.VMEM((2, 2, 2, HALF, D), BF),
        pltpu.VMEM((2, ROWS, WIDE), BF),
        semaphores(2, 2, 2),
        semaphores(2, 2, 2),
        semaphores(2),
    ]


def wide_back_first_kernel(place_ref, rounded_ref, second_ref, slope_ref, *refs):
    ups, downs, refs = refs[:4], refs[4:12], refs[12:]
    sends, (shift_ref, total_ref, *refs) = refs[:8], refs[8:]
    held, sems, sent, out_sems = refs[:3], refs[3:6], refs[6], refs[7]
    step = pl.program_id(0)

    @pl.when(step == 0)
    def _():
        wide_back_start(0, place_ref, slope_ref, ups, downs, held, sems)
        total_ref[...] = jnp.zeros_like(total_ref)

    up_grad = wide_back_step(
        step, rounded_ref, second_ref, slope_ref, ups, downs, held, sems, shift_ref, total_ref
    )
    for side in range(2):
        sent[step, side ^ place_ref[1]] = up_grad[:, side].astype(BF)

    def out_copy(at, half, dy):
        lanes = slice(half * TILE, (half + 1) * TILE)
        number = 4 * at + 2 * half + dy
        return copy(sent.at[at, dy, :, :, lanes], sends[number], out_sems.at[at, half, dy])

    pieces = [(half, dy) for half in range(2) for dy in range(2)]
    for at in range(2):

        @pl.when(step == at)
        def _():
            for half, dy in pieces:
                out_copy(at, half, dy).start()

    @pl.when(step == 1)
    def _():
        for at in range(2):
            for half, dy in pieces:
                out_copy(at, half, dy).wait()


def wide_back_first(place, rounded, second, slope, up_parts, down_parts):
    full = whole_block((ROWS, D))
    return pl.pallas_call(
        wide_back_first_kernel,
        grid=(2,),
        in_specs=[SMEM_SPEC, full, full] + [ANY_SPEC] * 13,
        out_specs=(ANY_SPEC,) * 8 + (whole_block((2, WIDE)), full),
        out_shape=(sds((4, SHARD, TILE), BF),) * 8 + (sds((2, WIDE), F32), sds((ROWS, D), F32)),
        scratch_shapes=wide_back_scratch()
        + [pltpu.VMEM((2, 2, 4, SHARD, WIDE), BF), semaphores(2, 2, 2)],
        **KERNEL,
    )(place, rounded, second, slope, *up_parts[2:4], *up_parts[6:8], *down_parts)


def wide_back_last_kernel(place_ref, rounded_ref, second_ref, slope_ref, *refs):
    ups, downs, refs = refs[:4], refs[4:12], refs[12:]
    before_ref, grad_ref, middle_ref, gains_ref, *refs = refs
    gots, refs = refs[:8], refs[8:]
    outs, (shift_ref, grad_out, rounded_out, small_ref, *refs) = refs[:2], refs[2:]
    held, sems, refs = refs[:3], refs[3:6], refs[6:]
    kept, got, total, grads, middles, roundeds, got_sems, out_sems, in_sems, row_sems = refs
    step = pl.program_id(0)
    fetched = (
        copy(before_ref, total, in_sems.at[0]),
        copy(grad_ref, grads, in_sems.at[1]),
        copy(middle_ref, middles, in_sems.at[2]),
    )

    pieces = [(half, dy) for half in range(2) for dy in range(2)]

    def got_copy(at, half, dy):
        lanes = slice(half * TILE, (half + 1) * TILE)
        target = got.at[at, dy, :, :, lanes]
        return copy(gots[4 * at + 2 * half + dy], target, got_sems.at[at, half, dy])

    @pl.when(step == 0)
    def _():
        fetched[0].start()
        wide_back_start(1, place_ref, slope_ref, ups, downs, held, sems)
        for at in range(2):
            for half, dy in pieces:
                got_copy(at, half, dy).start()
        fetched[1].start()
        fetched[2].start()
        fetched[0].wait()

    up_grad = wide_back_step(
        step, rounded_ref, second_ref, slope_ref, ups, downs, held, sems, shift_ref, total
    )
    for half, dy in pieces:
        lanes = slice(half * TILE, (half + 1) * TILE)
        copy(gots[0], got.at[step, dy, :, :, lanes], got_sems.at[step, half, dy]).wait()
    for side in range(2):
        at_side = side ^ place_ref[1]
        kept[step, at_side] = (up_grad[:, side] + got[step, at_side].astype(F32)).astype(BF)

    def out_copy(at, half, dy):
        lanes = slice(half * TILE, (half + 1) * TILE)
        target = outs[at].at[dy, :, half]
        return copy(kept.at[at, dy, :, :, lanes], target, out_sems.at[at, half, dy])

    for at in range(2):

        @pl.when(step == at)
        def _():
            for half, dy in pieces:
                out_copy(at, half, dy).start()

    @pl.when(step == 1)
    def _():
        fetched[1].wait()
        fetched[2].wait()
        sums = [jnp.zeros((1, D), F32)] * 4
        sent = []
        for index in range(CHUNKS):
            rows = chunk_rows(index)
            normed, inverse = normalize(middles[rows, :])
            grad_second = total[rows, :]
            grad = grads[rows, :] + norm_back(grad_second * gains_ref[1:2, :], normed, inverse)
            rounded = grad.astype(BF)
            grads[rows, :] = grad
            roundeds[rows, :] = rounded
            sent.append(copy(grads.at[rows, :], grad_out.at[rows, :], row_sems.at[index, 0]))
            sent.append(copy(roundeds.at[rows, :], rounded_out.at[rows, :], row_sems.at[index, 1]))
            sent[-2].start()
            sent[-1].start()
            terms = (
                grad_second * normed,
                grad_second,
                rounded.astype(F32),
                rounded_ref[rows, :].astype(F32),
            )
            sums = [old + col_sum(term) for old, term in zip(sums, terms)]
        small_ref[...] = jnp.zeros_like(small_ref)
        for number in range(4):
            small_ref[number : number + 1, :] = sums[number]
        for at in range(2):
            for half, dy in pieces:
                out_copy(at, half, dy).wait()
        for one in sent:
            one.wait()


def wide_back_last(
    place, rounded, second, slope, up_parts, down_parts, before, grad, middle, gains, *got
):
    full = whole_block((ROWS, D))
    out = sds((2, 4, 2, SHARD, TILE), BF)
    return pl.pallas_call(
        wide_back_last_kernel,
        grid=(2,),
        in_specs=[SMEM_SPEC, full, full]
        + [ANY_SPEC] * 16
        + [whole_block((2, D))]
        + [ANY_SPEC] * 8,
        out_specs=(ANY_SPEC, ANY_SPEC, whole_block((2, WIDE)), ANY_SPEC, ANY_SPEC, whole_block((8, D))),
        out_shape=(
            out,
            out,
            sds((2, WIDE), F32),
            sds((ROWS, D), F32),
            sds((ROWS, D), BF),
            sds((8, D), F32),
        ),
        scratch_shapes=wide_back_scratch()
        + [
            pltpu.VMEM((2, 2, 4, SHARD, WIDE), BF),
            pltpu.VMEM((2, 2, 4, SHARD, WIDE), BF),
            pltpu.VMEM((ROWS, D), F32),
            pltpu.VMEM((ROWS, D), F32),
            pltpu.VMEM((ROWS, D), F32),
            pltpu.VMEM((ROWS, D), BF),
            semaphores(2, 2, 2),
            semaphores(2, 2, 2),
            semaphores(3),
            semaphores(CHUNKS, 2),
        ],
        **KERNEL,
    )(
        place, rounded, second, slope, *up_parts[0:2], *up_parts[4:6], *down_parts,
        before, grad, middle, gains, *got
    )


def mix_back_kernel(place_ref, lengths_ref, rounded_ref, grad_ref, residual_ref, *refs):
    buffers, (packed_ref, log_ref, mixed_ref, gains_ref, biases_ref, *refs) = refs[:8], refs[8:]
    sends, (pre_out, rights_out, grad_out, rounded_out, small_ref, *refs) = refs[:4], refs[4:]
    held, packed, sent, pre, rights, grad_mixed, total, grads, roundeds, *refs = refs
    sems, in_sems, send_sems, pre_sem, right_sems, row_sems = refs
    x_at, y_at, c_at = place_ref[0], place_ref[1], place_ref[2]
    copies = quarter_copies(place_ref, buffers, held, sems)
    for one in copies:
        one.start()
    fetched = [
        copy(packed_ref.at[chunk_rows(at), :], packed.at[chunk_rows(at), :], in_sems.at[at])
        for at in range(SEQ_DEV)
    ]
    fetched.append(copy(grad_ref, grads, in_sems.at[SEQ_DEV]))
    for one in fetched:
        one.start()

    def send_grad(part, right):
        @pl.when(c_at ^ (part & 1) == 1)
        def _():
            left = mixed_ref[...] if part == 3 else pre[...]
            value = mul_tn(left, right).astype(BF).reshape(4, 2, SHARD, D)
            for side in range(2):
                sent[x_at ^ (part >> 1), side ^ y_at] = value[:, side]

    send_grad(3, rounded_ref[...])

    def first(rows, carry):
        normed, inverse = normalize(residual_ref[rows, :].astype(F32))
        pre[rows, :] = (normed * gains_ref[0:1, :] + biases_ref[0:1, :]).astype(BF)
        return carry

    over_chunks(first, 0)
    pre_copy = copy(pre, pre_out, pre_sem.at[0])
    pre_copy.start()
    for one in copies:
        one.wait()
    grad_mixed[...] = mul_nt(rounded_ref[...], square(held[:, :, :, 3 * D :])).astype(BF)
    masks = head_masks()
    row_ids = lax.broadcasted_iota(jnp.int32, (LEN, 1), 0)
    scale = 1.0 / math.sqrt(HEAD_DIM)

    def right_copy(seq, part):
        rows = pl.ds(pl.multiple_of(seq * LEN, LEN), LEN)
        lanes = slice(part * D, (part + 1) * D)
        return copy(rights.at[rows, lanes], rights_out.at[part, rows, :], right_sems.at[seq, part])

    def one_sequence(seq, carry):
        rows = pl.ds(pl.multiple_of(seq * LEN, LEN), LEN)
        copy(packed_ref.at[chunk_rows(0), :], packed.at[rows, :], in_sems.at[seq]).wait()
        valid = row_ids < lengths_ref[seq]
        for group in range(GROUPS):
            at_query = slice(group * 128, (group + 1) * 128)
            queries = stack_heads(packed[rows, at_query], masks)
            key_rows = packed[rows, D + group * 128 : D + (group + 1) * 128]
            value_rows = packed[rows, 2 * D + group * 128 : 2 * D + (group + 1) * 128]
            mixed_grads = stack_heads(grad_mixed[rows, at_query], masks)
            scores = scores_of(key_rows, queries, valid)
            probs = jnp.exp(scores - log_ref[seq * GROUPS + group])
            grad_probs = mul_nt(value_rows, mixed_grads)
            inner = jnp.sum(grad_probs * probs, 0, keepdims=True)
            grad_scores = (probs * (grad_probs - inner)).astype(BF)
            rights[rows, 2 * D + group * 128 : 2 * D + (group + 1) * 128] = mul_nn(probs.astype(BF), mixed_grads).astype(BF)
            rights[rows, D + group * 128 : D + (group + 1) * 128] = (mul_nn(grad_scores, queries) * scale).astype(BF)
            grad_queries = unstack_heads(mul_tn(key_rows, grad_scores))
            rights[rows, at_query] = (grad_queries * scale).astype(BF)
        for part in range(3):
            right_copy(seq, part).start()
        return carry

    lax.fori_loop(0, SEQ_DEV, one_sequence, 0)
    for part in range(3):
        send_grad(part, rights[:, part * D : (part + 1) * D])
    for dx in range(2):
        for dy in range(2):
            copy(sent.at[dx, dy], sends[2 * dx + dy], send_sems.at[dx, dy]).start()
    total[...] = mul_nt(rights[...], square(held[:, :, :, : 3 * D]))
    fetched[-1].wait()
    sums = [jnp.zeros((1, D), F32)] * 4
    out_copies = []
    for index in range(CHUNKS):
        rows = chunk_rows(index)
        normed, inverse = normalize(residual_ref[rows, :].astype(F32))
        grad_pre = total[rows, :]
        grad = grads[rows, :] + norm_back(grad_pre * gains_ref[0:1, :], normed, inverse)
        grads[rows, :] = grad
        roundeds[rows, :] = grad.astype(BF)
        out_copies.append(copy(grads.at[rows, :], grad_out.at[rows, :], row_sems.at[index, 0]))
        out_copies.append(copy(roundeds.at[rows, :], rounded_out.at[rows, :], row_sems.at[index, 1]))
        out_copies[-2].start()
        out_copies[-1].start()
        terms = (
            grad_pre * normed,
            grad_pre,
            rights[rows, 0:D].astype(F32),
            rights[rows, 2 * D : 3 * D].astype(F32),
        )
        sums = [old + col_sum(term) for old, term in zip(sums, terms)]
    small_ref[...] = jnp.zeros_like(small_ref)
    for number in range(4):
        small_ref[number : number + 1, :] = sums[number]
    for seq in range(SEQ_DEV):
        for part in range(3):
            right_copy(seq, part).wait()
    for dx in range(2):
        for dy in range(2):
            copy(sent.at[dx, dy], sends[2 * dx + dy], send_sems.at[dx, dy]).wait()
    for one in [pre_copy] + out_copies:
        one.wait()


def mix_back(
    place, lengths, rounded, middle_grad, residual, quarters, packed, logs, mixed, gains, biases
):
    part = sds((4, SHARD, D), BF)
    full = whole_block((ROWS, D))
    return pl.pallas_call(
        mix_back_kernel,
        out_shape=(part,) * 4
        + (
            sds((ROWS, D), BF),
            sds((3, ROWS, D), BF),
            sds((ROWS, D), F32),
            sds((ROWS, D), BF),
            sds((8, D), F32),
        ),
        grid=(1,),
        in_specs=[SMEM_SPEC, SMEM_SPEC, full, ANY_SPEC, full]
        + [ANY_SPEC] * 9
        + [whole_block((SEQ_DEV * GROUPS, 1, PER_GROUP * LEN)), full]
        + [whole_block((2, D)), whole_block((6, D))],
        out_specs=(ANY_SPEC,) * 8 + (whole_block((8, D)),),
        scratch_shapes=[
            pltpu.VMEM((4, 2, SHARD, 4 * D), BF),
            pltpu.VMEM((ROWS, 3 * D), BF),
            pltpu.VMEM((2, 2, 4, SHARD, D), BF),
            pltpu.VMEM((ROWS, D), BF),
            pltpu.VMEM((ROWS, 3 * D), BF),
            pltpu.VMEM((ROWS, D), BF),
            pltpu.VMEM((ROWS, D), F32),
            pltpu.VMEM((ROWS, D), F32),
            pltpu.VMEM((ROWS, D), BF),
            semaphores(8),
            semaphores(SEQ_DEV + 1),
            semaphores(2, 2),
            semaphores(1),
            semaphores(SEQ_DEV, 3),
            semaphores(CHUNKS, 2),
        ],
        **KERNEL,
    )(
        place, lengths, rounded, middle_grad, residual, *quarters, packed, logs, mixed, gains, biases
    )


def mix_back_last_kernel(place_ref, pre_ref, mixed_ref, rights_ref, rounded_ref, *refs):
    gots, outs, (lefts, rights, got, kept, sems, out_sems) = refs[:4], refs[4:6], refs[6:]
    y_at, c_at = place_ref[1], place_ref[2]
    parts = [(place_ref[0] ^ dx) * 2 + c_at for dx in range(2)]
    for dx in (1, 0):

        @pl.when(parts[dx] == 3)
        def _():
            copy(mixed_ref, lefts.at[dx], sems.at[dx, 3]).start()
            copy(rounded_ref, rights.at[dx], sems.at[dx, 0]).start()

        @pl.when(parts[dx] != 3)
        def _():
            copy(pre_ref, lefts.at[dx], sems.at[dx, 3]).start()
            copy(rights_ref.at[jnp.minimum(parts[dx], 2)], rights.at[dx], sems.at[dx, 0]).start()

        for dy in range(2):
            copy(gots[2 * dx + dy], got.at[dx, dy], sems.at[dx, 1 + dy]).start()
    for dx in (1, 0):
        copy(pre_ref, lefts.at[dx], sems.at[dx, 3]).wait()
        copy(rounded_ref, rights.at[dx], sems.at[dx, 0]).wait()
        value = mul_tn(lefts[dx], rights[dx]).reshape(4, 2, SHARD, D)
        for dy in range(2):
            copy(gots[0], got.at[dx, dy], sems.at[dx, 1 + dy]).wait()
        for side in range(2):
            at = side ^ y_at
            kept[dx, at] = (value[:, side] + got[dx, at].astype(F32)).astype(BF)
        copy(kept.at[dx], outs[1 - dx], out_sems.at[dx]).start()
    for dx in range(2):
        copy(kept.at[dx], outs[1 - dx], out_sems.at[dx]).wait()


def mix_back_last(place, pre, mixed, rights, rounded, *got):
    out = sds((2, 4, SHARD, D), BF)
    return pl.pallas_call(
        mix_back_last_kernel,
        grid=(1,),
        in_specs=[SMEM_SPEC] + [ANY_SPEC] * 8,
        out_specs=(ANY_SPEC,) * 2,
        out_shape=(out, out),
        scratch_shapes=[
            pltpu.VMEM((2, ROWS, D), BF),
            pltpu.VMEM((2, ROWS, D), BF),
            pltpu.VMEM((2, 2, 4, SHARD, D), BF),
            pltpu.VMEM((2, 2, 4, SHARD, D), BF),
            semaphores(2, 4),
            semaphores(2),
        ],
        **KERNEL,
    )(place, pre, mixed, rights, rounded, *got)


def finish_kernel(layer, olds, place_ref, *refs):
    quarters, halves, outs = refs[:4], refs[4:8], refs[8 + olds : 11 + olds]
    attn, ups, downs, sems = refs[11 + olds :]
    x_at, c_at = place_ref[0], place_ref[2]
    values = [ref[...] for ref in quarters]
    pairs = [
        (jnp.where(c_at == 0, own, other), jnp.where(c_at == 0, other, own))
        for own, other in (values[:2], values[2:])
    ]
    ordered = [jnp.where(x_at == 0, own, other) for own, other in zip(*pairs)]
    ordered += [jnp.where(x_at == 0, other, own) for own, other in zip(*pairs)]
    for quarter, value in enumerate(ordered):
        for tile in range(3):
            target, first, stride = (
                (attn, quarter * 5, 20) if tile == 2 else (ups, quarter * 10 + tile * 5, 40)
            )
            for block in range(5):
                target[pl.ds(first + block, SHARD, stride=stride), :] = value[
                    tile, :, block * 128 : (block + 1) * 128
                ].astype(F32)
    copies = [
        copy(target.at[: out.shape[1], :], out.at[layer], sems.at[number])
        for number, (target, out) in enumerate(zip((attn, ups, downs), outs))
    ]
    copies[0].start()
    copies[1].start()
    own, other = (
        halves[at][...].astype(F32) + halves[at + 2][...].astype(F32) for at in range(2)
    )
    turned = jnp.concatenate(
        [jnp.where(c_at == 0, own, other), jnp.where(c_at == 0, other, own)], 0
    ).T
    for block in range(5):
        downs[pl.ds(block, TILE, stride=5), :] = turned[:, block * 128 : (block + 1) * 128]
    copies[2].start()
    for one in copies:
        one.wait()


def finish(layer, place, quarters, halves, *old):
    attn, wide = (D * 4 * D // 8 // 128, 128), (D * FF // 8 // 128, 128)

    def kernel(*refs):
        finish_kernel(layer, len(old), *refs)

    return pl.pallas_call(
        kernel,
        grid=(1,),
        in_specs=[SMEM_SPEC]
        + [whole_block((3, SHARD, D))] * 4
        + [whole_block((HALF, TILE))] * 4
        + [ANY_SPEC] * len(old),
        out_specs=(ANY_SPEC,) * 3,
        out_shape=tuple(sds((LAYERS, *shape), F32) for shape in (attn, wide, wide)),
        scratch_shapes=[pltpu.VMEM((shape[0] + 40, 128), F32) for shape in (attn, wide, wide)]
        + [semaphores(3)],
        input_output_aliases={9 + number: number for number in range(len(old))},
        **KERNEL,
    )(place, *quarters, *halves, *old)


def swap(value, axis, name):
    with jax.named_scope(name):
        return lax.ppermute(value, axis, [(0, 1), (1, 0)])


def swaps(values, axis, name):
    return [swap(value, axis, name) for value in values]


class Order:
    def __init__(self):
        self.last = None

    def hold(self, *arrays):
        if self.last is not None:
            arrays = lax.optimization_barrier((arrays, self.last))[0]
        return arrays

    def __call__(self, function, *arrays):
        results = function(*self.hold(*arrays))
        self.last = jax.tree.leaves(results)[0]
        return results


def wide_sum(*values):
    total = values[0].astype(F32)
    for value in values[1:]:
        total = total + value.astype(F32)
    return total


def rounded_sum(*values):
    return wide_sum(*values).astype(BF)


def plus(own, other):
    return own + other


class Moves:
    def __init__(self, fsdp):
        self.z_size = fsdp // 2
        self.staged = fsdp == 8
        self.x_at = lax.axis_index("x")
        self.y_at = lax.axis_index("y")
        self.z_at = lax.axis_index("z")
        self.c_at = lax.axis_index("c")
        self.place = jnp.stack([self.x_at, self.y_at, self.c_at]).astype(jnp.int32)

    def hop(self, value, reach, name):
        with jax.named_scope(name):
            return lax.ppermute(value, "z", [(at, at ^ reach) for at in range(self.z_size)])

    def ordered(self, bit, own, other):
        return jnp.where(bit == 0, jnp.stack([own, other]), jnp.stack([other, own]))

    def by_side(self, value):
        value = value.reshape(4, 2, *value.shape[1:]).swapaxes(0, 1)
        return jnp.where(self.y_at == 0, value, value[::-1])

    def by_shard(self, value):
        value = jnp.where(self.y_at == 0, value, value[::-1]).swapaxes(0, 1)
        return value.reshape(8, *value.shape[2:])

    def own_quarter(self, flat):
        shard = flat.reshape(SHARD, -1, 128)
        step = shard.shape[1] // 4
        own = lax.dynamic_slice_in_dim(shard, (self.x_at * 2 + self.c_at) * step, step, 1)
        return own.reshape(SHARD, step // 5, 5, 128).swapaxes(0, 1).reshape(-1, SHARD, D)

    def own_half(self, flat):
        own = lax.dynamic_slice_in_dim(flat, self.c_at * HALF * 5, HALF * 5, 0)
        return own.reshape(1, HALF, D)

    def high(self, own, other):
        return self.ordered(self.z_at // 2, own, other)

    def low(self, pair, other):
        bit = self.z_at % 2
        line = jnp.where(bit == 0, jnp.stack([pair, other], 1), jnp.stack([other, pair], 1))
        return (line.reshape(4, *pair.shape[1:]),)

    def low_halves(self, pair, other):
        line = self.low(pair, other)[0][:, 0]
        return line[:2], line[2:]

    def part_near(self, *parts):
        total = wide_sum(*parts)
        total = total.reshape(2, 2, *total.shape[1:])
        near = self.z_at % 2
        return tuple(
            lax.dynamic_index_in_dim(total, at, 1, False).astype(BF) for at in (1 - near, near)
        )

    def part_far(self, *parts):
        total = wide_sum(*parts)
        far = self.z_at // 2
        return tuple(
            lax.dynamic_index_in_dim(total, at, 0, False).astype(BF) for at in (1 - far, far)
        )

    def along_z(self, part):
        return lax.psum_scatter(part, "z", scatter_dimension=0, tiled=False)

    def plain_quarters(self, flat):
        whole = lax.all_gather(flat, ("z", "y"), axis=0, tiled=True)
        whole = whole.reshape(8, SHARD, 4, -1, D).transpose(2, 0, 3, 1, 4)
        lines = []
        for number in range(4):
            quarter = (self.x_at ^ (number >> 1)) * 2 + (self.c_at ^ (number & 1))
            part = self.by_side(lax.dynamic_index_in_dim(whole, quarter, 0, False))
            lines += [part[dy] for dy in range(2)]
        return lines

    def plain_halves(self, flat):
        whole = lax.all_gather(flat, ("z", "y"), axis=0, tiled=True).reshape(8, 2, HALF, D)
        pairs = []
        for number in range(2):
            part = self.by_side(lax.dynamic_index_in_dim(whole, self.c_at ^ number, 1, False))
            pairs += [part[dy, 2 * at : 2 * at + 2] for dy in range(2) for at in range(2)]
        return pairs

    def plain_quarters_back(self, passed, keep):
        part = self.by_shard(rounded_sum(keep, swap(passed, "x", "quarters")))
        part = part.transpose(0, 2, 1, 3).reshape(D, -1)
        part = lax.psum_scatter(part, ("z", "y"), scatter_dimension=0, tiled=True)
        parts = lax.all_gather(part, ("x", "c"), axis=0, tiled=False)
        return parts.swapaxes(0, 1).astype(F32).reshape(-1, 128)

    def plain_halves_back(self, part):
        part = self.by_shard(part).transpose(0, 2, 1).reshape(FF, HALF)
        part = lax.psum_scatter(part, ("z", "y"), scatter_dimension=0, tiled=True).T
        part = rounded_sum(part, swap(part, "x", "halves"))
        return lax.all_gather(part, "c", axis=0, tiled=True).T.astype(F32).reshape(-1, 128)

    def sum_all(self, value):
        for axis in ("c", "x", "y"):
            value = value + swap(value, axis, "small")
        reach = 1
        while reach < self.z_size:
            value = value + self.hop(value, reach, "small")
            reach *= 2
        return value


def local(
    fsdp,
    inputs,
    targets,
    masked,
    lengths,
    attn_weight,
    up_weight,
    down_weight,
    norm_gains,
    layer_biases,
    up_bias,
    head_weight,
    final_gain,
    final_shift,
    head_bias,
):
    moves = Moves(fsdp)
    place = moves.place
    shifts = up_bias.reshape(LAYERS, STEPS, WIDE)
    run = Order()

    def mix_on(layer):
        return lambda r, *q: mix(place, lengths, r, q, norm_gains[layer], layer_biases[layer])

    def up_on(layer):
        return lambda second, *parts: up(place, second, parts, shifts[layer])

    def down_on(layer):
        return lambda m, active, *parts: down(place, m, active, parts, layer_biases[layer])

    def prepared(targets, masked, head_weight, head_bias):
        wide_bias = head_bias.reshape(1, VOCAB)
        return (
            targets.reshape(ROWS, 1),
            masked.reshape(ROWS, 1),
            jnp.pad(head_weight, ((0, 0), (0, 128 - VOCAB))),
            jnp.pad(wide_bias, ((0, 0), (0, 128 - VOCAB)), constant_values=-1e30),
        )

    def fan(lines, name):
        return [swaps(lines, axis, name + "_" + axis) for axis in "yxc"]

    def fan_y(y, name):
        return [swaps(y, axis, name + "_y" + axis) for axis in "xc"]

    def fan_x(x, yx, name):
        return swaps(x, "c", name + "_xc"), swaps(yx, "c", name + "_yxc")

    def in_place(own, y, x, c, yx, yc, xc, yxc):
        return [part[0] for part in (own, y, c, yc, x, yx, xc, yxc)]

    if moves.staged:
        a0 = run(moves.own_quarter, attn_weight[0])
        a0_far = moves.hop(a0, 2, "a0_far")
        u0 = run(moves.own_quarter, up_weight[0])
        u0_far = moves.hop(u0, 2, "u0_far")
        d0 = run(moves.own_half, down_weight[0])
        a0 = run(moves.high, a0, a0_far)
        a0_near = moves.hop(a0, 1, "a0_near")
        u0 = run(moves.high, u0, u0_far)
        u0_near = moves.hop(u0, 1, "u0_near")
        (d0,) = run.hold(d0)
        d0_far = moves.hop(d0, 2, "d0_far")
        a0 = run(moves.low, a0, a0_near)
        a0_y, a0_x, a0_c = fan(a0, "a0")
        j1 = run(
            lambda a, u: jnp.concatenate([moves.own_quarter(a), moves.own_quarter(u)]),
            *(attn_weight[1], up_weight[1]),
        )
        d1 = run(moves.own_half, down_weight[1])
        a0_y = run.hold(*a0_y)
        a0_yx, a0_yc = fan_y(a0_y, "a0")
        u0 = run(moves.low, u0, u0_near)
        u0_y, u0_x, u0_c = fan(u0, "u0")
        d0 = run(moves.high, d0, d0_far)
        d0_near = moves.hop(d0, 1, "d0_near")
        ready = run(prepared, targets, masked, head_weight, head_bias)
        a0_x, a0_yx = run.hold(a0_x, a0_yx)
        a0_xc, a0_yxc = fan_x(a0_x, a0_yx, "a0")
        quarters0 = in_place(a0, a0_y, a0_x, a0_c, a0_yx, a0_yc, a0_xc, a0_yxc)
        mixed0 = run(mix_on(0), inputs, *quarters0)
        u0_y = run.hold(*u0_y)
        u0_yx, u0_yc = fan_y(u0_y, "u0")
        d0 = run(moves.low_halves, d0, d0_near)
        d0_y, d0_c = swaps(d0, "y", "d0_y"), swaps(d0, "c", "d0_c")
        j1, d1 = run.hold(j1, d1)
        j1_far = moves.hop(j1, 2, "j1_far")
        u0_x = run.hold(*u0_x)
        u0_xc = swaps(u0_x, "c", "u0_xc")
        j1 = run(moves.high, j1, j1_far)
        j1_near = moves.hop(j1, 1, "j1_near")
        d0_y[0:1] = run.hold(d0_y[0])
        d0_yc = swaps(d0_y[:1], "c", "d0_yc")
        u0_yx = run.hold(*u0_yx)
        u0_yxc = swaps(u0_yx, "c", "u0_yxc")
        j1 = run(moves.low, j1, j1_near)
        j1_y, j1_x, j1_c = fan(j1, "j1")
        d0_y[1:2] = run.hold(d0_y[1])
        d0_yc += swaps(d0_y[1:], "c", "d0_yc")
        ups0 = in_place(u0, u0_y, u0_x, u0_c, u0_yx, u0_yc, u0_xc, u0_yxc)
        wide0 = run(up_on(0), mixed0[4], *ups0)
        (d1,) = run.hold(d1)
        d1_far = moves.hop(d1, 2, "d1_far")
        downs0 = (*d0, *d0_y, *d0_c, *d0_yc)
        residual1 = run(down_on(0), mixed0[3], wide0[0], *downs0)
        j1_x = run.hold(*j1_x)
        j1_xc = swaps(j1_x, "c", "j1_xc")
        j1_y = run.hold(*j1_y)
        j1_yx, j1_yc = fan_y(j1_y, "j1")
        d1 = run(moves.high, d1, d1_far)
        d1_near = moves.hop(d1, 1, "d1_near")
        d1 = run(moves.low_halves, d1, d1_near)
        d1_y, d1_c = swaps(d1, "y", "d1_y"), swaps(d1, "c", "d1_c")
        j1_yx = run.hold(*j1_yx)
        j1_yxc = swaps(j1_yx, "c", "j1_yxc")
        ups1 = in_place(j1, j1_y, j1_x, j1_c, j1_yx, j1_yc, j1_xc, j1_yxc)
        quarters1 = ups1
        mixed1 = run(mix_on(1), residual1, *quarters1)
        d1_y[0:1] = run.hold(d1_y[0])
        d1_yc = swaps(d1_y[:1], "c", "d1_yc")
        wide1 = run(up_on(1), mixed1[4], *ups1)
        d1_y[1:2] = run.hold(d1_y[1])
        d1_yc += swaps(d1_y[1:], "c", "d1_yc")
        downs1 = (*d1, *d1_y, *d1_c, *d1_yc)
        residual = run(down_on(1), mixed1[3], wide1[0], *downs1)
        weights = [(quarters0, ups0, downs0), (quarters1, ups1, downs1)]
        saved = [(inputs, *mixed0, *wide0), (residual1, *mixed1, *wide1)]
    else:
        weights, saved = [], []
        residual = inputs
        for layer in range(LAYERS):
            quarters = moves.plain_quarters(attn_weight[layer])
            ups = moves.plain_quarters(up_weight[layer])
            downs = moves.plain_halves(down_weight[layer])
            weights.append((quarters, ups, downs))
            mixed = mix_on(layer)(residual, *quarters)
            wide = up_on(layer)(mixed[4], *ups)
            saved.append((residual, *mixed, *wide))
            residual = down_on(layer)(mixed[3], wide[0], *downs)
        ready = prepared(targets, masked, head_weight, head_bias)
    activations, grad, rounded, head_small = run(
        head, residual, *ready, final_gain.reshape(1, D), final_shift.reshape(1, D)
    )

    def down_at(layer):
        return lambda rounded: down_back(place, rounded, saved[layer][6])

    def wide_first(layer):
        _, ups, downs = weights[layer]
        _, _, _, _, _, second, _, slope = saved[layer]
        return lambda rounded: wide_back_first(place, rounded, second, slope, ups, downs)

    def wide_last(layer):
        _, ups, downs = weights[layer]
        _, _, _, _, middle, second, _, slope = saved[layer]
        return lambda rounded, before, grad, *got: wide_back_last(
            place, rounded, second, slope, ups, downs, before, grad, middle, norm_gains[layer], *got
        )

    def mix_first(layer):
        residual, packed, logs, mixed, _, _, _, _ = saved[layer]
        quarters = weights[layer][0]
        gains, biases = norm_gains[layer], layer_biases[layer]
        return lambda rounded, grad: mix_back(
            place, lengths, rounded, grad, residual, quarters, packed, logs, mixed, gains, biases
        )

    def mix_last(*arrays):
        return mix_back_last(place, *arrays)

    def shift_rows(shift_send, shift_keep):
        send, keep = (part.reshape(2, 2, TILE)[::-1] for part in (shift_send, shift_keep))
        parts = moves.ordered(moves.c_at, keep, send).swapaxes(0, 1)
        return jnp.where(moves.x_at == 0, parts, parts[::-1]).reshape(TILES, TILE)

    def packed_small(head_small, *rest):
        small = [head_small]
        for layer in range(LAYERS):
            shift_send, shift_keep, wide_small, mix_small = rest[4 * layer : 4 * layer + 4]
            small += [shift_rows(shift_send, shift_keep), wide_small, mix_small]
        return jnp.concatenate(small, 0)

    def sum_at(at):
        return lambda keep, got, *rest: rounded_sum(keep[at], got[at], *rest)

    if moves.staged:
        *d1_send, d1_keep = run(down_at(1), rounded)
        d1_c = swaps(d1_send, "c", "d1_c")
        *u1_send, shift_send1, before = run(wide_first(1), rounded)
        u1_c = swaps(u1_send, "c", "u1_c")
        d1_y = swap(run(lambda k, *c: down_sum(1, k, c), d1_keep, *d1_c[:4]), "y", "d1_y")
        u1_pass, u1_keep, shift_keep1, grad, rounded1, wide_small1 = run(
            wide_last(1), rounded, before, grad, *u1_c
        )
        u1_x = swap(u1_pass, "x", "u1_x")
        *a1_send, pre1, rights1, grad, rounded, mix_small1 = run(mix_first(1), rounded1, grad)
        a1_c = swaps(a1_send, "c", "a1_c")
        *d0_send, d0_keep = run(down_at(0), rounded)
        d0_c = swaps(d0_send, "c", "d0_c")
        a1_pass, a1_keep = run(mix_last, pre1, saved[1][3], rights1, rounded1, *a1_c)
        a1_x = swap(a1_pass, "x", "a1_x")
        d1 = run(lambda k, y, *c: down_sum(0, k, c, y), d1_keep, d1_y, *d1_c[4:])
        d1 = moves.along_z(d1)
        d0_y = swap(run(lambda k, *c: down_sum(1, k, c), d0_keep, *d0_c[:4]), "y", "d0_y")
        *u0_send, shift_send0, before = run(wide_first(0), rounded)
        u0_c = swaps(u0_send, "c", "u0_c")
        u1_y = swap(run(sum_at(1), u1_keep, u1_x), "y", "u1_y")
        a1_y = swap(run(sum_at(1), a1_keep, a1_x), "y", "a1_y")
        u0_pass, u0_keep, shift_keep0, grad, rounded0, wide_small0 = run(
            wide_last(0), rounded, before, grad, *u0_c
        )
        u0_x = swap(u0_pass, "x", "u0_x")
        d0 = run(lambda k, y, *c: down_sum(0, k, c, y), d0_keep, d0_y, *d0_c[4:])
        d0 = moves.along_z(d0)
        (d1,) = run.hold(d1)
        d1_x, d1_c = swap(d1, "x", "d1_x"), swap(d1, "c", "d1_c")

        def last_sums(u, ux, uy, a, ax, ay):
            both = (wide_sum(u[0], ux[0], uy), wide_sum(a[0], ax[0], ay)[:, None])
            return moves.part_near(jnp.concatenate(both, 1))

        *a0_send, pre0, rights0, grad, rounded, mix_small0 = run(mix_first(0), rounded0, grad)
        a0_c = swaps(a0_send, "c", "a0_c")
        j1_send, j1_stay = run(last_sums, u1_keep, u1_x, u1_y, a1_keep, a1_x, a1_y)
        j1_near = moves.hop(j1_send, 1, "j1_near")
        a0_pass, a0_keep = run(mix_last, pre0, saved[0][3], rights0, rounded0, *a0_c)
        a0_x = swap(a0_pass, "x", "a0_x")
        small = run(
            packed_small,
            head_small,
            *(shift_send0, shift_keep0, wide_small0, mix_small0),
            *(shift_send1, shift_keep1, wide_small1, mix_small1),
        )
        small_c = swap(small, "c", "small_c")
        (d1_x,) = run.hold(d1_x)
        d1_xc = swap(d1_x, "c", "d1_xc")
        u0_y = swap(run(sum_at(1), u0_keep, u0_x), "y", "u0_y")
        small = run(plus, small, small_c)
        small_far = moves.hop(small, 2, "small_far")
        j1_send, j1_stay = run(moves.part_far, j1_stay, j1_near)
        j1_far = moves.hop(j1_send, 2, "j1_far")
        (d0,) = run.hold(d0)
        d0_x, d0_c = swap(d0, "x", "d0_x"), swap(d0, "c", "d0_c")
        small = run(plus, small, small_far)
        small_near = moves.hop(small, 1, "small_near")
        a0_y = swap(run(sum_at(1), a0_keep, a0_x), "y", "a0_y")
        u0 = moves.along_z(run(sum_at(0), u0_keep, u0_x, u0_y))
        j1 = run(rounded_sum, j1_stay, j1_far)
        j1_x, j1_c = swap(j1, "x", "j1_x"), swap(j1, "c", "j1_c")
        small = run(plus, small, small_near)
        small_x = swap(small, "x", "small_x")
        (d0_x,) = run.hold(d0_x)
        d0_xc = swap(d0_x, "c", "d0_xc")
        a0_send, a0_stay = run(lambda k, x, y: moves.part_near(k[0], x[0], y), a0_keep, a0_x, a0_y)
        a0_near = moves.hop(a0_send, 1, "a0_near")
        small = run(plus, small, small_x)
        small_y = swap(small, "y", "small_y")
        (j1_x,) = run.hold(j1_x)
        j1_xc = swap(j1_x, "c", "j1_xc")
        a0_send, a0_stay = run(moves.part_far, a0_stay, a0_near)
        a0_far = moves.hop(a0_send, 2, "a0_far")
        summed = run(plus, small, small_y)
        j0 = run(lambda u, *a: jnp.concatenate([u, rounded_sum(*a)[None]]), u0, a0_stay, a0_far)
        j0_x, j0_c = swap(j0, "x", "j0_x"), swap(j0, "c", "j0_c")
        done = run(
            lambda *v: finish(1, place, v[:4], v[4:]),
            *(j1, j1_c, j1_x, j1_xc, d1, d1_c, d1_x, d1_xc),
        )
        (j0_x,) = run.hold(j0_x)
        j0_xc = swap(j0_x, "c", "j0_xc")
        matrix_grads = run(
            lambda *v: finish(0, place, v[:4], v[4:8], *v[8:]),
            *(j0, j0_c, j0_x, j0_xc, d0, d0_c, d0_x, d0_xc, *done),
        )
    else:
        flats, smalls = [None] * LAYERS, [None] * LAYERS
        for layer in reversed(range(LAYERS)):
            *send, keep = down_at(layer)(rounded)
            got = swaps(send, "c", "down")
            got = jnp.stack([jnp.stack(got[4:]), jnp.stack(got[:4])])
            down_grad = moves.plain_halves_back(rounded_sum(keep, got))
            *send, shift_send, before = wide_first(layer)(rounded)
            passed, keep, shift_keep, grad, rounded, wide_small = wide_last(layer)(
                rounded, before, grad, *swaps(send, "c", "up")
            )
            up_grad = moves.plain_quarters_back(passed, keep)
            middle_rounded = rounded
            *send, pre, rights, grad, rounded, mix_small = mix_first(layer)(rounded, grad)
            got = swaps(send, "c", "attn")
            passed, keep = mix_last(pre, saved[layer][3], rights, middle_rounded, *got)
            attn_grad = moves.plain_quarters_back(passed[:, :, None], keep[:, :, None])
            flats[layer] = (attn_grad, up_grad, down_grad)
            smalls[layer] = (shift_send, shift_keep, wide_small, mix_small)
        summed = moves.sum_all(packed_small(head_small, *smalls[0], *smalls[1]))
        matrix_grads = [jnp.stack(pair) for pair in zip(*flats)]

    gains_grad, biases_grad, shifts_grad = [], [], []
    for layer in range(LAYERS):
        base = 40 + 24 * layer
        shifts_grad.append(summed[base : base + 8].reshape(FF))
        wide_sums = summed[base + 8 : base + 16]
        mix_sums = summed[base + 16 : base + 24]
        gains_grad.append(jnp.stack([mix_sums[0], wide_sums[0]]))
        biases_grad.append(
            jnp.stack([mix_sums[1], wide_sums[1], mix_sums[2], mix_sums[3], wide_sums[2], wide_sums[3]])
        )
    totals = summed[35]
    return (
        activations,
        grad,
        *matrix_grads,
        jnp.stack(gains_grad),
        jnp.stack(biases_grad),
        jnp.stack(shifts_grad),
        summed[:VOCAB].T,
        summed[32],
        summed[33],
        summed[34, :VOCAB],
        totals[0] / totals[2],
        totals[1] / totals[2],
        totals[2].astype(jnp.int32),
    )


def solution(mesh):
    fsdp, dp = mesh.shape["fsdp"], mesh.shape["dp"]
    fine = Mesh(mesh.devices.reshape(fsdp // 2, 2, dp // 2, 2), ("z", "y", "x", "c"))
    tokens = ("z", "y", "x", "c")
    flat = P(None, ("z", "y"), None)
    placed = (P(tokens, None), P(tokens), P(tokens), P(tokens), flat, flat, flat) + (P(),) * 7

    def run(*arrays):
        return local(fsdp, *arrays)

    return jax.shard_map(
        run,
        mesh=fine,
        in_specs=placed,
        out_specs=(P(tokens, None), P(tokens, None), flat, flat, flat) + (P(),) * 10,
        check_vma=False,
    )
```
